32 devices in a mesh: section: 2 (over x), ctx: 8 (over z, y), wshard: 2 (over core).
Axes of the slice: x: 2, y: 2, z: 4, core: 2. Of those that a mesh axis runs over, the one named last changes fastest.
Arguments:
- boundary: bfloat16 [2, 4, 2, 1024, 1024], P('section', None, 'wshard', 'ctx'), may hold values from -6 to 6
- segment_ids: int32 [4, 2, 1024], P(None, 'wshard', 'ctx'), may hold values from 0 to 1, never falling along the last dimension, each value on 1 to 768 neighbouring positions
- qkv_weight: bfloat16 [2, 1024, 3072], P('section', ('ctx', 'wshard')), may hold values from -0.1875 to 0.1875
- attn_out_weight: bfloat16 [2, 1024, 1024], P('section', ('ctx', 'wshard')), may hold values from -2 to 2
- ffn_in_weight: bfloat16 [2, 1024, 5248], P('section', ('ctx', 'wshard')), may hold values from -0.1875 to 0.1875
- ffn_out_weight: bfloat16 [2, 2624, 1024], P('section', None, ('ctx', 'wshard')), may hold values from -0.125 to 0.125
- norm_gains: bfloat16 [2, 2, 1024], P('section', None, ('ctx', 'wshard')), may hold values from 0.5 to 1.5
Outputs:
- boundary_out: bfloat16 [2, 4, 2, 1024, 1024], P('section', None, 'wshard', 'ctx')
- grad_qkv: float32 [2, 1024, 3072], P('section', ('ctx', 'wshard'))
- grad_attn_out: float32 [2, 1024, 1024], P('section', ('ctx', 'wshard'))
- grad_ffn_in: float32 [2, 1024, 5248], P('section', ('ctx', 'wshard'))
- grad_ffn_out: float32 [2, 2624, 1024], P('section', None, ('ctx', 'wshard'))
- grad_gains: float32 [2, 2, 1024], P('section', None, ('ctx', 'wshard'))
The draws below stay inside these ranges and needn't reach their ends.
Inputs may be any that keep to these rules, and one draw needn't show every extreme that they name: `segment_ids`: within each sequence the ids never fall; every id of 0 to 1 holds 1 to 768 tokens.
All inputs are finite; a program needn't handle non-finite values.
Results may differ from the reference program's by a relative error of at most 0.034.
Values may be sent and summed in bfloat16 or wider, within the bound.
No kernel may reach another device: no remote copies, remote signals or barrier semaphores. Data moves between devices by JAX's collectives and lax.ppermute only.
A program may use at most 320 MiB of HBM per device.

```python
import math
from functools import partial
import jax
import jax.numpy as jnp
import numpy as np
from jax import lax

D = 1024
HEADS = 16
HEAD_DIM = 64
FF = 2624
MICRO = 4
LEN = 1024
SEQS = 2
SECTIONS = 2
SEG_COUNT = 2
SEG_MOST = 768


def shard_levels(rng, extent, cuts, least, largest):
    gain, own = 1.0, jax.random.fold_in(rng, 6)
    for dim, blocks in cuts:
        draws = jnp.exp(jax.random.uniform(jax.random.fold_in(own, dim), (blocks,), jnp.float32, least / len(cuts), largest / len(cuts)))
        gain = gain * jnp.repeat(draws, extent[dim] // blocks).reshape([-1 if axis == dim else 1 for axis in range(len(extent))])
    return gain


def length_profile(amount, total, most, skew):
    weights = [(1 << 20) // math.isqrt(standing ** skew) + 1 for standing in range(2, amount + 1)]
    rest, counts = total - most - (amount - 1), [1] * (amount - 1)
    while rest > 0:
        movable = [i for i in range(amount - 1) if counts[i] < most]
        pool, left = sum([weights[i] for i in movable]), rest
        for i in movable:
            addition = min(most - counts[i], max(1, left * weights[i] // pool), rest)
            counts[i] = counts[i] + addition
            rest = rest - addition
    return np.array([most] + counts)


def ragged_sizes(own_key, number_of, total, most, skew):
    if number_of == 2:
        one = jax.random.randint(own_key, (), max(1, total - most), min(most, total - 1) + 1)
        return jnp.stack([one, total - one])
    tallies = jnp.asarray(length_profile(number_of, total, most, skew), jnp.int32)
    twos = (number_of - 1) // 2
    giver, taker = tallies[1:1 + 2 * twos:2], tallies[2:2 + 2 * twos:2]
    room = jnp.minimum(giver - 1, most - taker)
    moved = jax.random.randint(jax.random.fold_in(own_key, 1), (twos,), 0, 1 << 20) % (room + 1)
    tallies = tallies.at[1:1 + 2 * twos:2].set(giver - moved).at[2:2 + 2 * twos:2].set(taker + moved)
    return tallies[jax.random.permutation(jax.random.fold_in(own_key, 2), number_of)]


def centred(rng, extent, scale, limit, split=(), kind=jnp.bfloat16):
    array = jax.random.normal(rng, extent, jnp.float32) * scale
    if len(split) > 0:
        array = shard_levels(rng, extent, split, -0.22, 0.18) * array
    return jnp.clip(array, min=-limit, max=limit).astype(kind)


def setup_inputs(seed: int = 0) -> dict:
    arg_keys = jax.random.split(jax.random.key(seed), 8)
    boundary = centred(arg_keys[0], (SECTIONS, MICRO, SEQS, LEN, D), 1.0, 6.0, ((0, 2), (2, 2), (3, 8)))
    segment_ids = jax.vmap(lambda own: jnp.searchsorted(jnp.cumsum(ragged_sizes(own, SEG_COUNT, LEN, SEG_MOST, 1)), jnp.arange(LEN), side="right"))(jax.random.split(arg_keys[1], MICRO * SEQS)).reshape((MICRO, SEQS, LEN)).astype(jnp.int32)
    qkv_weight = centred(arg_keys[2], (SECTIONS, D, 3 * D), D ** -0.5, 0.1875, ((0, 2), (1, 16)))
    attn_out_weight = centred(arg_keys[3], (SECTIONS, D, D), (max(4, D // 128)) ** -0.5, 2.0, ((0, 2), (1, 16)))
    ffn_in_weight = centred(arg_keys[4], (SECTIONS, D, 2 * FF), D ** -0.5, 0.1875, ((0, 2), (1, 16)))
    ffn_out_weight = centred(arg_keys[5], (SECTIONS, FF, D), FF ** -0.5, 0.125, ((0, 2), (2, 16)))
    norm_gains = jnp.clip(1.0 + 0.1 * jax.random.normal(arg_keys[6], (SECTIONS, 2, D), jnp.float32), 0.5, 1.5).astype(jnp.bfloat16)
    return {"boundary": boundary, "segment_ids": segment_ids, "qkv_weight": qkv_weight, "attn_out_weight": attn_out_weight, "ffn_in_weight": ffn_in_weight, "ffn_out_weight": ffn_out_weight, "norm_gains": norm_gains}


@jax.custom_vjp
def low(v):
    return lax.optimization_barrier(v.astype(jnp.bfloat16)).astype(jnp.float32)

@jax.custom_vjp
def low_back(v):
    return v

def low_keep(v):
    return (low(v), None)

def low_pass(kept, grad):
    return (grad,)

def back_keep(v):
    return (v, None)

def back_low(kept, grad):
    return (low(grad),)
low.defvjp(low_keep, low_pass)
low_back.defvjp(back_keep, back_low)
EPSILON = 1e-05
ROPE_BASE = 160000.0
NEG_FILL = -1e+30
HIGHEST = lax.Precision.HIGHEST

def norm_rows(values, gain_row):
    center = values - lax.optimization_barrier(jnp.mean(values, axis=-1, keepdims=True))
    spread = lax.optimization_barrier(jnp.mean(center * center, axis=-1, keepdims=True))
    return center * lax.rsqrt(spread + EPSILON) * gain_row

def positions_of(segment):
    places = jnp.arange(segment.shape[0], dtype=jnp.int32)
    begins = jnp.concatenate([jnp.ones((1,), dtype=jnp.bool_), segment[1:] != segment[:-1]])
    firsts = lax.cummax(jnp.where(begins, places, 0).astype(jnp.int32), axis=0)
    return places - firsts

def rotate(heads_in, position):
    half_width = heads_in.shape[-1] // 2
    exponent = jnp.arange(half_width, dtype=jnp.float32) * (-2.0 / heads_in.shape[-1])
    angles = position.astype(jnp.float32)[:, None] * (ROPE_BASE ** exponent)[None, :]
    cosine = jnp.cos(angles)[:, None, :]
    sine_part = jnp.sin(angles)[:, None, :]
    first_half = heads_in[..., :half_width]
    second_half = heads_in[..., half_width:]
    return jnp.concatenate([first_half * cosine - second_half * sine_part, second_half * cosine + first_half * sine_part], axis=-1)

def attend(queries, keyset, valueset, segment):
    seq_length = queries.shape[0]
    key_block = min(512, seq_length)
    query_blocks = queries.reshape(seq_length // key_block, key_block, HEADS, HEAD_DIM)
    seg_blocks = segment.reshape(seq_length // key_block, key_block)

    def one_block(block_item):
        query_rows, seg_rows = block_item
        raw_scores = low_back(jnp.einsum('qhd,khd->hqk', query_rows, keyset, precision=HIGHEST)) * HEAD_DIM ** (-0.5)
        allowed = (seg_rows[:, None] == segment[None, :])[None]
        scores = jnp.where(allowed, raw_scores, NEG_FILL)
        row_top = lax.optimization_barrier(jnp.max(scores, axis=-1, keepdims=True))
        exp_terms = jnp.where(allowed, jnp.exp(scores - row_top), 0.0)
        row_total = lax.optimization_barrier(jnp.sum(exp_terms, axis=-1))
        weighted = low_back(jnp.einsum('hqk,khd->qhd', low(exp_terms), valueset, precision=HIGHEST))
        return weighted / jnp.transpose(row_total)[:, :, None]
    attended = lax.map(jax.checkpoint(one_block), (query_blocks, seg_blocks))
    return attended.reshape(seq_length, HEADS, HEAD_DIM)

def layer(inputs, qkv_mat, out_mat, in_mat, back_mat, gain_rows, segment, position):
    tok_count = inputs.shape[0]
    normed = low(norm_rows(inputs, gain_rows[0]))
    mixed_rows = low_back(jnp.dot(normed, qkv_mat, precision=HIGHEST))
    queries = low(rotate(mixed_rows[:, :D].reshape(tok_count, HEADS, HEAD_DIM), position))
    keyset = low(rotate(mixed_rows[:, D:2 * D].reshape(tok_count, HEADS, HEAD_DIM), position))
    valueset = low(mixed_rows[:, 2 * D:].reshape(tok_count, HEADS, HEAD_DIM))
    attended = low(attend(queries, keyset, valueset, segment).reshape(tok_count, D))
    hidden = inputs + low_back(jnp.dot(attended, out_mat, precision=HIGHEST))
    second = low(norm_rows(hidden, gain_rows[1]))
    upward = low_back(jnp.dot(second, in_mat, precision=HIGHEST))
    activated = low(jax.nn.gelu(upward[:, :FF], approximate=False) * upward[:, FF:])
    return hidden + jnp.dot(activated, back_mat, precision=HIGHEST)

def network(inputs, weights, segment, position):
    qkv_mat, out_mat, in_mat, back_mat, gain_mat = weights
    first_out = layer(inputs, qkv_mat[0], out_mat[0], in_mat[0], back_mat[0], gain_mat[0], segment, position)
    passed = low_back(low(first_out))
    return layer(passed, qkv_mat[1], out_mat[1], in_mat[1], back_mat[1], gain_mat[1], segment, position)

def reference(boundary, segment_ids, qkv_weight, attn_out_weight, ffn_in_weight, ffn_out_weight, norm_gains):
    weights = tuple((mat.astype(jnp.float32) for mat in (qkv_weight, attn_out_weight, ffn_in_weight, ffn_out_weight, norm_gains)))
    inputs_all = boundary[0].reshape(MICRO * SEQS, LEN, D).astype(jnp.float32)
    cotangents = boundary[1].reshape(MICRO * SEQS, LEN, D).astype(jnp.float32)
    segments = segment_ids.reshape(MICRO * SEQS, LEN)

    def one_sequence(totals, seq_item):
        inputs, cotangent, segment = seq_item
        position = positions_of(segment)
        outputs, pull_back = jax.vjp(partial(network, segment=segment, position=position), inputs, weights)
        grad_input, grad_weights = pull_back(cotangent)
        totals = tuple((total_mat + grad_mat for total_mat, grad_mat in zip(totals, grad_weights)))
        return (totals, (outputs.astype(jnp.bfloat16), grad_input.astype(jnp.bfloat16)))
    start_totals = tuple((jnp.zeros(mat.shape, jnp.float32) for mat in weights))
    totals, (all_outputs, all_grads) = lax.scan(one_sequence, start_totals, (inputs_all, cotangents, segments))
    boundary_out = jnp.stack([all_grads, all_outputs]).reshape(SECTIONS, MICRO, SEQS, LEN, D)
    return (boundary_out, totals[0], totals[1], totals[2], totals[3], totals[4])
```

```python
from functools import partial

import jax
import jax.numpy as jnp
from jax import lax
from jax.experimental import pallas as pl
from jax.experimental.pallas import tpu as pltpu
from jax.sharding import PartitionSpec as P

D = 1024
HEADS = 16
HEAD_DIM = 64
FF = 2624
FFP = 2688
LANES = 128
PAIRS = D // LANES
EPSILON = 1e-05
ROPE_BASE = 160000.0
NEG_FILL = -1e30
BF = jnp.bfloat16
F32 = jnp.float32
BOTH = ("ctx", "wshard")
VMEM = 60 * 1024 * 1024


def dot(a, b, dims):
    return lax.dot_general(a, b, (dims, ((), ())), preferred_element_type=F32)


NN = ((1,), (0,))
NT = ((1,), (1,))
TN = ((0,), (0,))


def params(limit=VMEM):
    return pltpu.CompilerParams(vmem_limit_bytes=limit)


def rope_block(v, cosine, sine):
    lane = lax.broadcasted_iota(jnp.int32, v.shape, 1) % HEAD_DIM
    other = jnp.where(
        lane < HEAD_DIM // 2,
        pltpu.roll(v, LANES - HEAD_DIM // 2, 1),
        pltpu.roll(v, HEAD_DIM // 2, 1),
    )
    return v * cosine + other * sine


def rope_kernel(v_ref, cos_ref, sin_ref, out_ref, *, rotated):
    cosine, sine = cos_ref[...], sin_ref[...]
    for j in range(v_ref.shape[1] // LANES):
        at = slice(j * LANES, (j + 1) * LANES)
        v = v_ref[:, at].astype(F32)
        if j * LANES < rotated:
            v = rope_block(v, cosine, sine)
        out_ref[:, at] = v.astype(BF)


def rope_apply(v, cosine, sine, rotated):
    return pl.pallas_call(
        partial(rope_kernel, rotated=rotated),
        out_shape=jax.ShapeDtypeStruct(v.shape, BF),
        compiler_params=params(),
    )(v, cosine, sine)


def head_mask(shape, head):
    lane = lax.broadcasted_iota(jnp.int32, shape, 1)
    return (lane >= HEAD_DIM) if head else (lane < HEAD_DIM)


def pick(mask, v, other=0.0):
    return jnp.where(mask, v, jnp.full(v.shape, other, v.dtype))


def attend_kernel(q_ref, k_ref, v_ref, segq_ref, segk_ref, o_ref, lse_ref, bias_ref):
    @pl.when(pl.program_id(0) == 0)
    def _():
        bias_ref[...] = jnp.where(segk_ref[...] == segq_ref[...], 0.0, NEG_FILL)

    k, v = k_ref[...], v_ref[...]
    q = q_ref[...] * jnp.asarray(HEAD_DIM**-0.5, BF)
    qmask, vmask = head_mask(q.shape, 0), head_mask(v.shape, 0)
    parts, stats = [], []
    for head in range(2):
        qh = pick(qmask if head == 0 else ~qmask, q)
        vh = pick(vmask if head == 0 else ~vmask, v, 1.0)
        s = dot(k, qh, NT) + bias_ref[...]
        top = jnp.max(s, axis=0, keepdims=True)
        e = jnp.exp(s - top).astype(BF)
        u = dot(vh, e, TN)
        if head == 0:
            total, value = u[HEAD_DIM:], u[:HEAD_DIM]
        else:
            total, value = u[:HEAD_DIM], u[HEAD_DIM:]
        parts.append(value / total)
        stats.append(top + jnp.log(total[:1]))
    o_ref[...] = jnp.concatenate(parts, axis=0).T.astype(BF)
    lse_ref[0] = jnp.concatenate(stats, axis=0)


def attend(q, k, v, segq, segk):
    rows, keys = q.shape[0], k.shape[0]
    return pl.pallas_call(
        attend_kernel,
        grid=(PAIRS,),
        in_specs=[
            pl.BlockSpec((rows, LANES), lambda p: (0, p)),
            pl.BlockSpec((keys, LANES), lambda p: (0, p)),
            pl.BlockSpec((keys, LANES), lambda p: (0, p)),
            pl.BlockSpec((1, rows), lambda p: (0, 0)),
            pl.BlockSpec((keys, 1), lambda p: (0, 0)),
        ],
        out_specs=[
            pl.BlockSpec((rows, LANES), lambda p: (0, p)),
            pl.BlockSpec((1, 2, rows), lambda p: (p, 0, 0)),
        ],
        out_shape=[
            jax.ShapeDtypeStruct((rows, D), BF),
            jax.ShapeDtypeStruct((PAIRS, 2, rows), F32),
        ],
        scratch_shapes=[pltpu.VMEM((keys, rows), F32)],
        compiler_params=params(),
    )(q, k, v, segq, segk)


def attend_back_kernel(
    q_ref, k_ref, v_ref, do_ref, o_ref, lse_ref, segq_ref, segk_ref, dq_ref, dk_ref, dv_ref, bias_ref
):
    @pl.when(pl.program_id(0) == 0)
    def _():
        bias_ref[...] = jnp.where(segk_ref[...] == segq_ref[...], 0.0, NEG_FILL)

    scale = jnp.asarray(HEAD_DIM**-0.5, BF)
    k, v, do = k_ref[...], v_ref[...], do_ref[...]
    q = q_ref[...] * scale
    prod = (do.astype(F32) * o_ref[...].astype(F32)).T
    lse = lse_ref[0]
    qmask, kmask = head_mask(q.shape, 0), head_mask(k.shape, 0)
    dq = dk = dv = 0.0
    for head in range(2):
        qm = qmask if head == 0 else ~qmask
        km = kmask if head == 0 else ~kmask
        qh, doh, kh = pick(qm, q), pick(qm, do), pick(km, k)
        delta = jnp.sum(prod[head * HEAD_DIM : (head + 1) * HEAD_DIM], axis=0, keepdims=True)
        s = dot(k, qh, NT) + bias_ref[...]
        p = jnp.exp(s - lse[head : head + 1])
        dp = dot(v, doh, NT)
        ds = (p * (dp - delta)).astype(BF)
        dv += dot(p.astype(BF), doh, NN)
        dk += dot(ds, qh, NN)
        dq += dot(ds, kh, TN)
    dq_ref[...] = dq * HEAD_DIM**-0.5
    dk_ref[...] = dk.astype(BF)
    dv_ref[...] = dv.astype(BF)


def attend_back(q, k, v, do, o, lse, segq, segk):
    rows, keys = q.shape[0], k.shape[0]
    qspec = pl.BlockSpec((rows, LANES), lambda p: (0, p))
    kspec = pl.BlockSpec((keys, LANES), lambda p: (0, p))
    return pl.pallas_call(
        attend_back_kernel,
        grid=(PAIRS,),
        in_specs=[
            qspec,
            kspec,
            kspec,
            qspec,
            qspec,
            pl.BlockSpec((1, 2, rows), lambda p: (p, 0, 0)),
            pl.BlockSpec((1, rows), lambda p: (0, 0)),
            pl.BlockSpec((keys, 1), lambda p: (0, 0)),
        ],
        out_specs=[qspec, kspec, kspec],
        out_shape=[
            jax.ShapeDtypeStruct((rows, D), F32),
            jax.ShapeDtypeStruct((keys, D), BF),
            jax.ShapeDtypeStruct((keys, D), BF),
        ],
        scratch_shapes=[pltpu.VMEM((keys, rows), F32)],
        compiler_params=params(),
    )(q, k, v, do, o, lse, segq, segk)


def norm_parts(values):
    center = values - jnp.mean(values, axis=-1, keepdims=True)
    spread = jnp.mean(center * center, axis=-1, keepdims=True)
    inverse = lax.rsqrt(spread + EPSILON)
    return center * inverse, inverse


def norm_back(hat, inverse, gain_row, grad):
    scaled = grad * gain_row
    return inverse * (
        scaled
        - jnp.mean(scaled, axis=-1, keepdims=True)
        - hat * jnp.mean(scaled * hat, axis=-1, keepdims=True)
    )


def gelu_parts(t):
    phi = 0.5 * (1.0 + lax.erf(t * 0.7071067811865476))
    density = 0.3989422804014327 * jnp.exp(-0.5 * t * t)
    return t * phi, phi + t * density


class Plan:
    def __init__(self, boundary):
        self.micro = boundary.shape[1]
        self.tok_rows = boundary.shape[3]
        self.n_ctx = lax.axis_size("ctx")
        self.nw = lax.axis_size("wshard")
        self.g = self.n_ctx // (self.micro * self.nw)
        self.r = self.tok_rows // (self.g * self.nw)
        self.i = lax.axis_index("ctx")
        self.w = lax.axis_index("wshard")
        self.rows = self.n_ctx * self.r
        self.members = self.g * self.nw

    def to_sequences(self, local):
        parts = local.reshape(self.micro, self.g, self.nw, self.r, D)
        parts = lax.all_to_all(parts.transpose(2, 0, 1, 3, 4), "wshard", 0, 0, tiled=True)
        parts = parts.transpose(1, 0, 2, 3, 4).reshape(self.n_ctx, self.r, D)
        return lax.all_to_all(parts, "ctx", 0, 0, tiled=True).reshape(self.rows, D)

    def from_sequences(self, rows):
        parts = lax.all_to_all(rows.reshape(self.n_ctx, self.r, D), "ctx", 0, 0, tiled=True)
        parts = parts.reshape(self.micro, self.nw, self.g, self.r, D).transpose(1, 0, 2, 3, 4)
        parts = lax.all_to_all(parts, "wshard", 0, 0, tiled=True)
        return parts.transpose(1, 2, 0, 3, 4).reshape(self.micro, self.tok_rows, D)

    def rotation(self, by):
        pairs = []
        for flat in range(self.n_ctx * self.nw):
            group, place = divmod(flat, self.members)
            pairs.append((flat, group * self.members + (place + by) % self.members))
        return pairs

    def gather_rows(self, rows):
        pieces = [rows]
        for by in range(1, self.members):
            pieces.append(lax.ppermute(rows, BOTH, self.rotation(by)))
        return jnp.concatenate(pieces, axis=0)

    def scatter_rows(self, terms):
        count = self.rows
        total = terms[:count].astype(F32)
        for by in range(1, self.members):
            piece = terms[by * count : (by + 1) * count]
            total += lax.ppermute(piece, BOTH, self.rotation(-by)).astype(F32)
        return total


def body(
    boundary, segment_ids, qkv_weight, attn_out_weight, ffn_in_weight, ffn_out_weight, norm_gains
):
    section = lax.axis_index("section")
    sections = lax.axis_size("section")
    plan = Plan(boundary)
    rows = plan.rows
    own = plan.to_sequences(boundary[0, :, 0])

    whole = lax.all_gather(segment_ids[:, 0], BOTH, axis=0)
    whole = whole.reshape(plan.n_ctx, plan.nw, plan.micro, plan.tok_rows)
    mine = plan.i // plan.g
    line = lax.dynamic_index_in_dim(whole, mine // plan.nw, 2, keepdims=False)
    line = lax.dynamic_index_in_dim(line, mine % plan.nw, 1, keepdims=False).reshape(-1)
    grid = line.reshape(plan.n_ctx, plan.members, plan.r)
    place = (plan.i % plan.g) * plan.nw + plan.w
    seg_pieces = [
        lax.dynamic_index_in_dim(
            grid, (place - by) % plan.members, 1, keepdims=False
        ).reshape(rows)
        for by in range(plan.members)
    ]
    segq = seg_pieces[0]
    segk = jnp.concatenate(seg_pieces)
    token = (
        lax.broadcasted_iota(jnp.int32, (plan.n_ctx, plan.r), 0) * plan.tok_rows
        + place * plan.r
        + lax.broadcasted_iota(jnp.int32, (plan.n_ctx, plan.r), 1)
    ).reshape(rows)
    first = jnp.sum((line[None, :] < segq[:, None]).astype(jnp.int32), axis=1)
    position = (token - first).astype(F32)
    half = HEAD_DIM // 2
    exponent = jnp.arange(half, dtype=F32) * (-2.0 / HEAD_DIM)
    angles = position[:, None] * (ROPE_BASE**exponent)[None, :]
    cosine, sine = jnp.cos(angles), jnp.sin(angles)
    cos_rows = jnp.concatenate([cosine] * 4, axis=1)
    sin_rows = jnp.concatenate([-sine, sine] * 2, axis=1)
    segq_row, segk_col = segq[None, :], segk[:, None]

    gain_cols = jnp.pad(norm_gains[0].T, ((0, 0), (0, LANES - 2)))
    pad = FFP - FF
    first_shard = jnp.concatenate([qkv_weight[0], gain_cols], axis=1)
    in_shard = jnp.concatenate(
        [
            jnp.pad(ffn_in_weight[0][:, :FF], ((0, 0), (0, pad))),
            jnp.pad(ffn_in_weight[0][:, FF:], ((0, 0), (0, pad))),
        ],
        axis=1,
    )
    back_shard = jnp.pad(ffn_out_weight[0].T, ((0, 0), (0, pad)))
    w_first = lax.all_gather(first_shard, BOTH, axis=0, tiled=True)
    w_attn = lax.all_gather(attn_out_weight[0], BOTH, axis=0, tiled=True)
    w_in = lax.all_gather(in_shard, BOTH, axis=0, tiled=True)
    w_back = lax.all_gather(back_shard, BOTH, axis=0, tiled=True)
    w_qkv = w_first[:, : 3 * D]
    gains = w_first[:, 3 * D : 3 * D + 2].T.astype(F32)

    def forward(x_low):
        x = x_low.astype(F32)
        hat, _ = norm_parts(x)
        a = (hat * gains[0]).astype(BF)
        kv = rope_apply(dot(a, w_qkv[:, D:], NN), cos_rows, sin_rows, D)
        kv_all = plan.gather_rows(kv)
        q = rope_apply(dot(a, w_qkv[:, :D], NN), cos_rows, sin_rows, D)
        k_all, v_all = kv_all[:, :D], kv_all[:, D:]
        o, lse = attend(q, k_all, v_all, segq_row, segk_col)
        h = x + dot(o, w_attn, NN)
        hat2, inv2 = norm_parts(h)
        b = (hat2 * gains[1]).astype(BF)
        u = dot(b, w_in, NN)
        act, slope = gelu_parts(u[:, :FFP])
        gate = u[:, FFP:]
        z = (act * gate).astype(BF)
        out = (h + dot(z, w_back, NT)).astype(BF)
        return out, (x, a, q, k_all, v_all, o, lse, h, b, act.astype(BF), (slope * gate).astype(BF), z)

    def backward(stash, grad, with_weights):
        x, a, q, k_all, v_all, o, lse, h, b, act, slope, z = stash
        dz = dot(grad, w_back, NN)
        du = jnp.concatenate([dz * slope, dz * act], axis=1).astype(BF)
        db = dot(du, w_in, NT)
        hat2, inv2 = norm_parts(h)
        dh = grad.astype(F32) + norm_back(hat2, inv2, gains[1], db)
        dhb = dh.astype(BF)
        do = dot(dhb, w_attn, NT).astype(BF)
        dq, dk_terms, dv_terms = attend_back(q, k_all, v_all, do, o, lse, segq_row, segk_col)
        dkv = plan.scatter_rows(jnp.concatenate([dk_terms, dv_terms], axis=1))
        dm = rope_apply(jnp.concatenate([dq, dkv], axis=1), cos_rows, -sin_rows, 2 * D)
        da = dot(dm, w_qkv, NT)
        hat1, inv1 = norm_parts(x)
        dx = (dh + norm_back(hat1, inv1, gains[0], da)).astype(BF)
        if not with_weights:
            return dx, None
        g_back = dot(grad, z, TN).astype(BF)
        g_in = dot(b, du, TN).astype(BF)
        g_attn = dot(o, dhb, TN).astype(BF)
        g_qkv = dot(a, dm, TN).astype(BF)
        g_gain = jnp.stack([jnp.sum(da * hat1, axis=0), jnp.sum(db * hat2, axis=0)], axis=1)
        g_gain = jnp.pad(g_gain, ((0, 0), (0, LANES - 2))).astype(BF)
        return dx, (g_back, g_in, g_attn, jnp.concatenate([g_qkv, g_gain], axis=1))

    def handed(array, by):
        pairs = [(s, s + by) for s in range(sections) if 0 <= s + by < sections]
        return lax.ppermute(array, "section", pairs)

    first_out, _ = forward(own)
    x_in = jnp.where(section == 0, own, handed(first_out, 1))
    out, stash = forward(x_in)
    first_dx, _ = backward(stash, own, False)
    grad_in = jnp.where(section == sections - 1, own, handed(first_dx, -1))
    dx, grads = backward(stash, grad_in, True)
    g_back, g_in, g_attn, g_first = (
        lax.psum_scatter(t, BOTH, scatter_dimension=0, tiled=True).astype(F32) for t in grads
    )
    boundary_local = plan.from_sequences(jnp.where(section == 0, dx, out))
    return (
        boundary_local[None, :, None],
        g_first[None, :, : 3 * D],
        g_attn[None],
        jnp.concatenate([g_in[:, :FF], g_in[:, FFP : FFP + FF]], axis=1)[None],
        g_back[:, :FF].T[None],
        g_first[:, 3 * D : 3 * D + 2].T[None],
    )


def solution(mesh):
    placed = (
        P("section", None, "wshard", "ctx", None),
        P(None, "wshard", "ctx"),
        P("section", ("ctx", "wshard"), None),
        P("section", ("ctx", "wshard"), None),
        P("section", ("ctx", "wshard"), None),
        P("section", None, ("ctx", "wshard")),
        P("section", None, ("ctx", "wshard")),
    )
    return jax.shard_map(
        body,
        mesh=mesh,
        in_specs=placed,
        out_specs=(placed[0],) + placed[2:],
        check_vma=False,
    )
```

```python
from functools import partial

import jax
import jax.numpy as jnp
from jax import lax
from jax.experimental import pallas as pl
from jax.experimental.pallas import tpu as pltpu
from jax.sharding import PartitionSpec as P

D = 1024
HEADS = 16
HEAD_DIM = 64
FF = 2624
FFP = 2688
FFB = 896
LANES = 128
PAIRS = D // LANES
WIDE = 4 * D + LANES
EPSILON = 1e-05
ROPE_BASE = 160000.0
NEG_FILL = -1e30
BF = jnp.bfloat16
F32 = jnp.float32
BOTH = ("ctx", "wshard")
VMEM = 60 * 1024 * 1024
NN = ((1,), (0,))
NT = ((1,), (1,))
TN = ((0,), (0,))
SMEM_SPEC = pl.BlockSpec(memory_space=pltpu.SMEM)


def dot(a, b, dims):
    return lax.dot_general(a, b, (dims, ((), ())), preferred_element_type=F32)


def after(value, *others):
    return lax.optimization_barrier((value,) + others)[0]


def shaped(shape, kind=BF):
    return jax.ShapeDtypeStruct(shape, kind)


def call(kernel, name, flops=0, moved=0, exps=0, **more):
    return pl.pallas_call(
        kernel,
        name=name,
        compiler_params=pltpu.CompilerParams(vmem_limit_bytes=VMEM),
        cost_estimate=pl.CostEstimate(
            flops=int(flops), bytes_accessed=int(moved), transcendentals=int(exps)
        ),
        **more,
    )


def whole(shape):
    return pl.BlockSpec(shape, lambda *_: (0,) * len(shape))


def rope_block(v, cosine, sine):
    lane = lax.broadcasted_iota(jnp.int32, v.shape, 1) % HEAD_DIM
    other = jnp.where(
        lane < HEAD_DIM // 2,
        pltpu.roll(v, LANES - HEAD_DIM // 2, 1),
        pltpu.roll(v, HEAD_DIM // 2, 1),
    )
    return v * cosine + other * sine


def norm_parts(values):
    center = values - jnp.mean(values, axis=-1, keepdims=True)
    spread = jnp.mean(center * center, axis=-1, keepdims=True)
    inverse = lax.rsqrt(spread + EPSILON)
    return center * inverse, inverse


def norm_back(values, gain_row, grad):
    hat, inverse = norm_parts(values)
    scaled = grad * gain_row
    back = inverse * (
        scaled
        - jnp.mean(scaled, axis=-1, keepdims=True)
        - hat * jnp.mean(scaled * hat, axis=-1, keepdims=True)
    )
    return back, jnp.sum(grad * hat, axis=0, keepdims=True)


def head_mask(shape, head):
    lane = lax.broadcasted_iota(jnp.int32, shape, 1)
    return (lane >= HEAD_DIM) if head else (lane < HEAD_DIM)


def pick(mask, v, other=0.0):
    return jnp.where(mask, v, jnp.full(v.shape, other, v.dtype))


def gains_of(wide):
    def kernel(w_ref, out_ref):
        out_ref[...] = w_ref[...].astype(F32).T[:8]

    return call(
        kernel,
        "gains",
        grid=(1,),
        in_specs=[pl.BlockSpec((D, LANES), lambda j: (0, 4 * D // LANES))],
        out_specs=whole((8, D)),
        out_shape=shaped((8, D), F32),
    )(wide)


def keys_values(x, gains, wide, cosine, sine):
    rows = x.shape[0]
    block = 512

    def kernel(x_ref, gain_ref, w_ref, cos_ref, sin_ref, a_ref, out_ref):
        @pl.when(pl.program_id(0) == 0)
        def _():
            hat, _ = norm_parts(x_ref[...].astype(F32))
            a_ref[...] = (hat * gain_ref[0:1]).astype(BF)

        m = dot(a_ref[...], w_ref[...], NN)
        for j in range(block // LANES):
            at = slice(j * LANES, (j + 1) * LANES)
            v = m[:, at]
            if j % 2 == 0:
                v = rope_block(v, cos_ref[...], sin_ref[...])
            out_ref[:, at] = v.astype(BF)

    return call(
        kernel,
        "keys_values",
        flops=2 * rows * D * 2 * D,
        moved=2 * (2 * D * D + 4 * rows * D),
        grid=(2 * D // block,),
        in_specs=[
            whole((rows, D)),
            whole((8, D)),
            pl.BlockSpec((D, block), lambda j: (0, j)),
            whole((rows, LANES)),
            whole((rows, LANES)),
        ],
        out_specs=[whole((rows, D)), pl.BlockSpec((rows, block), lambda j: (0, j))],
        out_shape=[shaped((rows, D)), shaped((rows, 2 * D))],
    )(x, gains, wide, cosine, sine)


def queries_of(a, wide, cosine, sine):
    rows = a.shape[0]
    block = 512

    def kernel(a_ref, w_ref, cos_ref, sin_ref, out_ref):
        m = dot(a_ref[...], w_ref[...], NN)
        for j in range(block // LANES):
            at = slice(j * LANES, (j + 1) * LANES)
            out_ref[:, at] = rope_block(m[:, at], cos_ref[...], sin_ref[...]).astype(BF)

    return call(
        kernel,
        "queries",
        flops=2 * rows * D * D,
        moved=2 * (D * D + 2 * rows * D),
        grid=(D // block,),
        in_specs=[
            whole((rows, D)),
            pl.BlockSpec((D, block), lambda j: (0, 2 * D // block + j)),
            whole((rows, LANES)),
            whole((rows, LANES)),
        ],
        out_specs=pl.BlockSpec((rows, block), lambda j: (0, j)),
        out_shape=shaped((rows, D)),
    )(a, wide, cosine, sine)


def attend(q, kv_list, segq, segk):
    rows = q.shape[0]
    members = len(kv_list)
    keys = members * rows

    def kernel(q_ref, segq_ref, segk_ref, *refs):
        kv_refs, (o_ref, lse_ref, bias_ref) = refs[:members], refs[members:]

        @pl.when(pl.program_id(0) == 0)
        def _():
            bias_ref[...] = jnp.where(segk_ref[...] == segq_ref[...], 0.0, NEG_FILL)

        k = jnp.concatenate([r[:, :LANES] for r in kv_refs], axis=0)
        v = jnp.concatenate([r[:, LANES:] for r in kv_refs], axis=0)
        q = q_ref[...] * jnp.asarray(HEAD_DIM**-0.5, BF)
        parts, stats = [], []
        for head in range(2):
            qh = pick(head_mask(q.shape, head), q)
            vh = pick(head_mask(v.shape, head), v, 1.0)
            s = dot(k, qh, NT) + bias_ref[...]
            top = jnp.max(s, axis=0, keepdims=True)
            e = jnp.exp(s - top).astype(BF)
            u = dot(vh, e, TN)
            low, high = u[:HEAD_DIM], u[HEAD_DIM:]
            value, total = (high, low) if head else (low, high)
            parts.append(value / total)
            stats.append(top + jnp.log(total[:1]))
        o_ref[...] = jnp.concatenate(parts, axis=0).T.astype(BF)
        lse_ref[0] = jnp.concatenate(stats, axis=0)

    return call(
        kernel,
        "attend",
        flops=8 * rows * keys * D,
        moved=2 * (2 * rows * D + 2 * keys * D),
        exps=rows * keys * HEADS,
        grid=(PAIRS,),
        in_specs=[
            pl.BlockSpec((rows, LANES), lambda p: (0, p)),
            whole((1, rows)),
            whole((keys, 1)),
        ]
        + [pl.BlockSpec((rows, 2 * LANES), lambda p: (0, p))] * members,
        out_specs=[
            pl.BlockSpec((rows, LANES), lambda p: (0, p)),
            pl.BlockSpec((1, 2, rows), lambda p: (p, 0, 0)),
        ],
        out_shape=[shaped((rows, D)), shaped((PAIRS, 2, rows), F32)],
        scratch_shapes=[pltpu.VMEM((keys, rows), F32)],
    )(q, segq, segk, *kv_list)


def project(x, o, gains, wide):
    rows = x.shape[0]
    block = 512
    steps = D // block

    def kernel(x_ref, o_ref, gain_ref, w_ref, h_ref, b_ref):
        j = pl.program_id(0)
        at = pl.ds(pl.multiple_of(j * block, block), block)
        h_ref[:, at] = x_ref[:, at].astype(F32) + dot(o_ref[...], w_ref[...], NN)

        @pl.when(j == steps - 1)
        def _():
            hat, _ = norm_parts(h_ref[...])
            b_ref[...] = (hat * gain_ref[1:2]).astype(BF)

    return call(
        kernel,
        "project",
        flops=2 * rows * D * D,
        moved=2 * D * D + 10 * rows * D,
        grid=(steps,),
        in_specs=[
            whole((rows, D)),
            whole((rows, D)),
            whole((8, D)),
            pl.BlockSpec((D, block), lambda j: (0, 3 * D // block + j)),
        ],
        out_specs=[whole((rows, D)), whole((rows, D))],
        out_shape=[shaped((rows, D), F32), shaped((rows, D))],
    )(x, o, gains, wide)


def ffn_in(b, w_in, keep):
    rows = b.shape[0]
    steps = FFP // FFB

    def kernel(b_ref, wa_ref, wg_ref, z_ref, *kept):
        a = dot(b_ref[...], wa_ref[...], NN)
        g = dot(b_ref[...], wg_ref[...], NN)
        phi = 0.5 * (1.0 + lax.erf(a * 0.7071067811865476))
        act = a * phi
        z_ref[...] = (act * g).astype(BF)
        if keep:
            density = 0.3989422804014327 * jnp.exp(-0.5 * a * a)
            kept[0][...] = act.astype(BF)
            kept[1][...] = ((phi + a * density) * g).astype(BF)

    out_spec = pl.BlockSpec((rows, FFB), lambda j: (0, j))
    count = 3 if keep else 1
    return call(
        kernel,
        "ffn_in",
        flops=4 * rows * D * FFP,
        moved=2 * (2 * D * FFP + rows * D + count * rows * FFP),
        grid=(steps,),
        in_specs=[
            whole((rows, D)),
            pl.BlockSpec((D, FFB), lambda j: (0, j)),
            pl.BlockSpec((D, FFB), lambda j: (0, steps + j)),
        ],
        out_specs=[out_spec] * count,
        out_shape=[shaped((rows, FFP))] * count,
    )(b, w_in, w_in)


def ffn_out(h, z, w_back):
    rows = h.shape[0]
    block = 256

    def kernel(h_ref, z_ref, w_ref, out_ref):
        out_ref[...] = (h_ref[...] + dot(z_ref[...], w_ref[...], NT)).astype(BF)

    return call(
        kernel,
        "ffn_out",
        flops=2 * rows * D * FFP,
        moved=2 * (D * FFP + rows * FFP + 3 * rows * D),
        grid=(D // block,),
        in_specs=[
            pl.BlockSpec((rows, block), lambda j: (0, j)),
            whole((rows, FFP)),
            pl.BlockSpec((block, FFP), lambda j: (j, 0)),
        ],
        out_specs=pl.BlockSpec((rows, block), lambda j: (0, j)),
        out_shape=shaped((rows, D)),
    )(h, z, w_back)


def ffn_back(grad, act, slope, w_back):
    rows = grad.shape[0]

    def kernel(g_ref, act_ref, slope_ref, w_ref, da_ref, dg_ref):
        dz = dot(g_ref[...], w_ref[...], NN)
        da_ref[...] = (dz * slope_ref[...].astype(F32)).astype(BF)
        dg_ref[...] = (dz * act_ref[...].astype(F32)).astype(BF)

    spec = pl.BlockSpec((rows, FFB), lambda j: (0, j))
    return call(
        kernel,
        "ffn_back",
        flops=2 * rows * D * FFP,
        moved=2 * (D * FFP + 4 * rows * FFP + rows * D),
        grid=(FFP // FFB,),
        in_specs=[whole((rows, D)), spec, spec, pl.BlockSpec((D, FFB), lambda j: (0, j))],
        out_specs=[spec, spec],
        out_shape=[shaped((rows, FFP))] * 2,
    )(grad, act, slope, w_back)


def hidden_back(grad, da, dg, h, gains, w_in):
    rows = grad.shape[0]
    block = 256
    steps = D // block

    def kernel(g_ref, da_ref, dg_ref, h_ref, gain_ref, w_ref, dh_ref, low_ref, sum_ref):
        j = pl.program_id(0)
        at = pl.ds(pl.multiple_of(j * block, block), block)
        dh_ref[:, at] = dot(da_ref[...], w_ref[:, :FFP], NT) + dot(dg_ref[...], w_ref[:, FFP:], NT)

        @pl.when(j == steps - 1)
        def _():
            back, total = norm_back(h_ref[...], gain_ref[1:2], dh_ref[...])
            dh = g_ref[...].astype(F32) + back
            dh_ref[...] = dh
            low_ref[...] = dh.astype(BF)
            sum_ref[...] = total

    return call(
        kernel,
        "hidden_back",
        flops=4 * rows * D * FFP,
        moved=2 * (2 * D * FFP + 2 * rows * FFP + 6 * rows * D),
        grid=(steps,),
        in_specs=[
            whole((rows, D)),
            whole((rows, FFP)),
            whole((rows, FFP)),
            whole((rows, D)),
            whole((8, D)),
            pl.BlockSpec((block, 2 * FFP), lambda j: (j, 0)),
        ],
        out_specs=[whole((rows, D)), whole((rows, D)), whole((1, D))],
        out_shape=[shaped((rows, D), F32), shaped((rows, D)), shaped((1, D), F32)],
    )(grad, da, dg, h, gains, w_in)


def attend_back(q, kv_list, dh_low, o, lse, segq, segk, wide, cosine, sine):
    rows = q.shape[0]
    members = len(kv_list)
    keys = members * rows

    def kernel(q_ref, dh_ref, w_ref, o_ref, lse_ref, segq_ref, segk_ref, cos_ref, sin_ref, *refs):
        kv_refs, (dq_ref, *dkv_refs, bias_ref) = refs[:members], refs[members:]

        @pl.when(pl.program_id(0) == 0)
        def _():
            bias_ref[...] = jnp.where(segk_ref[...] == segq_ref[...], 0.0, NEG_FILL)

        k = jnp.concatenate([r[:, :LANES] for r in kv_refs], axis=0)
        v = jnp.concatenate([r[:, LANES:] for r in kv_refs], axis=0)
        do = dot(dh_ref[...], w_ref[...], NT).astype(BF)
        q = q_ref[...] * jnp.asarray(HEAD_DIM**-0.5, BF)
        prod = (do.astype(F32) * o_ref[...].astype(F32)).T
        lse = lse_ref[0]
        dq = dk = dv = 0.0
        for head in range(2):
            mask = head_mask(q.shape, head)
            qh, doh = pick(mask, q), pick(mask, do)
            kh = pick(head_mask(k.shape, head), k)
            delta = jnp.sum(prod[head * HEAD_DIM : (head + 1) * HEAD_DIM], axis=0, keepdims=True)
            s = dot(k, qh, NT) + bias_ref[...]
            p = jnp.exp(s - lse[head : head + 1])
            ds = (p * (dot(v, doh, NT) - delta)).astype(BF)
            dv += dot(p.astype(BF), doh, NN)
            dk += dot(ds, qh, NN)
            dq += dot(ds, kh, TN)
        dq = rope_block(dq * HEAD_DIM**-0.5, cos_ref[...], -sin_ref[...])
        dq_ref[...] = dq.astype(BF)
        for m, out in enumerate(dkv_refs):
            out[:, :LANES] = dk[m * rows : (m + 1) * rows].astype(BF)
            out[:, LANES:] = dv[m * rows : (m + 1) * rows].astype(BF)

    spec = pl.BlockSpec((rows, LANES), lambda p: (0, p))
    kv_spec = pl.BlockSpec((rows, 2 * LANES), lambda p: (0, p))
    results = call(
        kernel,
        "attend_back",
        flops=20 * rows * keys * D,
        moved=2 * (6 * rows * D + 4 * keys * D),
        exps=rows * keys * HEADS,
        grid=(PAIRS,),
        in_specs=[
            spec,
            whole((rows, D)),
            pl.BlockSpec((LANES, D), lambda p: (p, 3)),
            spec,
            pl.BlockSpec((1, 2, rows), lambda p: (p, 0, 0)),
            whole((1, rows)),
            whole((keys, 1)),
            whole((rows, LANES)),
            whole((rows, LANES)),
        ]
        + [kv_spec] * members,
        out_specs=[spec] + [kv_spec] * members,
        out_shape=[shaped((rows, D))] + [shaped((rows, 2 * D))] * members,
        scratch_shapes=[pltpu.VMEM((keys, rows), F32)],
    )(q, dh_low, wide, o, lse, segq, segk, cosine, sine, *kv_list)
    return results[0], results[1:]


def input_back(x, dh, dq, dkv_list, gains, wide, cosine, sine):
    rows = x.shape[0]
    members = len(dkv_list)
    block = 256
    steps = D // block

    def kernel(x_ref, dh_ref, dq_ref, gain_ref, w_ref, cos_ref, sin_ref, *refs):
        dkv_refs, (dx_ref, dm_ref, sum_ref, da_ref) = refs[:members], refs[members:]
        j = pl.program_id(0)

        @pl.when(j == 0)
        def _():
            for b in range(2 * PAIRS):
                at = slice(b * LANES, (b + 1) * LANES)
                v = dkv_refs[0][:, at].astype(F32)
                for r in dkv_refs[1:]:
                    v += r[:, at].astype(F32)
                if b % 2 == 0:
                    v = rope_block(v, cos_ref[...], -sin_ref[...])
                dm_ref[:, at] = v.astype(BF)

        at = pl.ds(pl.multiple_of(j * block, block), block)
        da_ref[:, at] = dot(dm_ref[...], w_ref[:, : 2 * D], NT) + dot(
            dq_ref[...], w_ref[:, 2 * D :], NT
        )

        @pl.when(j == steps - 1)
        def _():
            back, total = norm_back(x_ref[...].astype(F32), gain_ref[0:1], da_ref[...])
            dx_ref[...] = (dh_ref[...] + back).astype(BF)
            sum_ref[...] = total

    return call(
        kernel,
        "input_back",
        flops=6 * rows * D * D,
        moved=2 * (3 * D * D + (2 * members + 7) * rows * D),
        grid=(steps,),
        in_specs=[
            whole((rows, D)),
            whole((rows, D)),
            whole((rows, D)),
            whole((8, D)),
            pl.BlockSpec((block, 3 * D), lambda j: (j, 0)),
            whole((rows, LANES)),
            whole((rows, LANES)),
        ]
        + [whole((rows, 2 * D))] * members,
        out_specs=[whole((rows, D)), whole((rows, 2 * D)), whole((1, D))],
        out_shape=[shaped((rows, D)), shaped((rows, 2 * D)), shaped((1, D), F32)],
        scratch_shapes=[pltpu.VMEM((rows, D), F32)],
    )(x, dh, dq, gains, wide, cosine, sine, *dkv_list)


def weight_rows(order, rows, pairs, extra=None):
    count = order.shape[0]
    tokens = pairs[0][0].shape[0]
    flat, columns = [], 0
    for left, rights in pairs:
        flat += [left] + list(rights)
        columns += sum(r.shape[1] for r in rights)
    if extra is not None:
        flat.append(extra)
        columns += LANES

    def kernel(order_ref, *refs):
        ins, out_ref, turned_ref, left_ref = refs[:-3], refs[-3], refs[-2], refs[-1]
        at = where = 0
        for left, rights in pairs:
            turned_ref[...] = ins[where][...].T
            where += 1
            for n in range(count):
                start = pl.multiple_of(order_ref[n] * rows, rows)
                left_ref[n * rows : (n + 1) * rows] = turned_ref[pl.ds(start, rows)]
            for right in rights:
                width = right.shape[1]
                for begin in range(0, width, 512):
                    end = min(begin + 512, width)
                    out_ref[:, at + begin : at + end] = dot(
                        left_ref[...], ins[where][:, begin:end], NN
                    ).astype(BF)
                at += width
                where += 1
        if extra is not None:
            for n in range(count):
                start = pl.multiple_of(order_ref[n] * rows, rows)
                out_ref[n * rows : (n + 1) * rows, at:] = ins[where][pl.ds(start, rows)]

    return call(
        kernel,
        "weight_rows",
        flops=2 * count * rows * tokens * columns,
        moved=2 * (count * rows * columns + sum(v.size for v in flat)),
        in_specs=[SMEM_SPEC] + [pl.BlockSpec(memory_space=pltpu.VMEM)] * len(flat),
        out_specs=pl.BlockSpec(memory_space=pltpu.VMEM),
        out_shape=shaped((count * rows, columns)),
        scratch_shapes=[
            pltpu.VMEM((D, tokens), BF),
            pltpu.VMEM((count * rows, tokens), BF),
        ],
    )(order, *flat)


def ring_add(core, mine, other, moving, rows, first, blocks, partial_moving):
    columns = mine.shape[1]

    def kernel(core_ref, mine_ref, other_ref, *refs):
        total = mine_ref[...].astype(F32) + other_ref[...].astype(F32)
        if moving is None:
            refs[0][...] = total.astype(BF)
            return
        moved = refs[0][...].astype(F32)
        if partial_moving:
            moved = jnp.where(core_ref[0] == pl.program_id(0), moved, 0.0)
        refs[1][...] = (total + moved).astype(BF)

    spec = pl.BlockSpec((rows, columns), lambda j: (first + j, 0))
    ins, specs = [core, mine, other], [SMEM_SPEC, spec, spec]
    if moving is not None:
        ins.append(moving)
        specs.append(
            pl.BlockSpec((rows, columns), (lambda j: (0, 0)) if partial_moving else (lambda j: (j, 0)))
        )
    return call(
        kernel,
        "ring_add",
        flops=2 * blocks * rows * columns,
        moved=8 * blocks * rows * columns,
        grid=(blocks,),
        in_specs=specs,
        out_specs=pl.BlockSpec((rows, columns), lambda j: (j, 0)),
        out_shape=shaped((blocks * rows, columns)),
    )(*ins)


class Plan:
    def __init__(self, boundary):
        self.micro = boundary.shape[1]
        self.tok_rows = boundary.shape[3]
        self.n_ctx = lax.axis_size("ctx")
        self.nw = lax.axis_size("wshard")
        self.g = self.n_ctx // (self.micro * self.nw)
        self.r = self.tok_rows // (self.g * self.nw)
        self.i = lax.axis_index("ctx")
        self.w = lax.axis_index("wshard")
        self.rows = self.n_ctx * self.r
        self.members = self.g * self.nw
        count = self.n_ctx
        chips = [2 * p if p < count // 2 else 2 * (count - 1 - p) + 1 for p in range(count)]
        self.half = count // 2
        self.way = 1 - 2 * self.w
        self.ring_pairs = []
        for p in range(count):
            self.ring_pairs.append((chips[p] * 2, chips[(p + 1) % count] * 2))
            self.ring_pairs.append((chips[p] * 2 + 1, chips[(p - 1) % count] * 2 + 1))
        place = jnp.where(self.i % 2 == 0, self.i // 2, count - 1 - self.i // 2)

        def chip(at):
            at = at % count
            return jnp.where(at < count // 2, 2 * at, 2 * (count - 1 - at) + 1)

        self.behind = [chip(place - self.way * k) for k in range(self.half + 1)]
        self.ahead = [chip(place + self.way * k) for k in range(self.half + 1)]
        self.wrows = D // (self.n_ctx * self.nw)
        near = range(self.half - 1, 0, -1)
        theirs = [2 * self.ahead[self.half] + 1 - self.w]
        mine = [2 * self.ahead[self.half] + self.w]
        for k in near:
            theirs += [2 * self.behind[k], 2 * self.behind[k] + 1]
            mine += [2 * self.ahead[k], 2 * self.ahead[k] + 1]
        mine += [2 * self.i, 2 * self.i + 1]
        self.theirs = jnp.stack(theirs).astype(jnp.int32)
        self.mine = jnp.stack(mine).astype(jnp.int32)
        self.core = self.w[None].astype(jnp.int32)

    def swap(self, array):
        return lax.ppermute(array, "wshard", [(0, 1), (1, 0)])

    def step(self, array):
        return lax.ppermute(array, BOTH, self.ring_pairs)

    def in_order(self, own, other):
        first = self.w == 0
        return jnp.concatenate(
            [jnp.where(first, own, other), jnp.where(first, other, own)], axis=0
        )

    def to_sequences(self, local):
        parts = local.reshape(self.micro, self.g, self.nw, self.r, D)
        parts = lax.all_to_all(parts.transpose(2, 0, 1, 3, 4), "wshard", 0, 0, tiled=True)
        parts = parts.transpose(1, 0, 2, 3, 4).reshape(self.n_ctx, self.r, D)
        return lax.all_to_all(parts, "ctx", 0, 0, tiled=True).reshape(self.rows, D)

    def from_sequences(self, rows):
        parts = lax.all_to_all(rows.reshape(self.n_ctx, self.r, D), "ctx", 0, 0, tiled=True)
        parts = parts.reshape(self.micro, self.nw, self.g, self.r, D).transpose(1, 0, 2, 3, 4)
        parts = lax.all_to_all(parts, "wshard", 0, 0, tiled=True)
        return parts.transpose(1, 2, 0, 3, 4).reshape(self.micro, self.tok_rows, D)

    def gather_weights(self, streams):
        whole_of, token = {}, {}
        rows = self.wrows

        def put(name, block, chip):
            whole_of[name] = lax.dynamic_update_index_in_dim(whole_of[name], block, chip, 0)

        def travel(name, shard, dep):
            whole_of[name] = jnp.zeros((self.n_ctx, self.nw * rows, shard.shape[1]), BF)
            current = self.in_order(shard, self.swap(shard))
            put(name, current, self.i)
            if dep is not None:
                current = after(current, dep)
            for k in range(1, self.half):
                current = self.step(current)
                yield current
                put(name, current, self.behind[k])
                put(name, self.swap(current), self.ahead[k])
            part = lax.dynamic_slice_in_dim(current, self.w * rows, rows, 0)
            part = self.step(part)
            yield part
            put(name, self.in_order(part, self.swap(part)), self.behind[self.half])

        def lane(items):
            dep = None
            for name, shard in items:
                for dep in travel(name, shard, dep):
                    yield dep

        lanes = [lane(items) for items in streams]
        while lanes:
            for one in list(lanes):
                if next(one, None) is None:
                    lanes.remove(one)
        return {n: v.reshape(D, v.shape[2]) for n, v in whole_of.items()}

    def reduce_weights(self, pairs, extra=None):
        rows = self.wrows
        other = self.swap(weight_rows(self.theirs, rows, pairs, extra))
        mine = weight_rows(self.mine, rows, pairs, extra)
        moving = self.step(ring_add(self.core, mine, other, None, rows, 0, 1, False))
        at = 1
        for k in range(self.half - 1, 0, -1):
            moving = self.step(
                ring_add(self.core, mine, other, moving, rows, at, 2, k == self.half - 1)
            )
            at += 2
        final = moving.astype(F32) + mine[at * rows :].astype(F32)
        keep = lax.dynamic_slice_in_dim(final, self.w * rows, rows, 0)
        give = lax.dynamic_slice_in_dim(final, (1 - self.w) * rows, rows, 0)
        return keep + self.swap(give.astype(BF)).astype(F32)

    def rotation(self, by):
        pairs = []
        for flat in range(self.n_ctx * self.nw):
            group, place = divmod(flat, self.members)
            pairs.append((flat, group * self.members + (place + by) % self.members))
        return pairs

    def gather_rows(self, rows):
        return [rows] + [
            lax.ppermute(rows, BOTH, self.rotation(by)) for by in range(1, self.members)
        ]

    def scatter_rows(self, terms):
        return [terms[0]] + [
            lax.ppermute(terms[by], BOTH, self.rotation(-by)) for by in range(1, self.members)
        ]


def interleave(keys, values):
    lead = keys.shape[0]
    both = jnp.stack([keys.reshape(lead, PAIRS, LANES), values.reshape(lead, PAIRS, LANES)], axis=2)
    return both.reshape(lead, 2 * D)


def apart(both):
    lead = both.shape[0]
    both = both.reshape(lead, PAIRS, 2, LANES)
    return both[:, :, 0].reshape(lead, D), both[:, :, 1].reshape(lead, D)


def body(
    boundary, segment_ids, qkv_weight, attn_out_weight, ffn_in_weight, ffn_out_weight, norm_gains
):
    section = lax.axis_index("section")
    sections = lax.axis_size("section")
    plan = Plan(boundary)
    rows = plan.rows
    own = plan.to_sequences(boundary[0, :, 0])

    pad = FFP - FF
    wide_shard = jnp.concatenate(
        [
            interleave(qkv_weight[0][:, D : 2 * D], qkv_weight[0][:, 2 * D :]),
            qkv_weight[0][:, :D],
            attn_out_weight[0],
            jnp.pad(norm_gains[0].T, ((0, 0), (0, LANES - 2))),
        ],
        axis=1,
    )
    in_shard = jnp.concatenate(
        [
            jnp.pad(ffn_in_weight[0][:, :FF], ((0, 0), (0, pad))),
            jnp.pad(ffn_in_weight[0][:, FF:], ((0, 0), (0, pad))),
        ],
        axis=1,
    )
    back_shard = jnp.pad(ffn_out_weight[0].T, ((0, 0), (0, pad)))
    weights = plan.gather_weights(
        [[("wide", wide_shard), ("back", back_shard)], [("in", in_shard)]]
    )
    wide, w_in, w_back = weights["wide"], weights["in"], weights["back"]
    gains = gains_of(wide)

    ids = segment_ids[:, 0]
    ids = plan.in_order(ids[None], plan.swap(ids[None])).transpose(1, 0, 2)
    ids = jnp.repeat(ids.reshape(plan.micro * plan.nw, plan.tok_rows), plan.g, axis=0)
    line = lax.all_to_all(ids, "ctx", 0, 0, tiled=True).reshape(-1)
    grid = line.reshape(plan.n_ctx, plan.members, plan.r)
    place = (plan.i % plan.g) * plan.nw + plan.w
    seg_pieces = [
        lax.dynamic_index_in_dim(grid, (place - by) % plan.members, 1, keepdims=False).reshape(rows)
        for by in range(plan.members)
    ]
    segq = seg_pieces[0]
    segk = jnp.concatenate(seg_pieces)
    token = (
        lax.broadcasted_iota(jnp.int32, (plan.n_ctx, plan.r), 0) * plan.tok_rows
        + place * plan.r
        + lax.broadcasted_iota(jnp.int32, (plan.n_ctx, plan.r), 1)
    ).reshape(rows)
    first = jnp.sum((line[None, :] < segq[:, None]).astype(jnp.int32), axis=1)
    position = (token - first).astype(F32)
    exponent = jnp.arange(HEAD_DIM // 2, dtype=F32) * (-2.0 / HEAD_DIM)
    angles = position[:, None] * (ROPE_BASE**exponent)[None, :]
    cosine, sine = jnp.cos(angles), jnp.sin(angles)
    cos_rows = jnp.concatenate([cosine] * 4, axis=1)
    sin_rows = jnp.concatenate([-sine, sine] * 2, axis=1)
    segq_row, segk_col = segq[None, :], segk[:, None]

    def forward(x, keep):
        a, kv = keys_values(x, gains, wide, cos_rows, sin_rows)
        kv_list = plan.gather_rows(kv)
        q = queries_of(a, wide, cos_rows, sin_rows)
        o, lse = attend(q, kv_list, segq_row, segk_col)
        h, b = project(x, o, gains, wide)
        z, *kept = ffn_in(b, w_in, keep)
        out = ffn_out(h, z, w_back)
        return out, (x, a, q, kv_list, o, lse, h, b, z, kept)

    def backward(stash, grad, with_weights):
        x, a, q, kv_list, o, lse, h, b, z, (act, slope) = stash
        sums = []
        if with_weights:
            sums.append(plan.reduce_weights([(grad, [z])]))
        da, dg = ffn_back(grad, act, slope, w_back)
        if with_weights:
            sums.append(plan.reduce_weights([(b, [da, dg])]))
        dh, dh_low, gain_second = hidden_back(grad, da, dg, h, gains, w_in)
        dq, terms = attend_back(
            q, kv_list, dh_low, o, lse, segq_row, segk_col, wide, cos_rows, sin_rows
        )
        dkv_list = plan.scatter_rows(terms)
        dx, dkv, gain_first = input_back(x, dh, dq, dkv_list, gains, wide, cos_rows, sin_rows)
        if with_weights:
            cols = jnp.concatenate([gain_first, gain_second], axis=0).T
            cols = jnp.pad(cols, ((0, 0), (0, LANES - 2))).astype(BF)
            sums.append(plan.reduce_weights([(a, [dkv, dq]), (o, [dh_low])], cols))
        return dx, sums

    def handed(array, by):
        pairs = [(s, s + by) for s in range(sections) if 0 <= s + by < sections]
        return lax.ppermute(array, "section", pairs)

    first_out, _ = forward(own, False)
    x_in = jnp.where(section == 0, own, handed(first_out, 1))
    out, stash = forward(x_in, True)
    first_dx, _ = backward(stash, own, False)
    grad_in = jnp.where(section == sections - 1, own, handed(first_dx, -1))
    dx, (g_back, g_in, g_wide) = backward(stash, grad_in, True)
    boundary_local = plan.from_sequences(jnp.where(section == 0, dx, out))
    g_key, g_value = apart(g_wide[:, : 2 * D])
    return (
        boundary_local[None, :, None],
        jnp.concatenate([g_wide[:, 2 * D : 3 * D], g_key, g_value], axis=1)[None],
        g_wide[None, :, 3 * D : 4 * D],
        jnp.concatenate([g_in[:, :FF], g_in[:, FFP : FFP + FF]], axis=1)[None],
        g_back[:, :FF].T[None],
        g_wide[:, 4 * D : 4 * D + 2].T[None],
    )


def solution(mesh):
    placed = (
        P("section", None, "wshard", "ctx", None),
        P(None, "wshard", "ctx"),
        P("section", ("ctx", "wshard"), None),
        P("section", ("ctx", "wshard"), None),
        P("section", ("ctx", "wshard"), None),
        P("section", None, ("ctx", "wshard")),
        P("section", None, ("ctx", "wshard")),
    )
    return jax.shard_map(
        body,
        mesh=mesh,
        in_specs=placed,
        out_specs=(placed[0],) + placed[2:],
        check_vma=False,
    )
```

```python
from functools import partial

import jax
import jax.numpy as jnp
from jax import lax
from jax.experimental import pallas as pl
from jax.experimental.pallas import tpu as pltpu
from jax.sharding import PartitionSpec as P

D = 1024
HEADS = 16
HEAD_DIM = 64
FF = 2624
FFP = 2688
FFB = 896
LANES = 128
PAIRS = D // LANES
EPSILON = 1e-05
ROPE_BASE = 160000.0
NEG_FILL = -1e30
BF = jnp.bfloat16
F32 = jnp.float32
BOTH = ("ctx", "wshard")
IDS = 16
PENALTY = -(2.0**100)
NN = ((1,), (0,))
NT = ((1,), (1,))
TN = ((0,), (0,))
SMEM_SPEC = pl.BlockSpec(memory_space=pltpu.SMEM)


def dot(a, b, dims):
    return lax.dot_general(a, b, (dims, ((), ())), preferred_element_type=F32)


def after(value, *others):
    return lax.optimization_barrier((value,) + others)[0]


def shaped(shape, kind=BF):
    return jax.ShapeDtypeStruct(shape, kind)


def call(kernel, name, limit=20, flops=0, moved=0, exps=0, **more):
    return pl.pallas_call(
        kernel,
        name=name,
        compiler_params=pltpu.CompilerParams(vmem_limit_bytes=limit * 1024 * 1024),
        cost_estimate=pl.CostEstimate(
            flops=int(flops), bytes_accessed=int(moved), transcendentals=int(exps)
        ),
        **more,
    )


def whole(shape):
    return pl.BlockSpec(shape, lambda *_: (0,) * len(shape))


def rope_block(v, cosine, sine):
    lane = lax.broadcasted_iota(jnp.int32, v.shape, 1) % HEAD_DIM
    other = jnp.where(
        lane < HEAD_DIM // 2,
        pltpu.roll(v, LANES - HEAD_DIM // 2, 1),
        pltpu.roll(v, HEAD_DIM // 2, 1),
    )
    return v * cosine + other * sine


def norm_parts(values):
    center = values - jnp.mean(values, axis=-1, keepdims=True)
    spread = jnp.mean(center * center, axis=-1, keepdims=True)
    inverse = lax.rsqrt(spread + EPSILON)
    return center * inverse, inverse


def norm_back(values, gain_row, grad):
    hat, inverse = norm_parts(values)
    scaled = grad * gain_row
    back = inverse * (
        scaled
        - jnp.mean(scaled, axis=-1, keepdims=True)
        - hat * jnp.mean(scaled * hat, axis=-1, keepdims=True)
    )
    return back, jnp.sum(grad * hat, axis=0, keepdims=True)


def head_mask(shape, head):
    lane = lax.broadcasted_iota(jnp.int32, shape, 1)
    return (lane >= HEAD_DIM) if head else (lane < HEAD_DIM)


def pick(mask, v, other=0.0):
    return jnp.where(mask, v, jnp.full(v.shape, other, v.dtype))


def gains_of(w_mix):
    def kernel(w_ref, out_ref):
        out_ref[...] = w_ref[...].astype(F32).T[:8]

    return call(
        kernel,
        "gains",
        grid=(1,),
        in_specs=[pl.BlockSpec((D, LANES), lambda j: (0, 4 * D // LANES))],
        out_specs=whole((8, D)),
        out_shape=shaped((8, D), F32),
    )(w_mix)


def keys_values(x, gains, w_kv, cosine, sine):
    rows = x.shape[0]
    block = 512

    def kernel(x_ref, gain_ref, w_ref, cos_ref, sin_ref, a_ref, out_ref):
        @pl.when(pl.program_id(0) == 0)
        def _():
            hat, _ = norm_parts(x_ref[...].astype(F32))
            a_ref[...] = (hat * gain_ref[0:1]).astype(BF)

        m = dot(a_ref[...], w_ref[...], NN)
        for j in range(block // LANES):
            at = slice(j * LANES, (j + 1) * LANES)
            v = m[:, at]
            if j % 2 == 0:
                v = rope_block(v, cos_ref[...], sin_ref[...])
            out_ref[:, at] = v.astype(BF)

    return call(
        kernel,
        "keys_values",
        flops=2 * rows * D * 2 * D,
        moved=2 * (2 * D * D + 4 * rows * D),
        grid=(2 * D // block,),
        in_specs=[
            whole((rows, D)),
            whole((8, D)),
            pl.BlockSpec((D, block), lambda j: (0, j)),
            whole((rows, LANES)),
            whole((rows, LANES)),
        ],
        out_specs=[whole((rows, D)), pl.BlockSpec((rows, block), lambda j: (0, j))],
        out_shape=[shaped((rows, D)), shaped((rows, 2 * D))],
    )(x, gains, w_kv, cosine, sine)


def queries_of(a, w_mix, cosine, sine):
    rows = a.shape[0]
    block = 512

    def kernel(a_ref, w_ref, cos_ref, sin_ref, out_ref):
        m = dot(a_ref[...], w_ref[...], NN)
        for j in range(block // LANES):
            at = slice(j * LANES, (j + 1) * LANES)
            out_ref[:, at] = rope_block(m[:, at], cos_ref[...], sin_ref[...]).astype(BF)

    return call(
        kernel,
        "queries",
        flops=2 * rows * D * D,
        moved=2 * (D * D + 2 * rows * D),
        grid=(D // block,),
        in_specs=[
            whole((rows, D)),
            pl.BlockSpec((D, block), lambda j: (0, 2 * D // block + j)),
            whole((rows, LANES)),
            whole((rows, LANES)),
        ],
        out_specs=pl.BlockSpec((rows, block), lambda j: (0, j)),
        out_shape=shaped((rows, D)),
    )(a, w_mix, cosine, sine)


def key_marks(seg):
    lane = jnp.arange(LANES) % HEAD_DIM
    return jnp.where(lane < IDS, (seg[:, None] == lane), lane < IDS + 3).astype(BF)
def query_marks(seg):
    lane = jnp.arange(LANES) % HEAD_DIM
    return jnp.where((lane < IDS) & (seg[:, None] != lane), PENALTY, 0.0).astype(BF)

def split3(v):
    a = v.astype(BF).astype(F32)
    b = (v - a).astype(BF).astype(F32)
    return a, b, v - a - b


def attend(q, kv_list, qmarks, kmarks, begin, count):
    rows = q.shape[0]
    members = len(kv_list)
    keys = members * rows

    def kernel(q_ref, qm_ref, km_ref, *refs):
        kv_refs, (o_ref, lse_ref) = refs[:members], refs[members:]
        k = jnp.concatenate([r[:, :LANES] for r in kv_refs], axis=0)
        v = jnp.concatenate([r[:, LANES:] for r in kv_refs], axis=0)
        q = q_ref[...] * jnp.asarray(HEAD_DIM**-0.5, BF)
        parts, stats = [], []
        for head in range(2):
            mine = head_mask((rows, LANES), head)
            theirs = head_mask((keys, LANES), head)
            s = dot(jnp.where(theirs, k, km_ref[...]), jnp.where(mine, q, qm_ref[...]), NT)
            top = jnp.max(s, axis=0, keepdims=True)
            e = jnp.exp(s - top).astype(BF)
            u = dot(pick(theirs, v, 1.0), e, TN)
            low, high = u[:HEAD_DIM], u[HEAD_DIM:]
            value, total = (high, low) if head else (low, high)
            parts.append(value / total)
            stats.append(top + jnp.log(total[:1]))
        o_ref[...] = jnp.concatenate(parts, axis=0).T.astype(BF)
        lse_ref[0] = jnp.concatenate(stats, axis=0)

    return call(
        kernel,
        "attend",
        flops=8 * rows * keys * count * LANES,
        moved=2 * (2 * rows + 2 * keys) * count * LANES,
        exps=rows * keys * count * 2,
        grid=(count,),
        in_specs=[
            pl.BlockSpec((rows, LANES), lambda p: (0, begin + p)),
            whole((rows, LANES)),
            whole((keys, LANES)),
        ]
        + [pl.BlockSpec((rows, 2 * LANES), lambda p: (0, begin + p))] * members,
        out_specs=[
            pl.BlockSpec((rows, LANES), lambda p: (0, p)),
            pl.BlockSpec((1, 2, rows), lambda p: (p, 0, 0)),
        ],
        out_shape=[shaped((rows, count * LANES)), shaped((count, 2, rows), F32)],
    )(q, qmarks, kmarks, *kv_list)

def project(x, o_list, gains, w_mix):
    rows = x.shape[0]
    block = 512
    steps = D // block

    def kernel(x_ref, gain_ref, w_ref, *refs):
        o_refs, (h_ref, b_ref) = refs[:-2], refs[-2:]
        j = pl.program_id(0)
        at = pl.ds(pl.multiple_of(j * block, block), block)
        total = x_ref[:, at].astype(F32)
        begin = 0
        for o_ref in o_refs:
            end = begin + o_ref.shape[1]
            total += dot(o_ref[...], w_ref[begin:end], NN)
            begin = end
        h_ref[:, at] = total

        @pl.when(j == steps - 1)
        def _():
            hat, _ = norm_parts(h_ref[...])
            b_ref[...] = (hat * gain_ref[1:2]).astype(BF)

    return call(
        kernel,
        "project",
        flops=2 * rows * D * D,
        moved=2 * D * D + 10 * rows * D,
        grid=(steps,),
        in_specs=[
            whole((rows, D)),
            whole((8, D)),
            pl.BlockSpec((D, block), lambda j: (0, 3 * D // block + j)),
        ]
        + [whole(o.shape) for o in o_list],
        out_specs=[whole((rows, D)), whole((rows, D))],
        out_shape=[shaped((rows, D), F32), shaped((rows, D))],
    )(x, gains, w_mix, *o_list)


def ffn_in(b, w_in, w_gate, keep):
    rows = b.shape[0]
    steps = FFP // FFB

    def kernel(b_ref, wa_ref, wg_ref, z_ref, *kept):
        a = dot(b_ref[...], wa_ref[...], NN)
        g = dot(b_ref[...], wg_ref[...], NN)
        phi = 0.5 * (1.0 + lax.erf(a * 0.7071067811865476))
        act = a * phi
        z_ref[...] = (act * g).astype(BF)
        if keep:
            density = 0.3989422804014327 * jnp.exp(-0.5 * a * a)
            kept[0][...] = act.astype(BF)
            kept[1][...] = ((phi + a * density) * g).astype(BF)

    out_spec = pl.BlockSpec((rows, FFB), lambda j: (0, j))
    count = 3 if keep else 1
    return call(
        kernel,
        "ffn_in",
        flops=4 * rows * D * FFP,
        moved=2 * (2 * D * FFP + rows * D + count * rows * FFP),
        grid=(steps,),
        in_specs=[whole((rows, D))] + [pl.BlockSpec((D, FFB), lambda j: (0, j))] * 2,
        out_specs=[out_spec] * count,
        out_shape=[shaped((rows, FFP))] * count,
    )(b, w_in, w_gate)


def ffn_out(h, z, w_back):
    rows = h.shape[0]
    block = 256

    def kernel(h_ref, z_ref, w_ref, out_ref):
        out_ref[...] = (h_ref[...] + dot(z_ref[...], w_ref[...], NT)).astype(BF)

    return call(
        kernel,
        "ffn_out",
        flops=2 * rows * D * FFP,
        moved=2 * (D * FFP + rows * FFP + 3 * rows * D),
        grid=(D // block,),
        in_specs=[
            pl.BlockSpec((rows, block), lambda j: (0, j)),
            whole((rows, FFP)),
            pl.BlockSpec((block, FFP), lambda j: (j, 0)),
        ],
        out_specs=pl.BlockSpec((rows, block), lambda j: (0, j)),
        out_shape=shaped((rows, D)),
    )(h, z, w_back)


def ffn_back(grad, act, slope, w_back):
    rows = grad.shape[0]

    def kernel(g_ref, act_ref, slope_ref, w_ref, da_ref, dg_ref):
        dz = dot(g_ref[...], w_ref[...], NN)
        da_ref[...] = (dz * slope_ref[...].astype(F32)).astype(BF)
        dg_ref[...] = (dz * act_ref[...].astype(F32)).astype(BF)

    spec = pl.BlockSpec((rows, FFB), lambda j: (0, j))
    return call(
        kernel,
        "ffn_back",
        flops=2 * rows * D * FFP,
        moved=2 * (D * FFP + 4 * rows * FFP + rows * D),
        grid=(FFP // FFB,),
        in_specs=[whole((rows, D)), spec, spec, pl.BlockSpec((D, FFB), lambda j: (0, j))],
        out_specs=[spec, spec],
        out_shape=[shaped((rows, FFP))] * 2,
    )(grad, act, slope, w_back)


def hidden_back(grad, da, dg, h, gains, w_in, w_gate):
    rows = grad.shape[0]
    block = 256
    steps = D // block

    def kernel(g_ref, da_ref, dg_ref, h_ref, gain_ref, wa_ref, wg_ref, dh_ref, low_ref, sum_ref):
        j = pl.program_id(0)
        at = pl.ds(pl.multiple_of(j * block, block), block)
        dh_ref[:, at] = dot(da_ref[...], wa_ref[...], NT) + dot(dg_ref[...], wg_ref[...], NT)

        @pl.when(j == steps - 1)
        def _():
            back, total = norm_back(h_ref[...], gain_ref[1:2], dh_ref[...])
            dh = g_ref[...].astype(F32) + back
            dh_ref[...] = dh
            low_ref[...] = dh.astype(BF)
            sum_ref[...] = total

    return call(
        kernel,
        "hidden_back",
        flops=4 * rows * D * FFP,
        moved=2 * (2 * D * FFP + 2 * rows * FFP + 6 * rows * D),
        grid=(steps,),
        in_specs=[
            whole((rows, D)),
            whole((rows, FFP)),
            whole((rows, FFP)),
            whole((rows, D)),
            whole((8, D)),
        ]
        + [pl.BlockSpec((block, FFP), lambda j: (j, 0))] * 2,
        out_specs=[whole((rows, D)), whole((rows, D)), whole((1, D))],
        out_shape=[shaped((rows, D), F32), shaped((rows, D)), shaped((1, D), F32)],
    )(grad, da, dg, h, gains, w_in, w_gate)


def attend_back(q, kv_list, dh_low, o, lse, qmarks, kmarks, w_mix, cosine, sine, begin):
    count = o.shape[1] // LANES
    rows = q.shape[0]
    members = len(kv_list)
    keys = members * rows

    def kernel(q_ref, dh_ref, w_ref, o_ref, lse_ref, qm_ref, km_ref, cos_ref, sin_ref, *refs):
        kv_refs, (dq_ref, *dkv_refs) = refs[:members], refs[members:]
        k = jnp.concatenate([r[:, :LANES] for r in kv_refs], axis=0)
        v = jnp.concatenate([r[:, LANES:] for r in kv_refs], axis=0)
        do = dot(dh_ref[...], w_ref[...], NT).astype(BF)
        q = q_ref[...] * jnp.asarray(HEAD_DIM**-0.5, BF)
        prod = do.astype(F32) * o_ref[...].astype(F32)
        lse = lse_ref[0]
        row = lax.broadcasted_iota(jnp.int32, (LANES, rows), 0)
        beside = jnp.zeros((LANES, rows), F32)
        for head in range(2):
            for n, part in enumerate(split3(-lse[head : head + 1])):
                beside = jnp.where(row == IDS + n + (HEAD_DIM if head == 0 else 0), part, beside)
        beside = beside.T.astype(BF) + qm_ref[...]
        lane = lax.broadcasted_iota(jnp.int32, (rows, LANES), 1)
        dks, dvs, dqs = [], [], []
        for head in range(2):
            mine = head_mask((rows, LANES), head)
            theirs = head_mask((keys, LANES), head)
            delta = jnp.sum(jnp.where(mine, prod, 0.0), axis=1, keepdims=True)
            there = jnp.zeros((rows, LANES), F32)
            for n, part in enumerate(split3(-delta)):
                there = jnp.where(lane == IDS + n + (HEAD_DIM if head == 0 else 0), part, there)
            qh = jnp.where(mine, q, beside)
            doh = jnp.where(mine, do, there.astype(BF))
            kh = jnp.where(theirs, k, km_ref[...])
            vh = jnp.where(theirs, v, km_ref[...])
            p = jnp.exp(dot(kh, qh, NT))
            ds = (p * dot(vh, doh, NT)).astype(BF)
            dvs.append(dot(p.astype(BF), do, NN))
            dks.append(dot(ds, q, NN))
            dqs.append(dot(ds, k, TN))
        first = head_mask((rows, LANES), 0)
        dq = jnp.where(first, dqs[0], dqs[1])
        dq = rope_block(dq * HEAD_DIM**-0.5, cos_ref[...], -sin_ref[...])
        dq_ref[...] = dq.astype(BF)
        for m, out in enumerate(dkv_refs):
            cut = slice(m * rows, (m + 1) * rows)
            out[:, :LANES] = jnp.where(first, dks[0][cut], dks[1][cut]).astype(BF)
            out[:, LANES:] = jnp.where(first, dvs[0][cut], dvs[1][cut]).astype(BF)

    spec = pl.BlockSpec((rows, LANES), lambda p: (0, p))
    kv_spec = pl.BlockSpec((rows, 2 * LANES), lambda p: (0, p))
    results = call(
        kernel,
        "attend_back",
        flops=20 * rows * keys * count * LANES,
        moved=2 * (6 * rows + 4 * keys) * count * LANES,
        exps=rows * keys * 2 * count,
        grid=(count,),
        in_specs=[
            pl.BlockSpec((rows, LANES), lambda p: (0, begin + p)),
            whole((rows, D)),
            pl.BlockSpec((LANES, D), lambda p: (begin + p, 3)),
            spec,
            pl.BlockSpec((1, 2, rows), lambda p: (p, 0, 0)),
            whole((rows, LANES)),
            whole((keys, LANES)),
            whole((rows, LANES)),
            whole((rows, LANES)),
        ]
        + [pl.BlockSpec((rows, 2 * LANES), lambda p: (0, begin + p))] * members,
        out_specs=[spec] + [kv_spec] * members,
        out_shape=[shaped((rows, count * LANES))] + [shaped((rows, 2 * count * LANES))] * members,
    )(q, dh_low, w_mix, o, lse, qmarks, kmarks, cosine, sine, *kv_list)
    return results[0], results[1:]


def keys_back(terms, cosine, sine):
    rows, columns = terms[0].shape

    def kernel(cos_ref, sin_ref, *refs):
        for b in range(columns // LANES):
            at = slice(b * LANES, (b + 1) * LANES)
            v = refs[0][:, at].astype(F32)
            for r in refs[1:-1]:
                v += r[:, at].astype(F32)
            if b % 2 == 0:
                v = rope_block(v, cos_ref[...], -sin_ref[...])
            refs[-1][:, at] = v.astype(BF)

    return call(
        kernel,
        "keys_back",
        flops=10 * rows * columns,
        moved=2 * (len(terms) + 1) * rows * columns,
        grid=(1,),
        in_specs=[whole((rows, LANES))] * 2 + [whole((rows, columns))] * len(terms),
        out_specs=whole((rows, columns)),
        out_shape=shaped((rows, columns)),
    )(cosine, sine, *terms)


def input_back(x, dh, dq_list, dkv_list, gains, w_kv, w_mix):
    rows = x.shape[0]
    block = 256
    steps = D // block
    grads = list(dkv_list) + list(dq_list)

    def kernel(x_ref, dh_ref, gain_ref, wkv_ref, wq_ref, *refs):
        grad_refs, (dx_ref, sum_ref, da_ref) = refs[:-3], refs[-3:]
        j = pl.program_id(0)
        total = 0.0
        begin = 0
        for n, ref in enumerate(grad_refs):
            if n == len(dkv_list):
                begin = 0
            end = begin + ref.shape[1]
            w_ref = wkv_ref if n < len(dkv_list) else wq_ref
            total += dot(ref[...], w_ref[:, begin:end], NT)
            begin = end
        da_ref[:, pl.ds(pl.multiple_of(j * block, block), block)] = total

        @pl.when(j == steps - 1)
        def _():
            back, total = norm_back(x_ref[...].astype(F32), gain_ref[0:1], da_ref[...])
            dx_ref[...] = (dh_ref[...] + back).astype(BF)
            sum_ref[...] = total

    return call(
        kernel,
        "input_back",
        flops=6 * rows * D * D,
        moved=2 * (3 * D * D + 10 * rows * D),
        grid=(steps,),
        in_specs=[
            whole((rows, D)),
            whole((rows, D)),
            whole((8, D)),
            pl.BlockSpec((block, 2 * D), lambda j: (j, 0)),
            pl.BlockSpec((block, D), lambda j: (j, 2)),
        ]
        + [whole(g.shape) for g in grads],
        out_specs=[whole((rows, D)), whole((1, D))],
        out_shape=[shaped((rows, D)), shaped((1, D), F32)],
        scratch_shapes=[pltpu.VMEM((rows, D), F32)],
    )(x, dh, gains, w_kv, w_mix, *grads)


def weight_rows(order, rows, lefts, rights, other=None):
    count = order.shape[0]
    tokens = lefts[0].shape[0]
    columns = sum(r.shape[1] for r in rights)
    flat = list(lefts) + list(rights) + ([] if other is None else [other])
    added = 0 if other is None else other.shape[0]
    outs = 1 if other is None else 2

    def kernel(order_ref, *refs):
        left_refs, right_refs = refs[: len(lefts)], refs[len(lefts) : len(lefts) + len(rights)]
        out_refs, (turned_ref, left_ref) = refs[len(flat) : len(flat) + outs], refs[-2:]
        at = 0
        for ref in left_refs:
            turned_ref[at : at + ref.shape[1]] = ref[...].T
            at += ref.shape[1]
        for n in range(count):
            start = pl.multiple_of(order_ref[n] * rows, rows)
            left_ref[n * rows : (n + 1) * rows] = turned_ref[pl.ds(start, rows)]
        at = 0
        for ref in right_refs:
            width = ref.shape[1]
            for begin in range(0, width, 512):
                end = min(begin + 512, width)
                cols = slice(at + begin, at + end)
                term = dot(left_ref[...], ref[:, begin:end], NN)
                if other is None:
                    out_refs[0][:, cols] = term.astype(BF)
                else:
                    other_ref = refs[len(flat) - 1]
                    near = term[:added] + other_ref[:, cols].astype(F32)
                    out_refs[0][:, cols] = near[:rows].astype(BF)
                    out_refs[1][: added - rows, cols] = near[rows:].astype(BF)
                    out_refs[1][added - rows :, cols] = term[added:].astype(BF)
            at += width

    shapes = [shaped((count * rows, columns))]
    if other is not None:
        shapes = [shaped((rows, columns)), shaped(((count - 1) * rows, columns))]
    size = 2 * (count * rows * columns + sum(v.size for v in flat))
    return call(
        kernel,
        "weight_rows",
        limit=max(8, 4 + int(1.25 * size) // (1024 * 1024)),
        flops=2 * count * rows * tokens * columns,
        moved=size,
        in_specs=[SMEM_SPEC] + [pl.BlockSpec(memory_space=pltpu.VMEM)] * len(flat),
        out_specs=[pl.BlockSpec(memory_space=pltpu.VMEM)] * outs,
        out_shape=shapes,
        scratch_shapes=[
            pltpu.VMEM((D, tokens), BF),
            pltpu.VMEM((count * rows, tokens), BF),
        ],
    )(order, *flat)


def ring_add(core, own, moving, first):
    rows = moving.shape[0] if first == 0 else moving.shape[0] // 2
    columns = own.shape[1]
    single = first == 0

    def kernel(core_ref, own_ref, moving_ref, out_ref):
        moved = moving_ref[...].astype(F32)
        if single:
            moved = jnp.where(core_ref[0] == pl.program_id(0), moved, 0.0)
        out_ref[...] = (own_ref[...].astype(F32) + moved).astype(BF)

    return call(
        kernel,
        "ring_add",
        limit=8,
        flops=4 * rows * columns,
        moved=12 * rows * columns,
        grid=(2,),
        in_specs=[
            SMEM_SPEC,
            pl.BlockSpec((rows, columns), lambda j: (first + j, 0)),
            pl.BlockSpec((rows, columns), (lambda j: (0, 0)) if single else (lambda j: (j, 0))),
        ],
        out_specs=pl.BlockSpec((rows, columns), lambda j: (j, 0)),
        out_shape=shaped((2 * rows, columns)),
    )(core, own, moving)


def blank(shape):
    def kernel(out_ref):
        pass

    return call(
        kernel,
        "blank",
        limit=1,
        out_specs=pl.BlockSpec(memory_space=pl.ANY),
        out_shape=shaped(shape),
    )()


class Plan:
    def __init__(self, boundary):
        self.micro = boundary.shape[1]
        self.tok_rows = boundary.shape[3]
        self.n_ctx = lax.axis_size("ctx")
        self.nw = lax.axis_size("wshard")
        self.g = self.n_ctx // (self.micro * self.nw)
        self.r = self.tok_rows // (self.g * self.nw)
        self.i = lax.axis_index("ctx")
        self.w = lax.axis_index("wshard")
        self.rows = self.n_ctx * self.r
        self.members = self.g * self.nw
        count = self.n_ctx
        chips = [2 * p if p < count // 2 else 2 * (count - 1 - p) + 1 for p in range(count)]
        self.half = count // 2
        self.way = 1 - 2 * self.w
        self.ring_pairs = []
        for p in range(count):
            self.ring_pairs.append((chips[p] * 2, chips[(p + 1) % count] * 2))
            self.ring_pairs.append((chips[p] * 2 + 1, chips[(p - 1) % count] * 2 + 1))
        place = jnp.where(self.i % 2 == 0, self.i // 2, count - 1 - self.i // 2)

        def chip(at):
            at = at % count
            return jnp.where(at < count // 2, 2 * at, 2 * (count - 1 - at) + 1)

        self.behind = [chip(place - self.way * k) for k in range(self.half + 1)]
        self.ahead = [chip(place + self.way * k) for k in range(self.half + 1)]
        self.wrows = D // (self.n_ctx * self.nw)
        near = range(self.half - 1, 0, -1)
        theirs = [2 * self.ahead[self.half] + 1 - self.w]
        mine = [2 * self.ahead[self.half] + self.w]
        for k in near:
            theirs += [2 * self.behind[k], 2 * self.behind[k] + 1]
            mine += [2 * self.ahead[k], 2 * self.ahead[k] + 1]
        mine += [2 * self.i, 2 * self.i + 1]
        self.theirs = jnp.stack(theirs).astype(jnp.int32)
        self.mine = jnp.stack(mine).astype(jnp.int32)
        self.core = self.w[None].astype(jnp.int32)

    def swap(self, array):
        return lax.ppermute(array, "wshard", [(0, 1), (1, 0)])

    def step(self, array):
        return lax.ppermute(array, BOTH, self.ring_pairs)

    def in_order(self, own, other):
        first = self.w == 0
        return jnp.concatenate(
            [jnp.where(first, own, other), jnp.where(first, other, own)], axis=0
        )

    def across(self, local):
        parts = local.reshape(self.micro, self.g, self.nw, self.r, D)
        parts = lax.all_to_all(parts.transpose(2, 0, 1, 3, 4), "wshard", 0, 0, tiled=True)
        return parts.transpose(1, 0, 2, 3, 4).reshape(self.n_ctx, self.r, D)

    def along(self, parts):
        return lax.all_to_all(parts, "ctx", 0, 0, tiled=True).reshape(self.rows, D)

    def from_sequences(self, rows):
        parts = lax.all_to_all(rows.reshape(self.n_ctx, self.r, D), "ctx", 0, 0, tiled=True)
        parts = parts.reshape(self.micro, self.nw, self.g, self.r, D).transpose(1, 0, 2, 3, 4)
        parts = lax.all_to_all(parts, "wshard", 0, 0, tiled=True)
        return parts.transpose(1, 2, 0, 3, 4).reshape(self.micro, self.tok_rows, D)

    def total(self, value):
        by = 1
        while by < self.n_ctx * self.nw:
            pairs = [(n, n ^ by) for n in range(self.n_ctx * self.nw)]
            value = value + lax.ppermute(value, BOTH, pairs)
            by *= 2
        return value

    def rotation(self, by):
        pairs = []
        for flat in range(self.n_ctx * self.nw):
            group, place = divmod(flat, self.members)
            pairs.append((flat, group * self.members + (place + by) % self.members))
        return pairs

    def gather_rows(self, rows):
        return [rows] + [
            lax.ppermute(rows, BOTH, self.rotation(by)) for by in range(1, self.members)
        ]

    def scatter_rows(self, terms):
        return [terms[0]] + [
            lax.ppermute(terms[by], BOTH, self.rotation(-by)) for by in range(1, self.members)
        ]


class Gather:
    def __init__(self, plan, shard, *deps):
        self.plan = plan
        self.rows = shard.shape[0]
        self.whole = blank((plan.n_ctx, plan.nw * self.rows, shard.shape[1]))
        self.current = plan.in_order(shard, plan.swap(shard))
        self.start = self.current
        self.put(self.current, plan.i)
        self.k = 0

    def put(self, block, chip):
        self.whole = lax.dynamic_update_index_in_dim(self.whole, block, chip, 0)

    def advance(self, *deps, late=()):
        plan = self.plan
        self.k += 1
        current = after(self.current, *deps) if deps else self.current
        if self.k < plan.half:
            current = plan.step(current)
            if late:
                current = after(current, *late)
            self.put(current, plan.behind[self.k])
            self.put(plan.swap(current), plan.ahead[self.k])
        else:
            part = lax.dynamic_slice_in_dim(current, plan.w * self.rows, self.rows, 0)
            current = plan.step(part)
            if late:
                current = after(current, *late)
            self.put(plan.in_order(current, plan.swap(current)), plan.behind[plan.half])
        self.current = current
        return current

    def result(self):
        return self.whole.reshape(D, self.whole.shape[2])


class Reduce:
    def __init__(self, plan, clock, lefts, rights):
        self.plan, self.clock = plan, clock
        self.lefts, self.rights = list(lefts), list(rights)
        self.k = plan.half

    def theirs(self):
        plan = self.plan
        lefts = [self.clock.tie(self.lefts[0])] + self.lefts[1:]
        (term,) = weight_rows(plan.theirs, plan.wrows, lefts, self.rights)
        self.other = plan.swap(self.clock.mark(term))

    def mine(self):
        plan = self.plan
        lefts = [self.clock.tie(self.lefts[0])] + self.lefts[1:]
        term, self.own = weight_rows(plan.mine, plan.wrows, lefts, self.rights, self.other)
        self.moving = plan.step(self.clock.mark(term))
        self.k -= 1

    def advance(self):
        plan = self.plan
        moving = self.clock.tie(self.moving)
        term = ring_add(plan.core, self.own, moving, 2 * (plan.half - 1 - self.k))
        self.moving = plan.step(self.clock.mark(term))
        self.k -= 1

    def result(self):
        plan = self.plan
        rows = plan.wrows
        final = self.moving.astype(F32) + self.own[-2 * rows :].astype(F32)
        keep = lax.dynamic_slice_in_dim(final, plan.w * rows, rows, 0)
        give = lax.dynamic_slice_in_dim(final, (1 - plan.w) * rows, rows, 0)
        return keep + plan.swap(give.astype(BF)).astype(F32)


class Clock:
    def __init__(self):
        self.last = None

    def tie(self, value):
        return value if self.last is None else after(value, self.last)

    def mark(self, value):
        self.last = value
        return value


def interleave(keys, values):
    lead = keys.shape[0]
    both = jnp.stack([keys.reshape(lead, PAIRS, LANES), values.reshape(lead, PAIRS, LANES)], axis=2)
    return both.reshape(lead, 2 * D)


def apart(both):
    lead = both.shape[0]
    both = both.reshape(lead, PAIRS, 2, LANES)
    return both[:, :, 0].reshape(lead, D), both[:, :, 1].reshape(lead, D)


def body(
    boundary, segment_ids, qkv_weight, attn_out_weight, ffn_in_weight, ffn_out_weight, norm_gains
):
    section = lax.axis_index("section")
    sections = lax.axis_size("section")
    plan = Plan(boundary)
    rows = plan.rows

    pad = FFP - FF
    wide_shard = jnp.concatenate(
        [
            interleave(qkv_weight[0][:, D : 2 * D], qkv_weight[0][:, 2 * D :]),
            qkv_weight[0][:, :D],
            attn_out_weight[0],
            jnp.pad(norm_gains[0].T, ((0, 0), (0, LANES - 2))),
        ],
        axis=1,
    )
    in_shard = jnp.pad(ffn_in_weight[0][:, :FF], ((0, 0), (0, pad)))
    gate_shard = jnp.pad(ffn_in_weight[0][:, FF:], ((0, 0), (0, pad)))
    back_shard = jnp.pad(ffn_out_weight[0].T, ((0, 0), (0, pad)))
    get_wide = Gather(plan, wide_shard)
    get_in = Gather(plan, in_shard)
    parts = plan.across(after(boundary[0, :, 0], get_wide.start, get_in.start))
    got = [get.advance() for get in (get_wide, get_in)]
    get_gate = Gather(plan, after(gate_shard, *got))
    get_back = Gather(plan, after(back_shard, *got))
    own = plan.along(after(parts, *got))
    got = [get.advance() for get in (get_wide, get_in)]
    ids = after(segment_ids[:, 0], *got)
    for _ in range(plan.half - 2):
        got = [get.advance() for get in (get_wide, get_in)]

    ids = plan.in_order(ids[None], plan.swap(ids[None])).transpose(1, 0, 2)
    ids = jnp.repeat(ids.reshape(plan.micro * plan.nw, plan.tok_rows), plan.g, axis=0)
    line = lax.all_to_all(ids, "ctx", 0, 0, tiled=True).reshape(-1)
    grid = line.reshape(plan.n_ctx, plan.members, plan.r)
    place = (plan.i % plan.g) * plan.nw + plan.w
    seg_pieces = [
        lax.dynamic_index_in_dim(grid, (place - by) % plan.members, 1, keepdims=False).reshape(rows)
        for by in range(plan.members)
    ]
    segq = seg_pieces[0]
    segk = jnp.concatenate(seg_pieces)
    token = (
        lax.broadcasted_iota(jnp.int32, (plan.n_ctx, plan.r), 0) * plan.tok_rows
        + place * plan.r
        + lax.broadcasted_iota(jnp.int32, (plan.n_ctx, plan.r), 1)
    ).reshape(rows)
    first = jnp.sum((line[None, :] < segq[:, None]).astype(jnp.int32), axis=1)
    position = (token - first).astype(F32)
    exponent = jnp.arange(HEAD_DIM // 2, dtype=F32) * (-2.0 / HEAD_DIM)
    angles = position[:, None] * (ROPE_BASE**exponent)[None, :]
    cosine, sine = jnp.cos(angles), jnp.sin(angles)
    cos_rows = jnp.concatenate([cosine] * 4, axis=1)
    sin_rows = jnp.concatenate([-sine, sine] * 2, axis=1)
    qmarks, kmarks = query_marks(segq), key_marks(segk)

    w_kv = w_mix = get_wide.result()
    w_in = get_in.result()
    gains = gains_of(w_mix)

    def first_half(x):
        a, kv = keys_values(x, gains, w_kv, cos_rows, sin_rows)
        kv_list = plan.gather_rows(kv)
        return a, kv_list, queries_of(a, w_mix, cos_rows, sin_rows)

    got = get_gate.advance(*got), get_back.advance(*got)
    _, kv_list, q = first_half(own)
    half = PAIRS // 2
    o_first, _ = attend(after(q, *got), kv_list, qmarks, kmarks, 0, half)
    got = get_gate.advance(late=(o_first,)), get_back.advance(late=(o_first,))
    o_last, _ = attend(after(q, *got), kv_list, qmarks, kmarks, half, half)
    while get_gate.k < plan.half:
        got = get_gate.advance(late=(o_last,)), get_back.advance(late=(o_last,))
    h, b = project(own, [o_first, o_last], gains, w_mix)
    w_gate, w_back = get_gate.result(), get_back.result()
    (z,) = ffn_in(b, w_in, w_gate, False)
    first_out = ffn_out(h, z, w_back)

    def forward(x):
        a, kv_list, q = first_half(x)
        o, lse = attend(q, kv_list, qmarks, kmarks, 0, PAIRS)
        h, b = project(x, [o], gains, w_mix)
        z, act, slope = ffn_in(b, w_in, w_gate, True)
        return ffn_out(h, z, w_back), (x, a, q, kv_list, o, lse, h, b, z, act, slope)

    def backward(stash, grad):
        x, a, q, kv_list, o, lse, h, b, z, act, slope = stash
        da, dg = ffn_back(grad, act, slope, w_back)
        dh, dh_low, _ = hidden_back(grad, da, dg, h, gains, w_in, w_gate)
        dq, terms = attend_back(
            q, kv_list, dh_low, o, lse, qmarks, kmarks, w_mix, cos_rows, sin_rows, 0
        )
        dkv = keys_back(plan.scatter_rows(terms), cos_rows, sin_rows)
        return input_back(x, dh, [dq], [dkv], gains, w_kv, w_mix)[0]

    def last_backward(stash, grad):
        x, a, q, kv_list, o, lse, h, b, z, act, slope = stash
        clock = Clock()
        back = Reduce(plan, clock, [grad], [z])
        da, dg = ffn_back(clock.tie(grad), act, slope, w_back)
        clock.mark(da)
        grow = Reduce(plan, clock, [b], [da, dg])
        grow.theirs()
        back.theirs()
        grow.mine()
        back.mine()
        dh, dh_low, gain_second = hidden_back(clock.tie(grad), da, dg, h, gains, w_in, w_gate)
        clock.mark(dh)
        grow.advance()
        back.advance()
        out = Reduce(plan, clock, [o], [dh_low])
        out.theirs()
        parts = []
        count = PAIRS // 4
        for n in range(4):
            cut = slice(n * count * LANES, (n + 1) * count * LANES)
            dq, terms = attend_back(
                clock.tie(q),
                kv_list,
                dh_low,
                o[:, cut],
                lse[n * count : (n + 1) * count],
                qmarks,
                kmarks,
                w_mix,
                cos_rows,
                sin_rows,
                n * count,
            )
            clock.mark(dq)
            parts.append((dq, plan.scatter_rows(terms)))
            if n == 0:
                out.mine()
            elif n == 1:
                for one in (grow, back, out):
                    one.advance()
        dkv_list = [keys_back(terms, cos_rows, sin_rows) for _, terms in parts]
        dq_list = [dq for dq, _ in parts]
        mixed = Reduce(plan, clock, [a], dkv_list + dq_list)
        mixed.theirs()
        for one in (grow, back, out):
            one.advance()
        dx, gain_first = input_back(clock.tie(x), dh, dq_list, dkv_list, gains, w_kv, w_mix)
        clock.mark(dx)
        mixed.mine()
        while mixed.k:
            for one in (grow, back, out, mixed):
                if one.k:
                    one.advance()
        gain = plan.total(jnp.concatenate([gain_first, gain_second], axis=0))
        start = (plan.i * plan.nw + plan.w) * plan.wrows
        gain = lax.dynamic_slice_in_dim(gain, start, plan.wrows, 1)
        return dx, [back.result(), grow.result(), out.result(), mixed.result(), gain]

    def handed(array, by):
        pairs = [(s, s + by) for s in range(sections) if 0 <= s + by < sections]
        return lax.ppermute(array, "section", pairs)

    x_in = jnp.where(section == 0, own, handed(first_out, 1))
    out, stash = forward(x_in)
    first_dx = backward(stash, own)
    grad_in = jnp.where(section == sections - 1, own, after(handed(first_dx, -1), out))
    dx, (g_back, g_in, g_attn, g_mix, g_gain) = last_backward(stash, grad_in)
    boundary_local = plan.from_sequences(jnp.where(section == 0, dx, out))
    g_key, g_value = apart(g_mix[:, : 2 * D])
    return (
        boundary_local[None, :, None],
        jnp.concatenate([g_mix[:, 2 * D :], g_key, g_value], axis=1)[None],
        g_attn[None],
        jnp.concatenate([g_in[:, :FF], g_in[:, FFP : FFP + FF]], axis=1)[None],
        g_back[:, :FF].T[None],
        g_gain[None],
    )


def solution(mesh):
    placed = (
        P("section", None, "wshard", "ctx", None),
        P(None, "wshard", "ctx"),
        P("section", ("ctx", "wshard"), None),
        P("section", ("ctx", "wshard"), None),
        P("section", ("ctx", "wshard"), None),
        P("section", None, ("ctx", "wshard")),
        P("section", None, ("ctx", "wshard")),
    )
    return jax.shard_map(
        body,
        mesh=mesh,
        in_specs=placed,
        out_specs=(placed[0],) + placed[2:],
        check_vma=False,
    )
```

```python
from functools import partial

import jax
import jax.numpy as jnp
from jax import lax
from jax.experimental import pallas as pl
from jax.experimental.pallas import tpu as pltpu
from jax.sharding import PartitionSpec as P

D = 1024
HEADS = 16
HEAD_DIM = 64
FF = 2624
FFP = 2688
FFB = 896
LANES = 128
PAIRS = D // LANES
EPSILON = 1e-05
ROPE_BASE = 160000.0
NEG_FILL = -1e30
BF = jnp.bfloat16
F32 = jnp.float32
BOTH = ("ctx", "wshard")
IDS = 16
PENALTY = -(2.0**100)
NN = ((1,), (0,))
NT = ((1,), (1,))
TN = ((0,), (0,))
SMEM_SPEC = pl.BlockSpec(memory_space=pltpu.SMEM)


def dot(a, b, dims):
    return lax.dot_general(a, b, (dims, ((), ())), preferred_element_type=F32)


def after(value, *others):
    return lax.optimization_barrier((value,) + others)[0]


def shaped(shape, kind=BF):
    return jax.ShapeDtypeStruct(shape, kind)


def call(kernel, name, limit=20, flops=0, moved=0, exps=0, **more):
    return pl.pallas_call(
        kernel,
        name=name,
        compiler_params=pltpu.CompilerParams(vmem_limit_bytes=limit * 1024 * 1024),
        cost_estimate=pl.CostEstimate(
            flops=int(flops), bytes_accessed=int(moved), transcendentals=int(exps)
        ),
        **more,
    )


def whole(shape):
    return pl.BlockSpec(shape, lambda *_: (0,) * len(shape))


def rope_block(v, cosine, sine):
    lane = lax.broadcasted_iota(jnp.int32, v.shape, 1) % HEAD_DIM
    other = jnp.where(
        lane < HEAD_DIM // 2,
        pltpu.roll(v, LANES - HEAD_DIM // 2, 1),
        pltpu.roll(v, HEAD_DIM // 2, 1),
    )
    return v * cosine + other * sine


def norm_parts(values):
    center = values - jnp.mean(values, axis=-1, keepdims=True)
    spread = jnp.mean(center * center, axis=-1, keepdims=True)
    inverse = lax.rsqrt(spread + EPSILON)
    return center * inverse, inverse


def norm_back(values, gain_row, grad):
    hat, inverse = norm_parts(values)
    scaled = grad * gain_row
    back = inverse * (
        scaled
        - jnp.mean(scaled, axis=-1, keepdims=True)
        - hat * jnp.mean(scaled * hat, axis=-1, keepdims=True)
    )
    return back, jnp.sum(grad * hat, axis=0, keepdims=True)


def head_mask(shape, head):
    lane = lax.broadcasted_iota(jnp.int32, shape, 1)
    return (lane >= HEAD_DIM) if head else (lane < HEAD_DIM)


def pick(mask, v, other=0.0):
    return jnp.where(mask, v, jnp.full(v.shape, other, v.dtype))


def gains_of(w_mix):
    def kernel(w_ref, out_ref):
        out_ref[...] = w_ref[...].astype(F32).T[:8]

    return call(
        kernel,
        "gains",
        grid=(1,),
        in_specs=[pl.BlockSpec((D, LANES), lambda j: (0, 4 * D // LANES))],
        out_specs=whole((8, D)),
        out_shape=shaped((8, D), F32),
    )(w_mix)


def keys_values(x, gains, w_kv, cosine, sine):
    rows = x.shape[0]
    block = 512

    def kernel(x_ref, gain_ref, w_ref, cos_ref, sin_ref, a_ref, out_ref):
        @pl.when(pl.program_id(0) == 0)
        def _():
            hat, _ = norm_parts(x_ref[...].astype(F32))
            a_ref[...] = (hat * gain_ref[0:1]).astype(BF)

        m = dot(a_ref[...], w_ref[...], NN)
        for j in range(block // LANES):
            at = slice(j * LANES, (j + 1) * LANES)
            v = m[:, at]
            if j % 2 == 0:
                v = rope_block(v, cos_ref[...], sin_ref[...])
            out_ref[:, at] = v.astype(BF)

    return call(
        kernel,
        "keys_values",
        flops=2 * rows * D * 2 * D,
        moved=2 * (2 * D * D + 4 * rows * D),
        grid=(2 * D // block,),
        in_specs=[
            whole((rows, D)),
            whole((8, D)),
            pl.BlockSpec((D, block), lambda j: (0, j)),
            whole((rows, LANES)),
            whole((rows, LANES)),
        ],
        out_specs=[whole((rows, D)), pl.BlockSpec((rows, block), lambda j: (0, j))],
        out_shape=[shaped((rows, D)), shaped((rows, 2 * D))],
    )(x, gains, w_kv, cosine, sine)


def queries_of(a, w_mix, cosine, sine):
    rows = a.shape[0]
    block = 512

    def kernel(a_ref, w_ref, cos_ref, sin_ref, out_ref):
        m = dot(a_ref[...], w_ref[...], NN)
        for j in range(block // LANES):
            at = slice(j * LANES, (j + 1) * LANES)
            out_ref[:, at] = rope_block(m[:, at], cos_ref[...], sin_ref[...]).astype(BF)

    return call(
        kernel,
        "queries",
        flops=2 * rows * D * D,
        moved=2 * (D * D + 2 * rows * D),
        grid=(D // block,),
        in_specs=[
            whole((rows, D)),
            pl.BlockSpec((D, block), lambda j: (0, 2 * D // block + j)),
            whole((rows, LANES)),
            whole((rows, LANES)),
        ],
        out_specs=pl.BlockSpec((rows, block), lambda j: (0, j)),
        out_shape=shaped((rows, D)),
    )(a, w_mix, cosine, sine)


def key_marks(seg):
    lane = jnp.arange(LANES) % HEAD_DIM
    return jnp.where(lane < IDS, (seg[:, None] == lane), lane < IDS + 3).astype(BF)
def query_marks(seg):
    lane = jnp.arange(LANES) % HEAD_DIM
    return jnp.where((lane < IDS) & (seg[:, None] != lane), PENALTY, 0.0).astype(BF)

def split3(v):
    a = v.astype(BF).astype(F32)
    b = (v - a).astype(BF).astype(F32)
    return a, b, v - a - b


def attend(q, kv_list, qmarks, kmarks, begin, count):
    rows = q.shape[0]
    members = len(kv_list)
    keys = members * rows

    def kernel(q_ref, qm_ref, km_ref, *refs):
        kv_refs, (o_ref, lse_ref) = refs[:members], refs[members:]
        k = jnp.concatenate([r[:, :LANES] for r in kv_refs], axis=0)
        v = jnp.concatenate([r[:, LANES:] for r in kv_refs], axis=0)
        q = q_ref[...] * jnp.asarray(HEAD_DIM**-0.5, BF)
        parts, stats = [], []
        for head in range(2):
            mine = head_mask((rows, LANES), head)
            theirs = head_mask((keys, LANES), head)
            s = dot(jnp.where(theirs, k, km_ref[...]), jnp.where(mine, q, qm_ref[...]), NT)
            top = jnp.max(s, axis=0, keepdims=True)
            e = jnp.exp(s - top).astype(BF)
            u = dot(pick(theirs, v, 1.0), e, TN)
            low, high = u[:HEAD_DIM], u[HEAD_DIM:]
            value, total = (high, low) if head else (low, high)
            parts.append(value / total)
            stats.append(top + jnp.log(total[:1]))
        o_ref[...] = jnp.concatenate(parts, axis=0).T.astype(BF)
        lse_ref[0] = jnp.concatenate(stats, axis=0)

    return call(
        kernel,
        "attend",
        flops=8 * rows * keys * count * LANES,
        moved=2 * (2 * rows + 2 * keys) * count * LANES,
        exps=rows * keys * count * 2,
        grid=(count,),
        in_specs=[
            pl.BlockSpec((rows, LANES), lambda p: (0, begin + p)),
            whole((rows, LANES)),
            whole((keys, LANES)),
        ]
        + [pl.BlockSpec((rows, 2 * LANES), lambda p: (0, begin + p))] * members,
        out_specs=[
            pl.BlockSpec((rows, LANES), lambda p: (0, p)),
            pl.BlockSpec((1, 2, rows), lambda p: (p, 0, 0)),
        ],
        out_shape=[shaped((rows, count * LANES)), shaped((count, 2, rows), F32)],
    )(q, qmarks, kmarks, *kv_list)

def project(x, o_list, gains, w_mix):
    rows = x.shape[0]
    block = 512
    steps = D // block

    def kernel(x_ref, gain_ref, w_ref, *refs):
        o_refs, (h_ref, b_ref) = refs[:-2], refs[-2:]
        j = pl.program_id(0)
        at = pl.ds(pl.multiple_of(j * block, block), block)
        total = x_ref[:, at].astype(F32)
        begin = 0
        for o_ref in o_refs:
            end = begin + o_ref.shape[1]
            total += dot(o_ref[...], w_ref[begin:end], NN)
            begin = end
        h_ref[:, at] = total

        @pl.when(j == steps - 1)
        def _():
            hat, _ = norm_parts(h_ref[...])
            b_ref[...] = (hat * gain_ref[1:2]).astype(BF)

    return call(
        kernel,
        "project",
        flops=2 * rows * D * D,
        moved=2 * D * D + 10 * rows * D,
        grid=(steps,),
        in_specs=[
            whole((rows, D)),
            whole((8, D)),
            pl.BlockSpec((D, block), lambda j: (0, 3 * D // block + j)),
        ]
        + [whole(o.shape) for o in o_list],
        out_specs=[whole((rows, D)), whole((rows, D))],
        out_shape=[shaped((rows, D), F32), shaped((rows, D))],
    )(x, gains, w_mix, *o_list)


def ffn_in(b, w_in, w_gate, keep):
    rows = b.shape[0]
    steps = FFP // FFB

    def kernel(b_ref, wa_ref, wg_ref, z_ref, *kept):
        a = dot(b_ref[...], wa_ref[...], NN)
        g = dot(b_ref[...], wg_ref[...], NN)
        phi = 0.5 * (1.0 + lax.erf(a * 0.7071067811865476))
        act = a * phi
        z_ref[...] = (act * g).astype(BF)
        if keep:
            density = 0.3989422804014327 * jnp.exp(-0.5 * a * a)
            kept[0][...] = act.astype(BF)
            kept[1][...] = ((phi + a * density) * g).astype(BF)

    out_spec = pl.BlockSpec((rows, FFB), lambda j: (0, j))
    count = 3 if keep else 1
    return call(
        kernel,
        "ffn_in",
        flops=4 * rows * D * FFP,
        moved=2 * (2 * D * FFP + rows * D + count * rows * FFP),
        grid=(steps,),
        in_specs=[whole((rows, D))] + [pl.BlockSpec((D, FFB), lambda j: (0, j))] * 2,
        out_specs=[out_spec] * count,
        out_shape=[shaped((rows, FFP))] * count,
    )(b, w_in, w_gate)


def ffn_out(h, z, w_back):
    rows = h.shape[0]
    block = 256

    def kernel(h_ref, z_ref, w_ref, out_ref):
        out_ref[...] = (h_ref[...] + dot(z_ref[...], w_ref[...], NT)).astype(BF)

    return call(
        kernel,
        "ffn_out",
        flops=2 * rows * D * FFP,
        moved=2 * (D * FFP + rows * FFP + 3 * rows * D),
        grid=(D // block,),
        in_specs=[
            pl.BlockSpec((rows, block), lambda j: (0, j)),
            whole((rows, FFP)),
            pl.BlockSpec((block, FFP), lambda j: (j, 0)),
        ],
        out_specs=pl.BlockSpec((rows, block), lambda j: (0, j)),
        out_shape=shaped((rows, D)),
    )(h, z, w_back)


def ffn_back(grad, act, slope, w_back):
    rows = grad.shape[0]

    def kernel(g_ref, act_ref, slope_ref, w_ref, da_ref, dg_ref):
        dz = dot(g_ref[...], w_ref[...], NN)
        da_ref[...] = (dz * slope_ref[...].astype(F32)).astype(BF)
        dg_ref[...] = (dz * act_ref[...].astype(F32)).astype(BF)

    spec = pl.BlockSpec((rows, FFB), lambda j: (0, j))
    return call(
        kernel,
        "ffn_back",
        flops=2 * rows * D * FFP,
        moved=2 * (D * FFP + 4 * rows * FFP + rows * D),
        grid=(FFP // FFB,),
        in_specs=[whole((rows, D)), spec, spec, pl.BlockSpec((D, FFB), lambda j: (0, j))],
        out_specs=[spec, spec],
        out_shape=[shaped((rows, FFP))] * 2,
    )(grad, act, slope, w_back)


def hidden_back(grad, da, dg, h, gains, w_in, w_gate):
    rows = grad.shape[0]
    block = 256
    steps = D // block

    def kernel(g_ref, da_ref, dg_ref, h_ref, gain_ref, wa_ref, wg_ref, dh_ref, low_ref, sum_ref):
        j = pl.program_id(0)
        at = pl.ds(pl.multiple_of(j * block, block), block)
        dh_ref[:, at] = dot(da_ref[...], wa_ref[...], NT) + dot(dg_ref[...], wg_ref[...], NT)

        @pl.when(j == steps - 1)
        def _():
            back, total = norm_back(h_ref[...], gain_ref[1:2], dh_ref[...])
            dh = g_ref[...].astype(F32) + back
            dh_ref[...] = dh
            low_ref[...] = dh.astype(BF)
            sum_ref[...] = total

    return call(
        kernel,
        "hidden_back",
        flops=4 * rows * D * FFP,
        moved=2 * (2 * D * FFP + 2 * rows * FFP + 6 * rows * D),
        grid=(steps,),
        in_specs=[
            whole((rows, D)),
            whole((rows, FFP)),
            whole((rows, FFP)),
            whole((rows, D)),
            whole((8, D)),
        ]
        + [pl.BlockSpec((block, FFP), lambda j: (j, 0))] * 2,
        out_specs=[whole((rows, D)), whole((rows, D)), whole((1, D))],
        out_shape=[shaped((rows, D), F32), shaped((rows, D)), shaped((1, D), F32)],
    )(grad, da, dg, h, gains, w_in, w_gate)


def attend_back(q, kv_list, dh_low, o, lse, qmarks, kmarks, w_mix, cosine, sine, begin):
    count = o.shape[1] // LANES
    rows = q.shape[0]
    members = len(kv_list)
    keys = members * rows

    def kernel(q_ref, dh_ref, w_ref, o_ref, lse_ref, qm_ref, km_ref, cos_ref, sin_ref, *refs):
        kv_refs, (dq_ref, *dkv_refs) = refs[:members], refs[members:]
        k = jnp.concatenate([r[:, :LANES] for r in kv_refs], axis=0)
        v = jnp.concatenate([r[:, LANES:] for r in kv_refs], axis=0)
        do = dot(dh_ref[...], w_ref[...], NT).astype(BF)
        q = q_ref[...] * jnp.asarray(HEAD_DIM**-0.5, BF)
        prod = do.astype(F32) * o_ref[...].astype(F32)
        lse = lse_ref[0]
        row = lax.broadcasted_iota(jnp.int32, (LANES, rows), 0)
        beside = jnp.zeros((LANES, rows), F32)
        for head in range(2):
            for n, part in enumerate(split3(-lse[head : head + 1])):
                beside = jnp.where(row == IDS + n + (HEAD_DIM if head == 0 else 0), part, beside)
        beside = beside.T.astype(BF) + qm_ref[...]
        lane = lax.broadcasted_iota(jnp.int32, (rows, LANES), 1)
        dks, dvs, dqs = [], [], []
        for head in range(2):
            mine = head_mask((rows, LANES), head)
            theirs = head_mask((keys, LANES), head)
            delta = jnp.sum(jnp.where(mine, prod, 0.0), axis=1, keepdims=True)
            there = jnp.zeros((rows, LANES), F32)
            for n, part in enumerate(split3(-delta)):
                there = jnp.where(lane == IDS + n + (HEAD_DIM if head == 0 else 0), part, there)
            qh = jnp.where(mine, q, beside)
            doh = jnp.where(mine, do, there.astype(BF))
            kh = jnp.where(theirs, k, km_ref[...])
            vh = jnp.where(theirs, v, km_ref[...])
            p = jnp.exp(dot(kh, qh, NT))
            ds = (p * dot(vh, doh, NT)).astype(BF)
            dvs.append(dot(p.astype(BF), do, NN))
            dks.append(dot(ds, q, NN))
            dqs.append(dot(ds, k, TN))
        first = head_mask((rows, LANES), 0)
        dq = jnp.where(first, dqs[0], dqs[1])
        dq = rope_block(dq * HEAD_DIM**-0.5, cos_ref[...], -sin_ref[...])
        dq_ref[...] = dq.astype(BF)
        for m, out in enumerate(dkv_refs):
            cut = slice(m * rows, (m + 1) * rows)
            out[:, :LANES] = jnp.where(first, dks[0][cut], dks[1][cut]).astype(BF)
            out[:, LANES:] = jnp.where(first, dvs[0][cut], dvs[1][cut]).astype(BF)

    spec = pl.BlockSpec((rows, LANES), lambda p: (0, p))
    kv_spec = pl.BlockSpec((rows, 2 * LANES), lambda p: (0, p))
    results = call(
        kernel,
        "attend_back",
        flops=20 * rows * keys * count * LANES,
        moved=2 * (6 * rows + 4 * keys) * count * LANES,
        exps=rows * keys * 2 * count,
        grid=(count,),
        in_specs=[
            pl.BlockSpec((rows, LANES), lambda p: (0, begin + p)),
            whole((rows, D)),
            pl.BlockSpec((LANES, D), lambda p: (begin + p, 3)),
            spec,
            pl.BlockSpec((1, 2, rows), lambda p: (p, 0, 0)),
            whole((rows, LANES)),
            whole((keys, LANES)),
            whole((rows, LANES)),
            whole((rows, LANES)),
        ]
        + [pl.BlockSpec((rows, 2 * LANES), lambda p: (0, begin + p))] * members,
        out_specs=[spec] + [kv_spec] * members,
        out_shape=[shaped((rows, count * LANES))] + [shaped((rows, 2 * count * LANES))] * members,
    )(q, dh_low, w_mix, o, lse, qmarks, kmarks, cosine, sine, *kv_list)
    return results[0], results[1:]


def keys_back(terms, cosine, sine):
    rows, columns = terms[0].shape

    def kernel(cos_ref, sin_ref, *refs):
        for b in range(columns // LANES):
            at = slice(b * LANES, (b + 1) * LANES)
            v = refs[0][:, at].astype(F32)
            for r in refs[1:-1]:
                v += r[:, at].astype(F32)
            if b % 2 == 0:
                v = rope_block(v, cos_ref[...], -sin_ref[...])
            refs[-1][:, at] = v.astype(BF)

    return call(
        kernel,
        "keys_back",
        flops=10 * rows * columns,
        moved=2 * (len(terms) + 1) * rows * columns,
        grid=(1,),
        in_specs=[whole((rows, LANES))] * 2 + [whole((rows, columns))] * len(terms),
        out_specs=whole((rows, columns)),
        out_shape=shaped((rows, columns)),
    )(cosine, sine, *terms)


def input_back(x, dh, dq_list, dkv_list, gains, w_kv, w_mix):
    rows = x.shape[0]
    block = 256
    steps = D // block
    grads = list(dkv_list) + list(dq_list)

    def kernel(x_ref, dh_ref, gain_ref, wkv_ref, wq_ref, *refs):
        grad_refs, (dx_ref, sum_ref, da_ref) = refs[:-3], refs[-3:]
        j = pl.program_id(0)
        total = 0.0
        begin = 0
        for n, ref in enumerate(grad_refs):
            if n == len(dkv_list):
                begin = 0
            end = begin + ref.shape[1]
            w_ref = wkv_ref if n < len(dkv_list) else wq_ref
            total += dot(ref[...], w_ref[:, begin:end], NT)
            begin = end
        da_ref[:, pl.ds(pl.multiple_of(j * block, block), block)] = total

        @pl.when(j == steps - 1)
        def _():
            back, total = norm_back(x_ref[...].astype(F32), gain_ref[0:1], da_ref[...])
            dx_ref[...] = (dh_ref[...] + back).astype(BF)
            sum_ref[...] = total

    return call(
        kernel,
        "input_back",
        flops=6 * rows * D * D,
        moved=2 * (3 * D * D + 10 * rows * D),
        grid=(steps,),
        in_specs=[
            whole((rows, D)),
            whole((rows, D)),
            whole((8, D)),
            pl.BlockSpec((block, 2 * D), lambda j: (j, 0)),
            pl.BlockSpec((block, D), lambda j: (j, 2)),
        ]
        + [whole(g.shape) for g in grads],
        out_specs=[whole((rows, D)), whole((1, D))],
        out_shape=[shaped((rows, D)), shaped((1, D), F32)],
        scratch_shapes=[pltpu.VMEM((rows, D), F32)],
    )(x, dh, gains, w_kv, w_mix, *grads)


def weight_rows(order, rows, pairs, others=None):
    count = order.shape[0]
    tokens = pairs[0][0][0].shape[0]
    widths = [sum(r.shape[1] for r in rights) for _, rights in pairs]
    columns = sum(widths)
    flat = [v for lefts, rights in pairs for v in list(lefts) + list(rights)]
    flat += [] if others is None else list(others)
    added = 0 if others is None else others[0].shape[0]
    outs = 1 if others is None else 2

    def kernel(order_ref, *refs):
        out_refs, (turned_ref, left_ref) = refs[len(flat) : len(flat) + outs], refs[-2:]
        other_refs = [] if others is None else refs[len(flat) - len(others) : len(flat)]
        spans, at = [], 0
        for ref in other_refs:
            spans.append((at, at + ref.shape[1], ref))
            at += ref.shape[1]
        at = where = 0
        for lefts, rights in pairs:
            row = 0
            for _ in lefts:
                ref = refs[where]
                turned_ref[row : row + ref.shape[1]] = ref[...].T
                row += ref.shape[1]
                where += 1
            for n in range(count):
                start = pl.multiple_of(order_ref[n] * rows, rows)
                left_ref[n * rows : (n + 1) * rows] = turned_ref[pl.ds(start, rows)]
            for _ in rights:
                ref = refs[where]
                width = ref.shape[1]
                for begin in range(0, width, 512):
                    end = min(begin + 512, width)
                    cols = slice(at + begin, at + end)
                    term = dot(left_ref[...], ref[:, begin:end], NN)
                    if others is None:
                        out_refs[0][:, cols] = term.astype(BF)
                        continue
                    low, other_ref = next((a, r) for a, b, r in spans if a <= cols.start < b)
                    there = slice(cols.start - low, cols.stop - low)
                    near = term[:added] + other_ref[:, there].astype(F32)
                    out_refs[0][:, cols] = near[:rows].astype(BF)
                    out_refs[1][: added - rows, cols] = near[rows:].astype(BF)
                    out_refs[1][added - rows :, cols] = term[added:].astype(BF)
                at += width
                where += 1

    shapes = [shaped((count * rows, columns))]
    if others is not None:
        shapes = [shaped((rows, columns)), shaped(((count - 1) * rows, columns))]
    size = 2 * (count * rows * columns + sum(v.size for v in flat))
    return call(
        kernel,
        "weight_rows",
        limit=max(8, 4 + int(1.25 * size) // (1024 * 1024)),
        flops=2 * count * rows * tokens * columns,
        moved=size,
        in_specs=[SMEM_SPEC] + [pl.BlockSpec(memory_space=pltpu.VMEM)] * len(flat),
        out_specs=[pl.BlockSpec(memory_space=pltpu.VMEM)] * outs,
        out_shape=shapes,
        scratch_shapes=[
            pltpu.VMEM((D, tokens), BF),
            pltpu.VMEM((count * rows, tokens), BF),
        ],
    )(order, *flat)


def ring_add(core, own, moving, first):
    rows = moving.shape[0] if first == 0 else moving.shape[0] // 2
    columns = own.shape[1]
    single = first == 0

    def kernel(core_ref, own_ref, moving_ref, out_ref):
        moved = moving_ref[...].astype(F32)
        if single:
            moved = jnp.where(core_ref[0] == pl.program_id(0), moved, 0.0)
        out_ref[...] = (own_ref[...].astype(F32) + moved).astype(BF)

    return call(
        kernel,
        "ring_add",
        limit=8,
        flops=4 * rows * columns,
        moved=12 * rows * columns,
        grid=(2,),
        in_specs=[
            SMEM_SPEC,
            pl.BlockSpec((rows, columns), lambda j: (first + j, 0)),
            pl.BlockSpec((rows, columns), (lambda j: (0, 0)) if single else (lambda j: (j, 0))),
        ],
        out_specs=pl.BlockSpec((rows, columns), lambda j: (j, 0)),
        out_shape=shaped((2 * rows, columns)),
    )(core, own, moving)


def blank(shape):
    def kernel(out_ref):
        pass

    return call(
        kernel,
        "blank",
        limit=1,
        out_specs=pl.BlockSpec(memory_space=pl.ANY),
        out_shape=shaped(shape),
    )()


class Plan:
    def __init__(self, boundary):
        self.micro = boundary.shape[1]
        self.tok_rows = boundary.shape[3]
        self.n_ctx = lax.axis_size("ctx")
        self.nw = lax.axis_size("wshard")
        self.g = self.n_ctx // (self.micro * self.nw)
        self.r = self.tok_rows // (self.g * self.nw)
        self.i = lax.axis_index("ctx")
        self.w = lax.axis_index("wshard")
        self.rows = self.n_ctx * self.r
        self.members = self.g * self.nw
        count = self.n_ctx
        chips = [2 * p if p < count // 2 else 2 * (count - 1 - p) + 1 for p in range(count)]
        self.half = count // 2
        self.way = 1 - 2 * self.w
        self.ring_pairs = []
        for p in range(count):
            self.ring_pairs.append((chips[p] * 2, chips[(p + 1) % count] * 2))
            self.ring_pairs.append((chips[p] * 2 + 1, chips[(p - 1) % count] * 2 + 1))
        place = jnp.where(self.i % 2 == 0, self.i // 2, count - 1 - self.i // 2)

        def chip(at):
            at = at % count
            return jnp.where(at < count // 2, 2 * at, 2 * (count - 1 - at) + 1)

        self.behind = [chip(place - self.way * k) for k in range(self.half + 1)]
        self.ahead = [chip(place + self.way * k) for k in range(self.half + 1)]
        self.wrows = D // (self.n_ctx * self.nw)
        near = range(self.half - 1, 0, -1)
        theirs = [2 * self.ahead[self.half] + 1 - self.w]
        mine = [2 * self.ahead[self.half] + self.w]
        for k in near:
            theirs += [2 * self.behind[k], 2 * self.behind[k] + 1]
            mine += [2 * self.ahead[k], 2 * self.ahead[k] + 1]
        mine += [2 * self.i, 2 * self.i + 1]
        self.theirs = jnp.stack(theirs).astype(jnp.int32)
        self.mine = jnp.stack(mine).astype(jnp.int32)
        self.core = self.w[None].astype(jnp.int32)

    def swap(self, array):
        return lax.ppermute(array, "wshard", [(0, 1), (1, 0)])

    def step(self, array):
        return lax.ppermute(array, BOTH, self.ring_pairs)

    def in_order(self, own, other):
        first = self.w == 0
        return jnp.concatenate(
            [jnp.where(first, own, other), jnp.where(first, other, own)], axis=0
        )

    def across(self, local):
        parts = local.reshape(self.micro, self.g, self.nw, self.r, D)
        parts = lax.all_to_all(parts.transpose(2, 0, 1, 3, 4), "wshard", 0, 0, tiled=True)
        return parts.transpose(1, 0, 2, 3, 4).reshape(self.n_ctx, self.r, D)

    def along(self, parts):
        return lax.all_to_all(parts, "ctx", 0, 0, tiled=True).reshape(self.rows, D)

    def back_along(self, rows):
        return lax.all_to_all(rows.reshape(self.n_ctx, self.r, D), "ctx", 0, 0, tiled=True)

    def back_across(self, parts):
        parts = parts.reshape(self.micro, self.nw, self.g, self.r, D).transpose(1, 0, 2, 3, 4)
        parts = lax.all_to_all(parts, "wshard", 0, 0, tiled=True)
        return parts.transpose(1, 2, 0, 3, 4).reshape(self.micro, self.tok_rows, D)

    def total(self, value):
        by = 1
        while by < self.n_ctx * self.nw:
            pairs = [(n, n ^ by) for n in range(self.n_ctx * self.nw)]
            value = value + lax.ppermute(value, BOTH, pairs)
            by *= 2
        return value

    def rotation(self, by):
        pairs = []
        for flat in range(self.n_ctx * self.nw):
            group, place = divmod(flat, self.members)
            pairs.append((flat, group * self.members + (place + by) % self.members))
        return pairs

    def gather_rows(self, rows):
        return [rows] + [
            lax.ppermute(rows, BOTH, self.rotation(by)) for by in range(1, self.members)
        ]

    def scatter_rows(self, terms):
        return [terms[0]] + [
            lax.ppermute(terms[by], BOTH, self.rotation(-by)) for by in range(1, self.members)
        ]


class Gather:
    def __init__(self, plan, shard, *deps):
        self.plan = plan
        self.rows = shard.shape[0]
        self.whole = blank((plan.n_ctx, plan.nw * self.rows, shard.shape[1]))
        self.current = plan.in_order(shard, plan.swap(shard))
        self.start = self.current
        self.put(self.current, plan.i)
        self.k = 0

    def put(self, block, chip):
        self.whole = lax.dynamic_update_index_in_dim(self.whole, block, chip, 0)

    def advance(self, *deps, late=()):
        plan = self.plan
        self.k += 1
        current = after(self.current, *deps) if deps else self.current
        if self.k < plan.half:
            current = plan.step(current)
            if late:
                current = after(current, *late)
            self.put(current, plan.behind[self.k])
            self.put(plan.swap(current), plan.ahead[self.k])
        else:
            part = lax.dynamic_slice_in_dim(current, plan.w * self.rows, self.rows, 0)
            current = plan.step(part)
            if late:
                current = after(current, *late)
            self.put(plan.in_order(current, plan.swap(current)), plan.behind[plan.half])
        self.current = current
        return current

    def result(self):
        return self.whole.reshape(D, self.whole.shape[2])


class Reduce:
    def __init__(self, plan, clock):
        self.plan, self.clock = plan, clock
        self.pairs, self.others = [], []
        self.k = plan.half

    def theirs(self, *pairs):
        plan = self.plan
        lefts, rights = pairs[0]
        tied = [([self.clock.tie(lefts[0])] + list(lefts[1:]), rights)] + list(pairs[1:])
        (term,) = weight_rows(plan.theirs, plan.wrows, tied)
        self.others.append(plan.swap(self.clock.mark(term)))
        self.pairs += list(pairs)

    def mine(self):
        plan = self.plan
        lefts, rights = self.pairs[0]
        tied = [([self.clock.tie(lefts[0])] + list(lefts[1:]), rights)] + self.pairs[1:]
        term, self.own = weight_rows(plan.mine, plan.wrows, tied, self.others)
        self.moving = plan.step(self.clock.mark(term))
        self.k -= 1

    def advance(self):
        plan = self.plan
        moving = self.clock.tie(self.moving)
        term = ring_add(plan.core, self.own, moving, 2 * (plan.half - 1 - self.k))
        self.moving = plan.step(self.clock.mark(term))
        self.k -= 1

    def result(self):
        plan = self.plan
        rows = plan.wrows
        final = self.moving.astype(F32) + self.own[-2 * rows :].astype(F32)
        keep = lax.dynamic_slice_in_dim(final, plan.w * rows, rows, 0)
        give = lax.dynamic_slice_in_dim(final, (1 - plan.w) * rows, rows, 0)
        return keep + plan.swap(give.astype(BF)).astype(F32)


class Clock:
    def __init__(self):
        self.last = None

    def tie(self, value):
        return value if self.last is None else after(value, self.last)

    def mark(self, value):
        self.last = value
        return value


def interleave(keys, values):
    lead = keys.shape[0]
    both = jnp.stack([keys.reshape(lead, PAIRS, LANES), values.reshape(lead, PAIRS, LANES)], axis=2)
    return both.reshape(lead, 2 * D)


def apart(both):
    lead = both.shape[0]
    both = both.reshape(lead, PAIRS, 2, LANES)
    return both[:, :, 0].reshape(lead, D), both[:, :, 1].reshape(lead, D)


def body(
    boundary, segment_ids, qkv_weight, attn_out_weight, ffn_in_weight, ffn_out_weight, norm_gains
):
    section = lax.axis_index("section")
    sections = lax.axis_size("section")
    plan = Plan(boundary)
    rows = plan.rows

    pad = FFP - FF
    wide_shard = jnp.concatenate(
        [
            interleave(qkv_weight[0][:, D : 2 * D], qkv_weight[0][:, 2 * D :]),
            qkv_weight[0][:, :D],
            attn_out_weight[0],
            jnp.pad(norm_gains[0].T, ((0, 0), (0, LANES - 2))),
        ],
        axis=1,
    )
    in_shard = jnp.pad(ffn_in_weight[0][:, :FF], ((0, 0), (0, pad)))
    gate_shard = jnp.pad(ffn_in_weight[0][:, FF:], ((0, 0), (0, pad)))
    back_shard = jnp.pad(ffn_out_weight[0].T, ((0, 0), (0, pad)))
    get_wide = Gather(plan, wide_shard)
    get_in = Gather(plan, in_shard)
    parts = plan.across(after(boundary[0, :, 0], get_wide.start, get_in.start))
    got = [get.advance() for get in (get_wide, get_in)]
    get_gate = Gather(plan, after(gate_shard, *got))
    get_back = Gather(plan, after(back_shard, *got))
    own = plan.along(after(parts, *got))
    got = [get.advance() for get in (get_wide, get_in)]
    ids = after(segment_ids[:, 0], *got)
    for n in range(plan.half - 2):
        got = get_wide.advance(), get_in.advance(*([own] if n == plan.half - 3 else []))
        if n == 0:
            got_first = got
    got_gate, got_back = get_gate.advance(got[1]), get_back.advance(got[0])

    ids = plan.in_order(ids[None], plan.swap(ids[None])).transpose(1, 0, 2)
    ids = jnp.repeat(ids.reshape(plan.micro * plan.nw, plan.tok_rows), plan.g, axis=0)
    line = after(lax.all_to_all(ids, "ctx", 0, 0, tiled=True).reshape(-1), *got_first)
    grid = line.reshape(plan.n_ctx, plan.members, plan.r)
    place = (plan.i % plan.g) * plan.nw + plan.w
    seg_pieces = [
        lax.dynamic_index_in_dim(grid, (place - by) % plan.members, 1, keepdims=False).reshape(rows)
        for by in range(plan.members)
    ]
    segq = seg_pieces[0]
    segk = jnp.concatenate(seg_pieces)
    token = (
        lax.broadcasted_iota(jnp.int32, (plan.n_ctx, plan.r), 0) * plan.tok_rows
        + place * plan.r
        + lax.broadcasted_iota(jnp.int32, (plan.n_ctx, plan.r), 1)
    ).reshape(rows)
    first = jnp.sum((line[None, :] < segq[:, None]).astype(jnp.int32), axis=1)
    position = (token - first).astype(F32)
    exponent = jnp.arange(HEAD_DIM // 2, dtype=F32) * (-2.0 / HEAD_DIM)
    angles = position[:, None] * (ROPE_BASE**exponent)[None, :]
    cosine, sine = jnp.cos(angles), jnp.sin(angles)
    cos_rows = jnp.concatenate([cosine] * 4, axis=1)
    sin_rows = jnp.concatenate([-sine, sine] * 2, axis=1)
    qmarks, kmarks = query_marks(segq), key_marks(segk)

    w_kv = w_mix = get_wide.result()
    w_in = get_in.result()
    gains = gains_of(w_mix)

    def first_half(x):
        a, kv = keys_values(x, gains, w_kv, cos_rows, sin_rows)
        kv_list = plan.gather_rows(kv)
        return a, kv_list, queries_of(a, w_mix, cos_rows, sin_rows)

    _, kv_list, q = first_half(after(own, got_gate))
    got_gate = get_gate.advance()
    o, _ = attend(after(q, got_back, got_gate), kv_list, qmarks, kmarks, 0, PAIRS)
    got = get_back.advance(late=(o,)), get_gate.advance(late=(o,))
    h, b = project(own, [after(o, *got)], gains, w_mix)
    for one in (get_gate, get_back):
        while one.k < plan.half:
            one.advance()
    w_gate, w_back = get_gate.result(), get_back.result()
    (z,) = ffn_in(b, w_in, w_gate, False)
    first_out = ffn_out(h, z, w_back)

    def forward(x):
        a, kv_list, q = first_half(x)
        o, lse = attend(q, kv_list, qmarks, kmarks, 0, PAIRS)
        h, b = project(x, [o], gains, w_mix)
        z, act, slope = ffn_in(b, w_in, w_gate, True)
        return ffn_out(h, z, w_back), (x, a, q, kv_list, o, lse, h, b, z, act, slope)

    def backward(stash, grad):
        x, a, q, kv_list, o, lse, h, b, z, act, slope = stash
        da, dg = ffn_back(grad, act, slope, w_back)
        dh, dh_low, _ = hidden_back(grad, da, dg, h, gains, w_in, w_gate)
        dq, terms = attend_back(
            q, kv_list, dh_low, o, lse, qmarks, kmarks, w_mix, cos_rows, sin_rows, 0
        )
        dkv = keys_back(plan.scatter_rows(terms), cos_rows, sin_rows)
        return input_back(x, dh, [dq], [dkv], gains, w_kv, w_mix)[0]

    def last_backward(stash, grad, choose):
        x, a, q, kv_list, o, lse, h, b, z, act, slope = stash
        clock = Clock()
        back, grow, out, mixed = (Reduce(plan, clock) for _ in range(4))
        da, dg = ffn_back(clock.tie(grad), act, slope, w_back)
        clock.mark(da)
        grow.theirs(([b], [da, dg]))
        back.theirs(([grad], [z]))
        grow.mine()
        back.mine()
        dh, dh_low, gain_second = hidden_back(clock.tie(grad), da, dg, h, gains, w_in, w_gate)
        clock.mark(dh)
        grow.advance()
        back.advance()
        out.theirs(([o], [dh_low]))
        parts = []
        count = PAIRS // 4
        for n in range(4):
            cut = slice(n * count * LANES, (n + 1) * count * LANES)
            dq, terms = attend_back(
                clock.tie(q),
                kv_list,
                dh_low,
                o[:, cut],
                lse[n * count : (n + 1) * count],
                qmarks,
                kmarks,
                w_mix,
                cos_rows,
                sin_rows,
                n * count,
            )
            clock.mark(dq)
            parts.append((dq, plan.scatter_rows(terms)))
            if n == 0:
                out.mine()
            elif n == 1:
                for one in (grow, back, out):
                    one.advance()
        dkv_list = [keys_back(terms, cos_rows, sin_rows) for _, terms in parts]
        dq_list = [dq for dq, _ in parts]
        mixed.theirs(([a], dkv_list + dq_list))
        for one in (grow, back, out):
            one.advance()
        dx, gain_first = input_back(clock.tie(x), dh, dq_list, dkv_list, gains, w_kv, w_mix)
        clock.mark(dx)
        mixed.mine()
        mixed.moving = after(mixed.moving, grow.moving, back.moving)
        mixed.advance()
        sent = plan.back_along(after(choose(dx), clock.last))
        gain = jnp.concatenate([gain_first, gain_second], axis=0)
        gain = plan.total(after(gain, clock.last))
        for one in (grow, back, out):
            while one.k:
                one.advance()
        while mixed.k:
            if mixed.k == 1:
                mixed.moving = after(mixed.moving, sent)
            mixed.advance()
        start = (plan.i * plan.nw + plan.w) * plan.wrows
        gain = lax.dynamic_slice_in_dim(gain, start, plan.wrows, 1)
        return sent, [back.result(), grow.result(), out.result(), mixed.result(), gain]

    def handed(array, by):
        pairs = [(s, s + by) for s in range(sections) if 0 <= s + by < sections]
        return lax.ppermute(array, "section", pairs)

    x_in = jnp.where(section == 0, own, handed(first_out, 1))
    out, stash = forward(x_in)
    first_dx = backward(stash, own)
    grad_in = jnp.where(section == sections - 1, own, after(handed(first_dx, -1), out))
    sent, (g_back, g_grow, g_attn, g_mix, g_gain) = last_backward(
        stash, grad_in, lambda dx: jnp.where(section == 0, dx, out)
    )
    boundary_local = plan.back_across(sent)
    g_key, g_value = apart(g_mix[:, : 2 * D])
    return (
        boundary_local[None, :, None],
        jnp.concatenate([g_mix[:, 2 * D :], g_key, g_value], axis=1)[None],
        g_attn[None],
        jnp.concatenate([g_grow[:, :FF], g_grow[:, FFP : FFP + FF]], axis=1)[None],
        g_back[:, :FF].T[None],
        g_gain[None],
    )


def solution(mesh):
    placed = (
        P("section", None, "wshard", "ctx", None),
        P(None, "wshard", "ctx"),
        P("section", ("ctx", "wshard"), None),
        P("section", ("ctx", "wshard"), None),
        P("section", ("ctx", "wshard"), None),
        P("section", None, ("ctx", "wshard")),
        P("section", None, ("ctx", "wshard")),
    )
    return jax.shard_map(
        body,
        mesh=mesh,
        in_specs=placed,
        out_specs=(placed[0],) + placed[2:],
        check_vma=False,
    )
```

```python
from functools import partial

import jax
import jax.numpy as jnp
from jax import lax
from jax.experimental import pallas as pl
from jax.experimental.pallas import tpu as pltpu
from jax.sharding import PartitionSpec as P

D = 1024
HEADS = 16
HEAD_DIM = 64
FF = 2624
FFP = 2688
FFB = 896
LANES = 128
PAIRS = D // LANES
EPSILON = 1e-05
ROPE_BASE = 160000.0
NEG_FILL = -1e30
BF = jnp.bfloat16
F32 = jnp.float32
BOTH = ("ctx", "wshard")
IDS = 16
PENALTY = -(2.0**100)
NN = ((1,), (0,))
NT = ((1,), (1,))
TN = ((0,), (0,))
SMEM_SPEC = pl.BlockSpec(memory_space=pltpu.SMEM)


def dot(a, b, dims):
    return lax.dot_general(a, b, (dims, ((), ())), preferred_element_type=F32)


def after(value, *others):
    return lax.optimization_barrier((value,) + others)[0]


def shaped(shape, kind=BF):
    return jax.ShapeDtypeStruct(shape, kind)


def call(kernel, name, limit=20, flops=0, moved=0, exps=0, **more):
    return pl.pallas_call(
        kernel,
        name=name,
        compiler_params=pltpu.CompilerParams(vmem_limit_bytes=limit * 1024 * 1024),
        cost_estimate=pl.CostEstimate(
            flops=int(flops), bytes_accessed=int(moved), transcendentals=int(exps)
        ),
        **more,
    )


def whole(shape):
    return pl.BlockSpec(shape, lambda *_: (0,) * len(shape))


def rope_block(v, cosine, sine):
    lane = lax.broadcasted_iota(jnp.int32, v.shape, 1) % HEAD_DIM
    other = jnp.where(
        lane < HEAD_DIM // 2,
        pltpu.roll(v, LANES - HEAD_DIM // 2, 1),
        pltpu.roll(v, HEAD_DIM // 2, 1),
    )
    return v * cosine + other * sine


def norm_parts(values):
    center = values - jnp.mean(values, axis=-1, keepdims=True)
    spread = jnp.mean(center * center, axis=-1, keepdims=True)
    inverse = lax.rsqrt(spread + EPSILON)
    return center * inverse, inverse


def norm_back(values, gain_row, grad):
    hat, inverse = norm_parts(values)
    scaled = grad * gain_row
    back = inverse * (
        scaled
        - jnp.mean(scaled, axis=-1, keepdims=True)
        - hat * jnp.mean(scaled * hat, axis=-1, keepdims=True)
    )
    return back, jnp.sum(grad * hat, axis=0, keepdims=True)


def head_mask(shape, head):
    lane = lax.broadcasted_iota(jnp.int32, shape, 1)
    return (lane >= HEAD_DIM) if head else (lane < HEAD_DIM)


def pick(mask, v, other=0.0):
    return jnp.where(mask, v, jnp.full(v.shape, other, v.dtype))


def gains_of(w_mix):
    def kernel(w_ref, out_ref):
        out_ref[...] = w_ref[...].astype(F32).T[:8]

    return call(
        kernel,
        "gains",
        grid=(1,),
        in_specs=[pl.BlockSpec((D, LANES), lambda j: (0, 4 * D // LANES))],
        out_specs=whole((8, D)),
        out_shape=shaped((8, D), F32),
    )(w_mix)


def keys_values(x, gains, w_kv, cosine, sine):
    rows = x.shape[0]
    block = 512

    def kernel(x_ref, gain_ref, w_ref, cos_ref, sin_ref, a_ref, out_ref):
        @pl.when(pl.program_id(0) == 0)
        def _():
            hat, _ = norm_parts(x_ref[...].astype(F32))
            a_ref[...] = (hat * gain_ref[0:1]).astype(BF)

        m = dot(a_ref[...], w_ref[...], NN)
        for j in range(block // LANES):
            at = slice(j * LANES, (j + 1) * LANES)
            v = m[:, at]
            if j % 2 == 0:
                v = rope_block(v, cos_ref[...], sin_ref[...])
            out_ref[:, at] = v.astype(BF)

    return call(
        kernel,
        "keys_values",
        flops=2 * rows * D * 2 * D,
        moved=2 * (2 * D * D + 4 * rows * D),
        grid=(2 * D // block,),
        in_specs=[
            whole((rows, D)),
            whole((8, D)),
            pl.BlockSpec((D, block), lambda j: (0, j)),
            whole((rows, LANES)),
            whole((rows, LANES)),
        ],
        out_specs=[whole((rows, D)), pl.BlockSpec((rows, block), lambda j: (0, j))],
        out_shape=[shaped((rows, D)), shaped((rows, 2 * D))],
    )(x, gains, w_kv, cosine, sine)


def queries_of(a, w_mix, cosine, sine):
    rows = a.shape[0]
    block = 512

    def kernel(a_ref, w_ref, cos_ref, sin_ref, out_ref):
        m = dot(a_ref[...], w_ref[...], NN)
        for j in range(block // LANES):
            at = slice(j * LANES, (j + 1) * LANES)
            out_ref[:, at] = rope_block(m[:, at], cos_ref[...], sin_ref[...]).astype(BF)

    return call(
        kernel,
        "queries",
        flops=2 * rows * D * D,
        moved=2 * (D * D + 2 * rows * D),
        grid=(D // block,),
        in_specs=[
            whole((rows, D)),
            pl.BlockSpec((D, block), lambda j: (0, 2 * D // block + j)),
            whole((rows, LANES)),
            whole((rows, LANES)),
        ],
        out_specs=pl.BlockSpec((rows, block), lambda j: (0, j)),
        out_shape=shaped((rows, D)),
    )(a, w_mix, cosine, sine)


def key_marks(seg):
    lane = jnp.arange(LANES) % HEAD_DIM
    return jnp.where(lane < IDS, (seg[:, None] == lane), lane < IDS + 3).astype(BF)
def query_marks(seg):
    lane = jnp.arange(LANES) % HEAD_DIM
    return jnp.where((lane < IDS) & (seg[:, None] != lane), PENALTY, 0.0).astype(BF)

def split3(v):
    a = v.astype(BF).astype(F32)
    b = (v - a).astype(BF).astype(F32)
    return a, b, v - a - b


def attend(q, kv_list, qmarks, kmarks, begin, count, wide=2, ahead=2):
    rows = q.shape[0]
    members = len(kv_list)
    keys = members * rows

    def kernel(q_ref, qm_ref, km_ref, *refs):
        kv_refs, (o_ref, lse_ref) = refs[:members], refs[members:]
        heads = []
        for w in range(wide):
            k = jnp.concatenate([r[:, 2 * w * LANES : (2 * w + 1) * LANES] for r in kv_refs], axis=0)
            v = jnp.concatenate([r[:, (2 * w + 1) * LANES : (2 * w + 2) * LANES] for r in kv_refs], axis=0)
            q = q_ref[:, w * LANES : (w + 1) * LANES] * jnp.asarray(HEAD_DIM**-0.5, BF)
            for head in range(2):
                heads.append((w, head, q, k, v))

        def score(n):
            w, head, q, k, v = heads[n]
            mine, theirs = head_mask(q.shape, head), head_mask(k.shape, head)
            return dot(jnp.where(theirs, k, km_ref[...]), jnp.where(mine, q, qm_ref[...]), NT)

        waiting = [score(n) for n in range(ahead)]
        parts, stats = [], []
        for n, (w, head, q, k, v) in enumerate(heads):
            if n + ahead < len(heads):
                waiting.append(score(n + ahead))
            s = waiting[n]
            top = jnp.max(s, axis=0, keepdims=True)
            e = jnp.exp(s - top).astype(BF)
            u = dot(pick(head_mask(v.shape, head), v, 1.0), e, TN)
            low, high = u[:HEAD_DIM], u[HEAD_DIM:]
            value, total = (high, low) if head else (low, high)
            parts.append(value / total)
            stats.append(top + jnp.log(total[:1]))
        for w in range(wide):
            o_ref[:, w * LANES : (w + 1) * LANES] = jnp.concatenate(parts[2 * w : 2 * w + 2], axis=0).T.astype(BF)
            lse_ref[w] = jnp.concatenate(stats[2 * w : 2 * w + 2], axis=0)

    first = begin // wide
    return call(
        kernel,
        "attend",
        limit=28,
        flops=8 * rows * keys * count * LANES,
        moved=2 * (2 * rows + 2 * keys) * count * LANES,
        exps=rows * keys * count * 2,
        grid=(count // wide,),
        in_specs=[
            pl.BlockSpec((rows, wide * LANES), lambda p: (0, first + p)),
            whole((rows, LANES)),
            whole((keys, LANES)),
        ]
        + [pl.BlockSpec((rows, 2 * wide * LANES), lambda p: (0, first + p))] * members,
        out_specs=[
            pl.BlockSpec((rows, wide * LANES), lambda p: (0, p)),
            pl.BlockSpec((wide, 2, rows), lambda p: (p, 0, 0)),
        ],
        out_shape=[shaped((rows, count * LANES)), shaped((count, 2, rows), F32)],
    )(q, qmarks, kmarks, *kv_list)


def project(x, o_list, gains, w_mix):
    rows = x.shape[0]
    block = 512
    steps = D // block

    def kernel(x_ref, gain_ref, w_ref, *refs):
        o_refs, (h_ref, b_ref) = refs[:-2], refs[-2:]
        j = pl.program_id(0)
        at = pl.ds(pl.multiple_of(j * block, block), block)
        total = x_ref[:, at].astype(F32)
        begin = 0
        for o_ref in o_refs:
            end = begin + o_ref.shape[1]
            total += dot(o_ref[...], w_ref[begin:end], NN)
            begin = end
        h_ref[:, at] = total

        @pl.when(j == steps - 1)
        def _():
            hat, _ = norm_parts(h_ref[...])
            b_ref[...] = (hat * gain_ref[1:2]).astype(BF)

    return call(
        kernel,
        "project",
        flops=2 * rows * D * D,
        moved=2 * D * D + 10 * rows * D,
        grid=(steps,),
        in_specs=[
            whole((rows, D)),
            whole((8, D)),
            pl.BlockSpec((D, block), lambda j: (0, 3 * D // block + j)),
        ]
        + [whole(o.shape) for o in o_list],
        out_specs=[whole((rows, D)), whole((rows, D))],
        out_shape=[shaped((rows, D), F32), shaped((rows, D))],
    )(x, gains, w_mix, *o_list)


def ffn_in(b, w_in, w_gate, keep):
    rows = b.shape[0]
    steps = FFP // FFB

    def kernel(b_ref, wa_ref, wg_ref, z_ref, *kept):
        a = dot(b_ref[...], wa_ref[...], NN)
        g = dot(b_ref[...], wg_ref[...], NN)
        phi = 0.5 * (1.0 + lax.erf(a * 0.7071067811865476))
        act = a * phi
        z_ref[...] = (act * g).astype(BF)
        if keep:
            density = 0.3989422804014327 * jnp.exp(-0.5 * a * a)
            kept[0][...] = act.astype(BF)
            kept[1][...] = ((phi + a * density) * g).astype(BF)

    out_spec = pl.BlockSpec((rows, FFB), lambda j: (0, j))
    count = 3 if keep else 1
    return call(
        kernel,
        "ffn_in",
        flops=4 * rows * D * FFP,
        moved=2 * (2 * D * FFP + rows * D + count * rows * FFP),
        grid=(steps,),
        in_specs=[whole((rows, D))] + [pl.BlockSpec((D, FFB), lambda j: (0, j))] * 2,
        out_specs=[out_spec] * count,
        out_shape=[shaped((rows, FFP))] * count,
    )(b, w_in, w_gate)


def ffn_out(h, z, w_back):
    rows = h.shape[0]
    block = 256

    def kernel(h_ref, z_ref, w_ref, out_ref):
        out_ref[...] = (h_ref[...] + dot(z_ref[...], w_ref[...], NT)).astype(BF)

    return call(
        kernel,
        "ffn_out",
        flops=2 * rows * D * FFP,
        moved=2 * (D * FFP + rows * FFP + 3 * rows * D),
        grid=(D // block,),
        in_specs=[
            pl.BlockSpec((rows, block), lambda j: (0, j)),
            whole((rows, FFP)),
            pl.BlockSpec((block, FFP), lambda j: (j, 0)),
        ],
        out_specs=pl.BlockSpec((rows, block), lambda j: (0, j)),
        out_shape=shaped((rows, D)),
    )(h, z, w_back)


def ffn_back(grad, act, slope, w_back):
    rows = grad.shape[0]

    def kernel(g_ref, act_ref, slope_ref, w_ref, da_ref, dg_ref):
        dz = dot(g_ref[...], w_ref[...], NN)
        da_ref[...] = (dz * slope_ref[...].astype(F32)).astype(BF)
        dg_ref[...] = (dz * act_ref[...].astype(F32)).astype(BF)

    spec = pl.BlockSpec((rows, FFB), lambda j: (0, j))
    return call(
        kernel,
        "ffn_back",
        flops=2 * rows * D * FFP,
        moved=2 * (D * FFP + 4 * rows * FFP + rows * D),
        grid=(FFP // FFB,),
        in_specs=[whole((rows, D)), spec, spec, pl.BlockSpec((D, FFB), lambda j: (0, j))],
        out_specs=[spec, spec],
        out_shape=[shaped((rows, FFP))] * 2,
    )(grad, act, slope, w_back)


def hidden_back(grad, da, dg, h, gains, w_in, w_gate):
    rows = grad.shape[0]
    block = 256
    steps = D // block

    def kernel(g_ref, da_ref, dg_ref, h_ref, gain_ref, wa_ref, wg_ref, dh_ref, low_ref, sum_ref):
        j = pl.program_id(0)
        at = pl.ds(pl.multiple_of(j * block, block), block)
        dh_ref[:, at] = dot(da_ref[...], wa_ref[...], NT) + dot(dg_ref[...], wg_ref[...], NT)

        @pl.when(j == steps - 1)
        def _():
            back, total = norm_back(h_ref[...], gain_ref[1:2], dh_ref[...])
            dh = g_ref[...].astype(F32) + back
            dh_ref[...] = dh
            low_ref[...] = dh.astype(BF)
            sum_ref[...] = total

    return call(
        kernel,
        "hidden_back",
        flops=4 * rows * D * FFP,
        moved=2 * (2 * D * FFP + 2 * rows * FFP + 6 * rows * D),
        grid=(steps,),
        in_specs=[
            whole((rows, D)),
            whole((rows, FFP)),
            whole((rows, FFP)),
            whole((rows, D)),
            whole((8, D)),
        ]
        + [pl.BlockSpec((block, FFP), lambda j: (j, 0))] * 2,
        out_specs=[whole((rows, D)), whole((rows, D)), whole((1, D))],
        out_shape=[shaped((rows, D), F32), shaped((rows, D)), shaped((1, D), F32)],
    )(grad, da, dg, h, gains, w_in, w_gate)


def attend_back(q, kv_list, dh_low, o, lse, qmarks, kmarks, w_mix, cosine, sine, begin):
    count = o.shape[1] // LANES
    rows = q.shape[0]
    members = len(kv_list)
    keys = members * rows

    def kernel(q_ref, dh_ref, w_ref, o_ref, lse_ref, qm_ref, km_ref, cos_ref, sin_ref, *refs):
        kv_refs, (dq_ref, *dkv_refs) = refs[:members], refs[members:]
        k = jnp.concatenate([r[:, :LANES] for r in kv_refs], axis=0)
        v = jnp.concatenate([r[:, LANES:] for r in kv_refs], axis=0)
        do = dot(dh_ref[...], w_ref[...], NT).astype(BF)
        q = q_ref[...] * jnp.asarray(HEAD_DIM**-0.5, BF)
        prod = do.astype(F32) * o_ref[...].astype(F32)
        lse = lse_ref[0]
        row = lax.broadcasted_iota(jnp.int32, (LANES, rows), 0)
        beside = jnp.zeros((LANES, rows), F32)
        for head in range(2):
            for n, part in enumerate(split3(-lse[head : head + 1])):
                beside = jnp.where(row == IDS + n + (HEAD_DIM if head == 0 else 0), part, beside)
        beside = beside.T.astype(BF) + qm_ref[...]
        lane = lax.broadcasted_iota(jnp.int32, (rows, LANES), 1)
        dks, dvs, dqs = [], [], []
        for head in range(2):
            mine = head_mask((rows, LANES), head)
            theirs = head_mask((keys, LANES), head)
            delta = jnp.sum(jnp.where(mine, prod, 0.0), axis=1, keepdims=True)
            there = jnp.zeros((rows, LANES), F32)
            for n, part in enumerate(split3(-delta)):
                there = jnp.where(lane == IDS + n + (HEAD_DIM if head == 0 else 0), part, there)
            qh = jnp.where(mine, q, beside)
            doh = jnp.where(mine, do, there.astype(BF))
            kh = jnp.where(theirs, k, km_ref[...])
            vh = jnp.where(theirs, v, km_ref[...])
            p = jnp.exp(dot(kh, qh, NT))
            ds = (p * dot(vh, doh, NT)).astype(BF)
            dvs.append(dot(p.astype(BF), do, NN))
            dks.append(dot(ds, q, NN))
            dqs.append(dot(ds, k, TN))
        first = head_mask((rows, LANES), 0)
        dq = jnp.where(first, dqs[0], dqs[1])
        dq = rope_block(dq * HEAD_DIM**-0.5, cos_ref[...], -sin_ref[...])
        dq_ref[...] = dq.astype(BF)
        for m, out in enumerate(dkv_refs):
            cut = slice(m * rows, (m + 1) * rows)
            out[:, :LANES] = jnp.where(first, dks[0][cut], dks[1][cut]).astype(BF)
            out[:, LANES:] = jnp.where(first, dvs[0][cut], dvs[1][cut]).astype(BF)

    spec = pl.BlockSpec((rows, LANES), lambda p: (0, p))
    kv_spec = pl.BlockSpec((rows, 2 * LANES), lambda p: (0, p))
    results = call(
        kernel,
        "attend_back",
        flops=20 * rows * keys * count * LANES,
        moved=2 * (6 * rows + 4 * keys) * count * LANES,
        exps=rows * keys * 2 * count,
        grid=(count,),
        in_specs=[
            pl.BlockSpec((rows, LANES), lambda p: (0, begin + p)),
            whole((rows, D)),
            pl.BlockSpec((LANES, D), lambda p: (begin + p, 3)),
            spec,
            pl.BlockSpec((1, 2, rows), lambda p: (p, 0, 0)),
            whole((rows, LANES)),
            whole((keys, LANES)),
            whole((rows, LANES)),
            whole((rows, LANES)),
        ]
        + [pl.BlockSpec((rows, 2 * LANES), lambda p: (0, begin + p))] * members,
        out_specs=[spec] + [kv_spec] * members,
        out_shape=[shaped((rows, count * LANES))] + [shaped((rows, 2 * count * LANES))] * members,
    )(q, dh_low, w_mix, o, lse, qmarks, kmarks, cosine, sine, *kv_list)
    return results[0], results[1:]


def keys_back(terms, cosine, sine):
    rows, columns = terms[0].shape

    def kernel(cos_ref, sin_ref, *refs):
        for b in range(columns // LANES):
            at = slice(b * LANES, (b + 1) * LANES)
            v = refs[0][:, at].astype(F32)
            for r in refs[1:-1]:
                v += r[:, at].astype(F32)
            if b % 2 == 0:
                v = rope_block(v, cos_ref[...], -sin_ref[...])
            refs[-1][:, at] = v.astype(BF)

    return call(
        kernel,
        "keys_back",
        flops=10 * rows * columns,
        moved=2 * (len(terms) + 1) * rows * columns,
        grid=(1,),
        in_specs=[whole((rows, LANES))] * 2 + [whole((rows, columns))] * len(terms),
        out_specs=whole((rows, columns)),
        out_shape=shaped((rows, columns)),
    )(cosine, sine, *terms)


def input_back(x, dh, dq_list, dkv_list, gains, w_kv, w_mix):
    rows = x.shape[0]
    block = 256
    steps = D // block
    grads = list(dkv_list) + list(dq_list)

    def kernel(x_ref, dh_ref, gain_ref, wkv_ref, wq_ref, *refs):
        grad_refs, (dx_ref, sum_ref, da_ref) = refs[:-3], refs[-3:]
        j = pl.program_id(0)
        total = 0.0
        begin = 0
        for n, ref in enumerate(grad_refs):
            if n == len(dkv_list):
                begin = 0
            end = begin + ref.shape[1]
            w_ref = wkv_ref if n < len(dkv_list) else wq_ref
            total += dot(ref[...], w_ref[:, begin:end], NT)
            begin = end
        da_ref[:, pl.ds(pl.multiple_of(j * block, block), block)] = total

        @pl.when(j == steps - 1)
        def _():
            back, total = norm_back(x_ref[...].astype(F32), gain_ref[0:1], da_ref[...])
            dx_ref[...] = (dh_ref[...] + back).astype(BF)
            sum_ref[...] = total

    return call(
        kernel,
        "input_back",
        flops=6 * rows * D * D,
        moved=2 * (3 * D * D + 10 * rows * D),
        grid=(steps,),
        in_specs=[
            whole((rows, D)),
            whole((rows, D)),
            whole((8, D)),
            pl.BlockSpec((block, 2 * D), lambda j: (j, 0)),
            pl.BlockSpec((block, D), lambda j: (j, 2)),
        ]
        + [whole(g.shape) for g in grads],
        out_specs=[whole((rows, D)), whole((1, D))],
        out_shape=[shaped((rows, D)), shaped((1, D), F32)],
        scratch_shapes=[pltpu.VMEM((rows, D), F32)],
    )(x, dh, gains, w_kv, w_mix, *grads)


def weight_rows(order, rows, pairs, others=None):
    count = order.shape[0]
    tokens = pairs[0][0][0].shape[0]
    widths = [sum(r.shape[1] for r in rights) for _, rights in pairs]
    columns = sum(widths)
    flat = [v for lefts, rights in pairs for v in list(lefts) + list(rights)]
    flat += [] if others is None else list(others)
    added = 0 if others is None else others[0].shape[0]
    outs = 1 if others is None else 2

    def kernel(order_ref, *refs):
        out_refs, (turned_ref, left_ref) = refs[len(flat) : len(flat) + outs], refs[-2:]
        other_refs = [] if others is None else refs[len(flat) - len(others) : len(flat)]
        spans, at = [], 0
        for ref in other_refs:
            spans.append((at, at + ref.shape[1], ref))
            at += ref.shape[1]
        at = where = 0
        for lefts, rights in pairs:
            row = 0
            for _ in lefts:
                ref = refs[where]
                turned_ref[row : row + ref.shape[1]] = ref[...].T
                row += ref.shape[1]
                where += 1
            for n in range(count):
                start = pl.multiple_of(order_ref[n] * rows, rows)
                left_ref[n * rows : (n + 1) * rows] = turned_ref[pl.ds(start, rows)]
            for _ in rights:
                ref = refs[where]
                width = ref.shape[1]
                for begin in range(0, width, 512):
                    end = min(begin + 512, width)
                    cols = slice(at + begin, at + end)
                    term = dot(left_ref[...], ref[:, begin:end], NN)
                    if others is None:
                        out_refs[0][:, cols] = term.astype(BF)
                        continue
                    low, other_ref = next((a, r) for a, b, r in spans if a <= cols.start < b)
                    there = slice(cols.start - low, cols.stop - low)
                    near = term[:added] + other_ref[:, there].astype(F32)
                    out_refs[0][:, cols] = near[:rows].astype(BF)
                    out_refs[1][: added - rows, cols] = near[rows:].astype(BF)
                    out_refs[1][added - rows :, cols] = term[added:].astype(BF)
                at += width
                where += 1

    shapes = [shaped((count * rows, columns))]
    if others is not None:
        shapes = [shaped((rows, columns)), shaped(((count - 1) * rows, columns))]
    size = 2 * (count * rows * columns + sum(v.size for v in flat))
    return call(
        kernel,
        "weight_rows",
        limit=max(8, 4 + int(1.25 * size) // (1024 * 1024)),
        flops=2 * count * rows * tokens * columns,
        moved=size,
        in_specs=[SMEM_SPEC] + [pl.BlockSpec(memory_space=pltpu.VMEM)] * len(flat),
        out_specs=[pl.BlockSpec(memory_space=pltpu.VMEM)] * outs,
        out_shape=shapes,
        scratch_shapes=[
            pltpu.VMEM((D, tokens), BF),
            pltpu.VMEM((count * rows, tokens), BF),
        ],
    )(order, *flat)


def ring_add(core, own, moving, first):
    rows = moving.shape[0] if first == 0 else moving.shape[0] // 2
    columns = own.shape[1]
    single = first == 0

    def kernel(core_ref, own_ref, moving_ref, out_ref):
        moved = moving_ref[...].astype(F32)
        if single:
            moved = jnp.where(core_ref[0] == pl.program_id(0), moved, 0.0)
        out_ref[...] = (own_ref[...].astype(F32) + moved).astype(BF)

    return call(
        kernel,
        "ring_add",
        limit=8,
        flops=4 * rows * columns,
        moved=12 * rows * columns,
        grid=(2,),
        in_specs=[
            SMEM_SPEC,
            pl.BlockSpec((rows, columns), lambda j: (first + j, 0)),
            pl.BlockSpec((rows, columns), (lambda j: (0, 0)) if single else (lambda j: (j, 0))),
        ],
        out_specs=pl.BlockSpec((rows, columns), lambda j: (j, 0)),
        out_shape=shaped((2 * rows, columns)),
    )(core, own, moving)


def blank(shape):
    def kernel(out_ref):
        pass

    return call(
        kernel,
        "blank",
        limit=1,
        out_specs=pl.BlockSpec(memory_space=pl.ANY),
        out_shape=shaped(shape),
    )()


class Plan:
    def __init__(self, boundary):
        self.micro = boundary.shape[1]
        self.tok_rows = boundary.shape[3]
        self.n_ctx = lax.axis_size("ctx")
        self.nw = lax.axis_size("wshard")
        self.g = self.n_ctx // (self.micro * self.nw)
        self.r = self.tok_rows // (self.g * self.nw)
        self.i = lax.axis_index("ctx")
        self.w = lax.axis_index("wshard")
        self.rows = self.n_ctx * self.r
        self.members = self.g * self.nw
        count = self.n_ctx
        chips = [2 * p if p < count // 2 else 2 * (count - 1 - p) + 1 for p in range(count)]
        self.half = count // 2
        self.way = 1 - 2 * self.w
        self.ring_pairs = []
        for p in range(count):
            self.ring_pairs.append((chips[p] * 2, chips[(p + 1) % count] * 2))
            self.ring_pairs.append((chips[p] * 2 + 1, chips[(p - 1) % count] * 2 + 1))
        place = jnp.where(self.i % 2 == 0, self.i // 2, count - 1 - self.i // 2)

        def chip(at):
            at = at % count
            return jnp.where(at < count // 2, 2 * at, 2 * (count - 1 - at) + 1)

        self.behind = [chip(place - self.way * k) for k in range(self.half + 1)]
        self.ahead = [chip(place + self.way * k) for k in range(self.half + 1)]
        self.wrows = D // (self.n_ctx * self.nw)
        near = range(self.half - 1, 0, -1)
        theirs = [2 * self.ahead[self.half] + 1 - self.w]
        mine = [2 * self.ahead[self.half] + self.w]
        for k in near:
            theirs += [2 * self.behind[k], 2 * self.behind[k] + 1]
            mine += [2 * self.ahead[k], 2 * self.ahead[k] + 1]
        mine += [2 * self.i, 2 * self.i + 1]
        self.theirs = jnp.stack(theirs).astype(jnp.int32)
        self.mine = jnp.stack(mine).astype(jnp.int32)
        self.core = self.w[None].astype(jnp.int32)

    def swap(self, array):
        return lax.ppermute(array, "wshard", [(0, 1), (1, 0)])

    def step(self, array):
        return lax.ppermute(array, BOTH, self.ring_pairs)

    def in_order(self, own, other):
        first = self.w == 0
        return jnp.concatenate(
            [jnp.where(first, own, other), jnp.where(first, other, own)], axis=0
        )

    def across(self, local):
        parts = local.reshape(self.micro, self.g, self.nw, self.r, D)
        parts = lax.all_to_all(parts.transpose(2, 0, 1, 3, 4), "wshard", 0, 0, tiled=True)
        return parts.transpose(1, 0, 2, 3, 4).reshape(self.n_ctx, self.r, D)

    def along(self, parts):
        return lax.all_to_all(parts, "ctx", 0, 0, tiled=True).reshape(self.rows, D)

    def back_along(self, rows):
        return lax.all_to_all(rows.reshape(self.n_ctx, self.r, D), "ctx", 0, 0, tiled=True)

    def back_across(self, parts):
        parts = parts.reshape(self.micro, self.nw, self.g, self.r, D).transpose(1, 0, 2, 3, 4)
        parts = lax.all_to_all(parts, "wshard", 0, 0, tiled=True)
        return parts.transpose(1, 2, 0, 3, 4).reshape(self.micro, self.tok_rows, D)

    def total(self, value):
        by = 1
        while by < self.n_ctx * self.nw:
            pairs = [(n, n ^ by) for n in range(self.n_ctx * self.nw)]
            value = value + lax.ppermute(value, BOTH, pairs)
            by *= 2
        return value

    def rotation(self, by):
        pairs = []
        for flat in range(self.n_ctx * self.nw):
            group, place = divmod(flat, self.members)
            pairs.append((flat, group * self.members + (place + by) % self.members))
        return pairs

    def gather_rows(self, rows):
        return [rows] + [
            lax.ppermute(rows, BOTH, self.rotation(by)) for by in range(1, self.members)
        ]

    def scatter_rows(self, terms):
        return [terms[0]] + [
            lax.ppermute(terms[by], BOTH, self.rotation(-by)) for by in range(1, self.members)
        ]


class Gather:
    def __init__(self, plan, shard, *deps):
        self.plan = plan
        self.rows = shard.shape[0]
        self.whole = blank((plan.n_ctx, plan.nw * self.rows, shard.shape[1]))
        self.current = plan.in_order(shard, plan.swap(shard))
        self.start = self.current
        self.put(self.current, plan.i)
        self.k = 0

    def put(self, block, chip):
        self.whole = lax.dynamic_update_index_in_dim(self.whole, block, chip, 0)

    def advance(self, *deps, late=()):
        plan = self.plan
        self.k += 1
        current = after(self.current, *deps) if deps else self.current
        if self.k < plan.half:
            current = plan.step(current)
            if late:
                current = after(current, *late)
            self.put(current, plan.behind[self.k])
            self.put(plan.swap(current), plan.ahead[self.k])
        else:
            part = lax.dynamic_slice_in_dim(current, plan.w * self.rows, self.rows, 0)
            current = plan.step(part)
            if late:
                current = after(current, *late)
            self.put(plan.in_order(current, plan.swap(current)), plan.behind[plan.half])
        self.current = current
        return current

    def result(self):
        return self.whole.reshape(D, self.whole.shape[2])


class Reduce:
    def __init__(self, plan, clock):
        self.plan, self.clock = plan, clock
        self.pairs, self.others = [], []
        self.k = plan.half

    def theirs(self, *pairs):
        plan = self.plan
        lefts, rights = pairs[0]
        tied = [([self.clock.tie(lefts[0])] + list(lefts[1:]), rights)] + list(pairs[1:])
        (term,) = weight_rows(plan.theirs, plan.wrows, tied)
        self.others.append(plan.swap(self.clock.mark(term)))
        self.pairs += list(pairs)

    def mine(self):
        plan = self.plan
        lefts, rights = self.pairs[0]
        tied = [([self.clock.tie(lefts[0])] + list(lefts[1:]), rights)] + self.pairs[1:]
        term, self.own = weight_rows(plan.mine, plan.wrows, tied, self.others)
        self.moving = plan.step(self.clock.mark(term))
        self.k -= 1

    def advance(self):
        plan = self.plan
        moving = self.clock.tie(self.moving)
        term = ring_add(plan.core, self.own, moving, 2 * (plan.half - 1 - self.k))
        self.moving = plan.step(self.clock.mark(term))
        self.k -= 1

    def result(self):
        plan = self.plan
        rows = plan.wrows
        final = self.moving.astype(F32) + self.own[-2 * rows :].astype(F32)
        keep = lax.dynamic_slice_in_dim(final, plan.w * rows, rows, 0)
        give = lax.dynamic_slice_in_dim(final, (1 - plan.w) * rows, rows, 0)
        return keep + plan.swap(give.astype(BF)).astype(F32)


class Clock:
    def __init__(self):
        self.last = None

    def tie(self, value):
        return value if self.last is None else after(value, self.last)

    def mark(self, value):
        self.last = value
        return value


def interleave(keys, values):
    lead = keys.shape[0]
    both = jnp.stack([keys.reshape(lead, PAIRS, LANES), values.reshape(lead, PAIRS, LANES)], axis=2)
    return both.reshape(lead, 2 * D)


def apart(both):
    lead = both.shape[0]
    both = both.reshape(lead, PAIRS, 2, LANES)
    return both[:, :, 0].reshape(lead, D), both[:, :, 1].reshape(lead, D)


def body(
    boundary, segment_ids, qkv_weight, attn_out_weight, ffn_in_weight, ffn_out_weight, norm_gains
):
    section = lax.axis_index("section")
    sections = lax.axis_size("section")
    plan = Plan(boundary)
    rows = plan.rows

    pad = FFP - FF
    wide_shard = jnp.concatenate(
        [
            interleave(qkv_weight[0][:, D : 2 * D], qkv_weight[0][:, 2 * D :]),
            qkv_weight[0][:, :D],
            attn_out_weight[0],
            jnp.pad(norm_gains[0].T, ((0, 0), (0, LANES - 2))),
        ],
        axis=1,
    )
    in_shard = jnp.pad(ffn_in_weight[0][:, :FF], ((0, 0), (0, pad)))
    gate_shard = jnp.pad(ffn_in_weight[0][:, FF:], ((0, 0), (0, pad)))
    back_shard = jnp.pad(ffn_out_weight[0].T, ((0, 0), (0, pad)))
    get_wide = Gather(plan, wide_shard)
    get_in = Gather(plan, in_shard)
    parts = plan.across(after(boundary[0, :, 0], get_wide.start, get_in.start))
    got = [get.advance() for get in (get_wide, get_in)]
    get_gate = Gather(plan, after(gate_shard, *got))
    get_back = Gather(plan, after(back_shard, *got))
    own = plan.along(after(parts, *got))
    got = [get.advance() for get in (get_wide, get_in)]
    ids = after(segment_ids[:, 0], *got)
    for n in range(plan.half - 2):
        got = get_wide.advance(), get_in.advance(*([own] if n == plan.half - 3 else []))
        if n == 0:
            got_first = got
    got_gate, got_back = get_gate.advance(got[1]), get_back.advance(got[0])

    ids = plan.in_order(ids[None], plan.swap(ids[None])).transpose(1, 0, 2)
    ids = jnp.repeat(ids.reshape(plan.micro * plan.nw, plan.tok_rows), plan.g, axis=0)
    line = after(lax.all_to_all(ids, "ctx", 0, 0, tiled=True).reshape(-1), *got_first)
    grid = line.reshape(plan.n_ctx, plan.members, plan.r)
    place = (plan.i % plan.g) * plan.nw + plan.w
    seg_pieces = [
        lax.dynamic_index_in_dim(grid, (place - by) % plan.members, 1, keepdims=False).reshape(rows)
        for by in range(plan.members)
    ]
    segq = seg_pieces[0]
    segk = jnp.concatenate(seg_pieces)
    token = (
        lax.broadcasted_iota(jnp.int32, (plan.n_ctx, plan.r), 0) * plan.tok_rows
        + place * plan.r
        + lax.broadcasted_iota(jnp.int32, (plan.n_ctx, plan.r), 1)
    ).reshape(rows)
    first = jnp.sum((line[None, :] < segq[:, None]).astype(jnp.int32), axis=1)
    position = (token - first).astype(F32)
    exponent = jnp.arange(HEAD_DIM // 2, dtype=F32) * (-2.0 / HEAD_DIM)
    angles = position[:, None] * (ROPE_BASE**exponent)[None, :]
    cosine, sine = jnp.cos(angles), jnp.sin(angles)
    cos_rows = jnp.concatenate([cosine] * 4, axis=1)
    sin_rows = jnp.concatenate([-sine, sine] * 2, axis=1)
    qmarks, kmarks = query_marks(segq), key_marks(segk)

    w_kv = w_mix = get_wide.result()
    w_in = get_in.result()
    gains = gains_of(w_mix)

    def first_half(x):
        a, kv = keys_values(x, gains, w_kv, cos_rows, sin_rows)
        kv_list = plan.gather_rows(kv)
        return a, kv_list, queries_of(a, w_mix, cos_rows, sin_rows)

    _, kv_list, q = first_half(after(own, got_gate))
    got_gate = get_gate.advance()
    o, _ = attend(after(q, got_back, got_gate), kv_list, qmarks, kmarks, 0, PAIRS)
    got = get_back.advance(late=(o,)), get_gate.advance(late=(o,))
    h, b = project(own, [after(o, *got)], gains, w_mix)
    for one in (get_gate, get_back):
        while one.k < plan.half:
            one.advance()
    w_gate, w_back = get_gate.result(), get_back.result()
    (z,) = ffn_in(b, w_in, w_gate, False)
    first_out = ffn_out(h, z, w_back)

    def forward(x):
        a, kv_list, q = first_half(x)
        o, lse = attend(q, kv_list, qmarks, kmarks, 0, PAIRS)
        h, b = project(x, [o], gains, w_mix)
        z, act, slope = ffn_in(b, w_in, w_gate, True)
        return ffn_out(h, z, w_back), (x, a, q, kv_list, o, lse, h, b, z, act, slope)

    def backward(stash, grad):
        x, a, q, kv_list, o, lse, h, b, z, act, slope = stash
        da, dg = ffn_back(grad, act, slope, w_back)
        dh, dh_low, _ = hidden_back(grad, da, dg, h, gains, w_in, w_gate)
        dq, terms = attend_back(
            q, kv_list, dh_low, o, lse, qmarks, kmarks, w_mix, cos_rows, sin_rows, 0
        )
        dkv = keys_back(plan.scatter_rows(terms), cos_rows, sin_rows)
        return input_back(x, dh, [dq], [dkv], gains, w_kv, w_mix)[0]

    def last_backward(stash, grad, choose):
        x, a, q, kv_list, o, lse, h, b, z, act, slope = stash
        clock = Clock()
        back, grow, out, mixed = (Reduce(plan, clock) for _ in range(4))
        da, dg = ffn_back(clock.tie(grad), act, slope, w_back)
        clock.mark(da)
        grow.theirs(([b], [da, dg]))
        back.theirs(([grad], [z]))
        grow.mine()
        back.mine()
        dh, dh_low, gain_second = hidden_back(clock.tie(grad), da, dg, h, gains, w_in, w_gate)
        clock.mark(dh)
        grow.advance()
        back.advance()
        out.theirs(([o], [dh_low]))
        parts = []
        count = PAIRS // 4
        for n in range(4):
            cut = slice(n * count * LANES, (n + 1) * count * LANES)
            dq, terms = attend_back(
                clock.tie(q),
                kv_list,
                dh_low,
                o[:, cut],
                lse[n * count : (n + 1) * count],
                qmarks,
                kmarks,
                w_mix,
                cos_rows,
                sin_rows,
                n * count,
            )
            clock.mark(dq)
            parts.append((dq, plan.scatter_rows(terms)))
            if n == 0:
                out.mine()
            elif n == 1:
                for one in (grow, back, out):
                    one.advance()
        dkv_list = [keys_back(terms, cos_rows, sin_rows) for _, terms in parts]
        dq_list = [dq for dq, _ in parts]
        mixed.theirs(([a], dkv_list + dq_list))
        for one in (grow, back, out):
            one.advance()
        dx, gain_first = input_back(clock.tie(x), dh, dq_list, dkv_list, gains, w_kv, w_mix)
        clock.mark(dx)
        mixed.mine()
        mixed.moving = after(mixed.moving, grow.moving, back.moving)
        mixed.advance()
        sent = plan.back_along(after(choose(dx), clock.last))
        gain = jnp.concatenate([gain_first, gain_second], axis=0)
        gain = plan.total(after(gain, clock.last))
        for one in (grow, back, out):
            while one.k:
                one.advance()
        while mixed.k:
            if mixed.k == 1:
                mixed.moving = after(mixed.moving, sent)
            mixed.advance()
        start = (plan.i * plan.nw + plan.w) * plan.wrows
        gain = lax.dynamic_slice_in_dim(gain, start, plan.wrows, 1)
        return sent, [back.result(), grow.result(), out.result(), mixed.result(), gain]

    def handed(array, by):
        pairs = [(s, s + by) for s in range(sections) if 0 <= s + by < sections]
        return lax.ppermute(array, "section", pairs)

    x_in = jnp.where(section == 0, own, handed(first_out, 1))
    out, stash = forward(x_in)
    first_dx = backward(stash, own)
    grad_in = jnp.where(section == sections - 1, own, after(handed(first_dx, -1), out))
    sent, (g_back, g_grow, g_attn, g_mix, g_gain) = last_backward(
        stash, grad_in, lambda dx: jnp.where(section == 0, dx, out)
    )
    boundary_local = plan.back_across(sent)
    g_key, g_value = apart(g_mix[:, : 2 * D])
    return (
        boundary_local[None, :, None],
        jnp.concatenate([g_mix[:, 2 * D :], g_key, g_value], axis=1)[None],
        g_attn[None],
        jnp.concatenate([g_grow[:, :FF], g_grow[:, FFP : FFP + FF]], axis=1)[None],
        g_back[:, :FF].T[None],
        g_gain[None],
    )


def solution(mesh):
    placed = (
        P("section", None, "wshard", "ctx", None),
        P(None, "wshard", "ctx"),
        P("section", ("ctx", "wshard"), None),
        P("section", ("ctx", "wshard"), None),
        P("section", ("ctx", "wshard"), None),
        P("section", None, ("ctx", "wshard")),
        P("section", None, ("ctx", "wshard")),
    )
    return jax.shard_map(
        body,
        mesh=mesh,
        in_specs=placed,
        out_specs=(placed[0],) + placed[2:],
        check_vma=False,
    )
```

```python
from functools import partial

import jax
import jax.numpy as jnp
from jax import lax
from jax.experimental import pallas as pl
from jax.experimental.pallas import tpu as pltpu
from jax.sharding import PartitionSpec as P

D = 1024
HEADS = 16
HEAD_DIM = 64
FF = 2624
FFP = 2688
FFB = 896
LANES = 128
PAIRS = D // LANES
EPSILON = 1e-05
ROPE_BASE = 160000.0
NEG_FILL = -1e30
BF = jnp.bfloat16
F32 = jnp.float32
BOTH = ("ctx", "wshard")
IDS = 16
PENALTY = -(2.0**100)
NN = ((1,), (0,))
NT = ((1,), (1,))
TN = ((0,), (0,))
SMEM_SPEC = pl.BlockSpec(memory_space=pltpu.SMEM)


def dot(a, b, dims):
    return lax.dot_general(a, b, (dims, ((), ())), preferred_element_type=F32)


def after(value, *others):
    return lax.optimization_barrier((value,) + others)[0]


def shaped(shape, kind=BF):
    return jax.ShapeDtypeStruct(shape, kind)


def call(kernel, name, limit=20, flops=0, moved=0, exps=0, **more):
    return pl.pallas_call(
        kernel,
        name=name,
        compiler_params=pltpu.CompilerParams(vmem_limit_bytes=limit * 1024 * 1024),
        cost_estimate=pl.CostEstimate(
            flops=int(flops), bytes_accessed=int(moved), transcendentals=int(exps)
        ),
        **more,
    )


def whole(shape):
    return pl.BlockSpec(shape, lambda *_: (0,) * len(shape))


def rope_block(v, cosine, sine):
    lane = lax.broadcasted_iota(jnp.int32, v.shape, 1) % HEAD_DIM
    other = jnp.where(
        lane < HEAD_DIM // 2,
        pltpu.roll(v, LANES - HEAD_DIM // 2, 1),
        pltpu.roll(v, HEAD_DIM // 2, 1),
    )
    return v * cosine + other * sine


def norm_parts(values):
    center = values - jnp.mean(values, axis=-1, keepdims=True)
    spread = jnp.mean(center * center, axis=-1, keepdims=True)
    inverse = lax.rsqrt(spread + EPSILON)
    return center * inverse, inverse


def norm_back(values, gain_row, grad):
    hat, inverse = norm_parts(values)
    scaled = grad * gain_row
    back = inverse * (
        scaled
        - jnp.mean(scaled, axis=-1, keepdims=True)
        - hat * jnp.mean(scaled * hat, axis=-1, keepdims=True)
    )
    return back, jnp.sum(grad * hat, axis=0, keepdims=True)


def head_mask(shape, head):
    lane = lax.broadcasted_iota(jnp.int32, shape, 1)
    return (lane >= HEAD_DIM) if head else (lane < HEAD_DIM)


def pick(mask, v, other=0.0):
    return jnp.where(mask, v, jnp.full(v.shape, other, v.dtype))


def gains_of(w_mix):
    def kernel(w_ref, out_ref):
        out_ref[...] = w_ref[...].astype(F32).T[:8]

    return call(
        kernel,
        "gains",
        grid=(1,),
        in_specs=[pl.BlockSpec((D, LANES), lambda j: (0, 4 * D // LANES))],
        out_specs=whole((8, D)),
        out_shape=shaped((8, D), F32),
    )(w_mix)


def keys_values(x, gains, w_kv, cosine, sine):
    rows = x.shape[0]
    block = 512

    def kernel(x_ref, gain_ref, w_ref, cos_ref, sin_ref, a_ref, out_ref):
        @pl.when(pl.program_id(0) == 0)
        def _():
            hat, _ = norm_parts(x_ref[...].astype(F32))
            a_ref[...] = (hat * gain_ref[0:1]).astype(BF)

        m = dot(a_ref[...], w_ref[...], NN)
        for j in range(block // LANES):
            at = slice(j * LANES, (j + 1) * LANES)
            v = m[:, at]
            if j % 2 == 0:
                v = rope_block(v, cos_ref[...], sin_ref[...])
            out_ref[:, at] = v.astype(BF)

    return call(
        kernel,
        "keys_values",
        flops=2 * rows * D * 2 * D,
        moved=2 * (2 * D * D + 4 * rows * D),
        grid=(2 * D // block,),
        in_specs=[
            whole((rows, D)),
            whole((8, D)),
            pl.BlockSpec((D, block), lambda j: (0, j)),
            whole((rows, LANES)),
            whole((rows, LANES)),
        ],
        out_specs=[whole((rows, D)), pl.BlockSpec((rows, block), lambda j: (0, j))],
        out_shape=[shaped((rows, D)), shaped((rows, 2 * D))],
    )(x, gains, w_kv, cosine, sine)


def queries_of(a, w_mix, cosine, sine):
    rows = a.shape[0]
    block = 512

    def kernel(a_ref, w_ref, cos_ref, sin_ref, out_ref):
        m = dot(a_ref[...], w_ref[...], NN)
        for j in range(block // LANES):
            at = slice(j * LANES, (j + 1) * LANES)
            out_ref[:, at] = rope_block(m[:, at], cos_ref[...], sin_ref[...]).astype(BF)

    return call(
        kernel,
        "queries",
        flops=2 * rows * D * D,
        moved=2 * (D * D + 2 * rows * D),
        grid=(D // block,),
        in_specs=[
            whole((rows, D)),
            pl.BlockSpec((D, block), lambda j: (0, 2 * D // block + j)),
            whole((rows, LANES)),
            whole((rows, LANES)),
        ],
        out_specs=pl.BlockSpec((rows, block), lambda j: (0, j)),
        out_shape=shaped((rows, D)),
    )(a, w_mix, cosine, sine)


def key_marks(seg):
    lane = jnp.arange(LANES) % HEAD_DIM
    return jnp.where(lane < IDS, (seg[:, None] == lane), lane < IDS + 3).astype(BF)
def query_marks(seg):
    lane = jnp.arange(LANES) % HEAD_DIM
    return jnp.where((lane < IDS) & (seg[:, None] != lane), PENALTY, 0.0).astype(BF)

def split3(v):
    a = v.astype(BF).astype(F32)
    b = (v - a).astype(BF).astype(F32)
    return a, b, v - a - b


def attend(q, kv_list, qmarks, kmarks, begin, count, wide=2, ahead=2):
    rows = q.shape[0]
    members = len(kv_list)
    keys = members * rows

    def kernel(q_ref, qm_ref, km_ref, *refs):
        kv_refs, (o_ref, lse_ref) = refs[:members], refs[members:]
        heads = []
        for w in range(wide):
            k = jnp.concatenate([r[:, 2 * w * LANES : (2 * w + 1) * LANES] for r in kv_refs], axis=0)
            v = jnp.concatenate([r[:, (2 * w + 1) * LANES : (2 * w + 2) * LANES] for r in kv_refs], axis=0)
            q = q_ref[:, w * LANES : (w + 1) * LANES] * jnp.asarray(HEAD_DIM**-0.5, BF)
            for head in range(2):
                heads.append((w, head, q, k, v))

        def score(n):
            w, head, q, k, v = heads[n]
            mine, theirs = head_mask(q.shape, head), head_mask(k.shape, head)
            return dot(jnp.where(theirs, k, km_ref[...]), jnp.where(mine, q, qm_ref[...]), NT)

        waiting = [score(n) for n in range(ahead)]
        parts, stats = [], []
        for n, (w, head, q, k, v) in enumerate(heads):
            if n + ahead < len(heads):
                waiting.append(score(n + ahead))
            s = waiting[n]
            top = jnp.max(s, axis=0, keepdims=True)
            e = jnp.exp(s - top).astype(BF)
            u = dot(pick(head_mask(v.shape, head), v, 1.0), e, TN)
            low, high = u[:HEAD_DIM], u[HEAD_DIM:]
            value, total = (high, low) if head else (low, high)
            parts.append(value / total)
            stats.append(top + jnp.log(total[:1]))
        for w in range(wide):
            o_ref[:, w * LANES : (w + 1) * LANES] = jnp.concatenate(parts[2 * w : 2 * w + 2], axis=0).T.astype(BF)
            lse_ref[w] = jnp.concatenate(stats[2 * w : 2 * w + 2], axis=0)

    first = begin // wide
    return call(
        kernel,
        "attend",
        limit=28,
        flops=8 * rows * keys * count * LANES,
        moved=2 * (2 * rows + 2 * keys) * count * LANES,
        exps=rows * keys * count * 2,
        grid=(count // wide,),
        in_specs=[
            pl.BlockSpec((rows, wide * LANES), lambda p: (0, first + p)),
            whole((rows, LANES)),
            whole((keys, LANES)),
        ]
        + [pl.BlockSpec((rows, 2 * wide * LANES), lambda p: (0, first + p))] * members,
        out_specs=[
            pl.BlockSpec((rows, wide * LANES), lambda p: (0, p)),
            pl.BlockSpec((wide, 2, rows), lambda p: (p, 0, 0)),
        ],
        out_shape=[shaped((rows, count * LANES)), shaped((count, 2, rows), F32)],
    )(q, qmarks, kmarks, *kv_list)


def project(x, o_list, gains, w_mix):
    rows = x.shape[0]
    block = 512
    steps = D // block

    def kernel(x_ref, gain_ref, w_ref, *refs):
        o_refs, (h_ref, b_ref) = refs[:-2], refs[-2:]
        j = pl.program_id(0)
        at = pl.ds(pl.multiple_of(j * block, block), block)
        total = x_ref[:, at].astype(F32)
        begin = 0
        for o_ref in o_refs:
            end = begin + o_ref.shape[1]
            total += dot(o_ref[...], w_ref[begin:end], NN)
            begin = end
        h_ref[:, at] = total

        @pl.when(j == steps - 1)
        def _():
            hat, _ = norm_parts(h_ref[...])
            b_ref[...] = (hat * gain_ref[1:2]).astype(BF)

    return call(
        kernel,
        "project",
        flops=2 * rows * D * D,
        moved=2 * D * D + 10 * rows * D,
        grid=(steps,),
        in_specs=[
            whole((rows, D)),
            whole((8, D)),
            pl.BlockSpec((D, block), lambda j: (0, 3 * D // block + j)),
        ]
        + [whole(o.shape) for o in o_list],
        out_specs=[whole((rows, D)), whole((rows, D))],
        out_shape=[shaped((rows, D), F32), shaped((rows, D))],
    )(x, gains, w_mix, *o_list)


def ffn_in(b, w_in, w_gate, keep):
    rows = b.shape[0]
    steps = FFP // FFB

    def kernel(b_ref, wa_ref, wg_ref, z_ref, *kept):
        a = dot(b_ref[...], wa_ref[...], NN)
        g = dot(b_ref[...], wg_ref[...], NN)
        phi = 0.5 * (1.0 + lax.erf(a * 0.7071067811865476))
        act = a * phi
        z_ref[...] = (act * g).astype(BF)
        if keep:
            density = 0.3989422804014327 * jnp.exp(-0.5 * a * a)
            kept[0][...] = act.astype(BF)
            kept[1][...] = ((phi + a * density) * g).astype(BF)

    out_spec = pl.BlockSpec((rows, FFB), lambda j: (0, j))
    count = 3 if keep else 1
    return call(
        kernel,
        "ffn_in",
        flops=4 * rows * D * FFP,
        moved=2 * (2 * D * FFP + rows * D + count * rows * FFP),
        grid=(steps,),
        in_specs=[whole((rows, D))] + [pl.BlockSpec((D, FFB), lambda j: (0, j))] * 2,
        out_specs=[out_spec] * count,
        out_shape=[shaped((rows, FFP))] * count,
    )(b, w_in, w_gate)


def ffn_out(h, z, w_back):
    rows = h.shape[0]
    block = 256

    def kernel(h_ref, z_ref, w_ref, out_ref):
        out_ref[...] = (h_ref[...] + dot(z_ref[...], w_ref[...], NT)).astype(BF)

    return call(
        kernel,
        "ffn_out",
        flops=2 * rows * D * FFP,
        moved=2 * (D * FFP + rows * FFP + 3 * rows * D),
        grid=(D // block,),
        in_specs=[
            pl.BlockSpec((rows, block), lambda j: (0, j)),
            whole((rows, FFP)),
            pl.BlockSpec((block, FFP), lambda j: (j, 0)),
        ],
        out_specs=pl.BlockSpec((rows, block), lambda j: (0, j)),
        out_shape=shaped((rows, D)),
    )(h, z, w_back)


def ffn_back(grad, act, slope, w_back):
    rows = grad.shape[0]

    def kernel(g_ref, act_ref, slope_ref, w_ref, da_ref, dg_ref):
        dz = dot(g_ref[...], w_ref[...], NN)
        da_ref[...] = (dz * slope_ref[...].astype(F32)).astype(BF)
        dg_ref[...] = (dz * act_ref[...].astype(F32)).astype(BF)

    spec = pl.BlockSpec((rows, FFB), lambda j: (0, j))
    return call(
        kernel,
        "ffn_back",
        flops=2 * rows * D * FFP,
        moved=2 * (D * FFP + 4 * rows * FFP + rows * D),
        grid=(FFP // FFB,),
        in_specs=[whole((rows, D)), spec, spec, pl.BlockSpec((D, FFB), lambda j: (0, j))],
        out_specs=[spec, spec],
        out_shape=[shaped((rows, FFP))] * 2,
    )(grad, act, slope, w_back)


def hidden_back(grad, da, dg, h, gains, w_in, w_gate):
    rows = grad.shape[0]
    block = 256
    steps = D // block

    def kernel(g_ref, da_ref, dg_ref, h_ref, gain_ref, wa_ref, wg_ref, dh_ref, low_ref, sum_ref):
        j = pl.program_id(0)
        at = pl.ds(pl.multiple_of(j * block, block), block)
        dh_ref[:, at] = dot(da_ref[...], wa_ref[...], NT) + dot(dg_ref[...], wg_ref[...], NT)

        @pl.when(j == steps - 1)
        def _():
            back, total = norm_back(h_ref[...], gain_ref[1:2], dh_ref[...])
            dh = g_ref[...].astype(F32) + back
            dh_ref[...] = dh
            low_ref[...] = dh.astype(BF)
            sum_ref[...] = total

    return call(
        kernel,
        "hidden_back",
        flops=4 * rows * D * FFP,
        moved=2 * (2 * D * FFP + 2 * rows * FFP + 6 * rows * D),
        grid=(steps,),
        in_specs=[
            whole((rows, D)),
            whole((rows, FFP)),
            whole((rows, FFP)),
            whole((rows, D)),
            whole((8, D)),
        ]
        + [pl.BlockSpec((block, FFP), lambda j: (j, 0))] * 2,
        out_specs=[whole((rows, D)), whole((rows, D)), whole((1, D))],
        out_shape=[shaped((rows, D), F32), shaped((rows, D)), shaped((1, D), F32)],
    )(grad, da, dg, h, gains, w_in, w_gate)


def attend_back(q, kv_list, dh_low, o, lse, qmarks, kmarks, w_mix, cosine, sine, begin, wide=2, ahead=1):
    count = o.shape[1] // LANES
    rows = q.shape[0]
    members = len(kv_list)
    keys = members * rows

    def kernel(q_ref, dh_ref, w_ref, o_ref, lse_ref, qm_ref, km_ref, cos_ref, sin_ref, *refs):
        kv_refs, (dq_ref, *dkv_refs) = refs[:members], refs[members:]
        row = lax.broadcasted_iota(jnp.int32, (LANES, rows), 0)
        lane = lax.broadcasted_iota(jnp.int32, (rows, LANES), 1)
        first = head_mask((rows, LANES), 0)
        do_wide = dot(dh_ref[...], w_ref[...], NT).astype(BF)
        heads = []
        for w in range(wide):
            at = slice(w * LANES, (w + 1) * LANES)
            k = jnp.concatenate([r[:, 2 * w * LANES : (2 * w + 1) * LANES] for r in kv_refs], axis=0)
            v = jnp.concatenate([r[:, (2 * w + 1) * LANES : (2 * w + 2) * LANES] for r in kv_refs], axis=0)
            do = do_wide[:, at]
            q = q_ref[:, at] * jnp.asarray(HEAD_DIM**-0.5, BF)
            prod = do.astype(F32) * o_ref[:, at].astype(F32)
            beside = jnp.zeros((LANES, rows), F32)
            for head in range(2):
                for n, part in enumerate(split3(-lse_ref[w, head : head + 1])):
                    beside = jnp.where(row == IDS + n + (HEAD_DIM if head == 0 else 0), part, beside)
            beside = beside.T.astype(BF) + qm_ref[...]
            for head in range(2):
                mine = head_mask((rows, LANES), head)
                theirs = head_mask((keys, LANES), head)
                delta = jnp.sum(jnp.where(mine, prod, 0.0), axis=1, keepdims=True)
                there = jnp.zeros((rows, LANES), F32)
                for n, part in enumerate(split3(-delta)):
                    there = jnp.where(lane == IDS + n + (HEAD_DIM if head == 0 else 0), part, there)
                qh = jnp.where(mine, q, beside)
                doh = jnp.where(mine, do, there.astype(BF))
                kh = jnp.where(theirs, k, km_ref[...])
                vh = jnp.where(theirs, v, km_ref[...])
                heads.append((q, k, do, qh, doh, kh, vh))

        def score(n):
            q, k, do, qh, doh, kh, vh = heads[n]
            return dot(kh, qh, NT), dot(vh, doh, NT)

        dks, dvs, dqs = [], [], []
        waiting = [score(n) for n in range(ahead)]
        for n, (q, k, do, *_) in enumerate(heads):
            if n + ahead < len(heads):
                waiting.append(score(n + ahead))
            s, dp = waiting[n]
            p = jnp.exp(s)
            ds = (p * dp).astype(BF)
            dvs.append(dot(p.astype(BF), do, NN))
            dks.append(dot(ds, q, NN))
            dqs.append(dot(ds, k, TN))
        for w in range(wide):
            at = slice(w * LANES, (w + 1) * LANES)
            a, b = 2 * w, 2 * w + 1
            dq = jnp.where(first, dqs[a], dqs[b])
            dq = rope_block(dq * HEAD_DIM**-0.5, cos_ref[...], -sin_ref[...])
            dq_ref[:, at] = dq.astype(BF)
            for m, out in enumerate(dkv_refs):
                cut = slice(m * rows, (m + 1) * rows)
                low = slice(2 * w * LANES, (2 * w + 1) * LANES)
                high = slice((2 * w + 1) * LANES, (2 * w + 2) * LANES)
                out[:, low] = jnp.where(first, dks[a][cut], dks[b][cut]).astype(BF)
                out[:, high] = jnp.where(first, dvs[a][cut], dvs[b][cut]).astype(BF)

    start = begin // wide
    spec = pl.BlockSpec((rows, wide * LANES), lambda p: (0, p))
    kv_spec = pl.BlockSpec((rows, 2 * wide * LANES), lambda p: (0, p))
    results = call(
        kernel,
        "attend_back",
        limit=28,
        flops=20 * rows * keys * count * LANES,
        moved=2 * (6 * rows + 4 * keys) * count * LANES,
        exps=rows * keys * 2 * count,
        grid=(count // wide,),
        in_specs=[
            pl.BlockSpec((rows, wide * LANES), lambda p: (0, start + p)),
            whole((rows, D)),
            pl.BlockSpec((wide * LANES, D), lambda p: (start + p, 3)),
            spec,
            pl.BlockSpec((wide, 2, rows), lambda p: (p, 0, 0)),
            whole((rows, LANES)),
            whole((keys, LANES)),
            whole((rows, LANES)),
            whole((rows, LANES)),
        ]
        + [pl.BlockSpec((rows, 2 * wide * LANES), lambda p: (0, start + p))] * members,
        out_specs=[spec] + [kv_spec] * members,
        out_shape=[shaped((rows, count * LANES))] + [shaped((rows, 2 * count * LANES))] * members,
    )(q, dh_low, w_mix, o, lse, qmarks, kmarks, cosine, sine, *kv_list)
    return results[0], results[1:]


def keys_back(terms, cosine, sine):
    rows, columns = terms[0].shape

    def kernel(cos_ref, sin_ref, *refs):
        for b in range(columns // LANES):
            at = slice(b * LANES, (b + 1) * LANES)
            v = refs[0][:, at].astype(F32)
            for r in refs[1:-1]:
                v += r[:, at].astype(F32)
            if b % 2 == 0:
                v = rope_block(v, cos_ref[...], -sin_ref[...])
            refs[-1][:, at] = v.astype(BF)

    return call(
        kernel,
        "keys_back",
        flops=10 * rows * columns,
        moved=2 * (len(terms) + 1) * rows * columns,
        grid=(1,),
        in_specs=[whole((rows, LANES))] * 2 + [whole((rows, columns))] * len(terms),
        out_specs=whole((rows, columns)),
        out_shape=shaped((rows, columns)),
    )(cosine, sine, *terms)


def input_back(x, dh, dq_list, dkv_list, gains, w_kv, w_mix):
    rows = x.shape[0]
    block = 256
    steps = D // block
    grads = list(dkv_list) + list(dq_list)

    def kernel(x_ref, dh_ref, gain_ref, wkv_ref, wq_ref, *refs):
        grad_refs, (dx_ref, sum_ref, da_ref) = refs[:-3], refs[-3:]
        j = pl.program_id(0)
        total = 0.0
        begin = 0
        for n, ref in enumerate(grad_refs):
            if n == len(dkv_list):
                begin = 0
            end = begin + ref.shape[1]
            w_ref = wkv_ref if n < len(dkv_list) else wq_ref
            total += dot(ref[...], w_ref[:, begin:end], NT)
            begin = end
        da_ref[:, pl.ds(pl.multiple_of(j * block, block), block)] = total

        @pl.when(j == steps - 1)
        def _():
            back, total = norm_back(x_ref[...].astype(F32), gain_ref[0:1], da_ref[...])
            dx_ref[...] = (dh_ref[...] + back).astype(BF)
            sum_ref[...] = total

    return call(
        kernel,
        "input_back",
        flops=6 * rows * D * D,
        moved=2 * (3 * D * D + 10 * rows * D),
        grid=(steps,),
        in_specs=[
            whole((rows, D)),
            whole((rows, D)),
            whole((8, D)),
            pl.BlockSpec((block, 2 * D), lambda j: (j, 0)),
            pl.BlockSpec((block, D), lambda j: (j, 2)),
        ]
        + [whole(g.shape) for g in grads],
        out_specs=[whole((rows, D)), whole((1, D))],
        out_shape=[shaped((rows, D)), shaped((1, D), F32)],
        scratch_shapes=[pltpu.VMEM((rows, D), F32)],
    )(x, dh, gains, w_kv, w_mix, *grads)


def weight_rows(order, rows, pairs, others=None):
    count = order.shape[0]
    tokens = pairs[0][0][0].shape[0]
    widths = [sum(r.shape[1] for r in rights) for _, rights in pairs]
    columns = sum(widths)
    flat = [v for lefts, rights in pairs for v in list(lefts) + list(rights)]
    flat += [] if others is None else list(others)
    added = 0 if others is None else others[0].shape[0]
    outs = 1 if others is None else 2

    def kernel(order_ref, *refs):
        out_refs, (turned_ref, left_ref) = refs[len(flat) : len(flat) + outs], refs[-2:]
        other_refs = [] if others is None else refs[len(flat) - len(others) : len(flat)]
        spans, at = [], 0
        for ref in other_refs:
            spans.append((at, at + ref.shape[1], ref))
            at += ref.shape[1]
        at = where = 0
        for lefts, rights in pairs:
            row = 0
            for _ in lefts:
                ref = refs[where]
                turned_ref[row : row + ref.shape[1]] = ref[...].T
                row += ref.shape[1]
                where += 1
            for n in range(count):
                start = pl.multiple_of(order_ref[n] * rows, rows)
                left_ref[n * rows : (n + 1) * rows] = turned_ref[pl.ds(start, rows)]
            for _ in rights:
                ref = refs[where]
                width = ref.shape[1]
                for begin in range(0, width, 512):
                    end = min(begin + 512, width)
                    cols = slice(at + begin, at + end)
                    term = dot(left_ref[...], ref[:, begin:end], NN)
                    if others is None:
                        out_refs[0][:, cols] = term.astype(BF)
                        continue
                    low, other_ref = next((a, r) for a, b, r in spans if a <= cols.start < b)
                    there = slice(cols.start - low, cols.stop - low)
                    near = term[:added] + other_ref[:, there].astype(F32)
                    out_refs[0][:, cols] = near[:rows].astype(BF)
                    out_refs[1][: added - rows, cols] = near[rows:].astype(BF)
                    out_refs[1][added - rows :, cols] = term[added:].astype(BF)
                at += width
                where += 1

    shapes = [shaped((count * rows, columns))]
    if others is not None:
        shapes = [shaped((rows, columns)), shaped(((count - 1) * rows, columns))]
    size = 2 * (count * rows * columns + sum(v.size for v in flat))
    return call(
        kernel,
        "weight_rows",
        limit=max(8, 4 + int(1.25 * size) // (1024 * 1024)),
        flops=2 * count * rows * tokens * columns,
        moved=size,
        in_specs=[SMEM_SPEC] + [pl.BlockSpec(memory_space=pltpu.VMEM)] * len(flat),
        out_specs=[pl.BlockSpec(memory_space=pltpu.VMEM)] * outs,
        out_shape=shapes,
        scratch_shapes=[
            pltpu.VMEM((D, tokens), BF),
            pltpu.VMEM((count * rows, tokens), BF),
        ],
    )(order, *flat)


def ring_add(core, own, moving, first):
    rows = moving.shape[0] if first == 0 else moving.shape[0] // 2
    columns = own.shape[1]
    single = first == 0

    def kernel(core_ref, own_ref, moving_ref, out_ref):
        moved = moving_ref[...].astype(F32)
        if single:
            moved = jnp.where(core_ref[0] == pl.program_id(0), moved, 0.0)
        out_ref[...] = (own_ref[...].astype(F32) + moved).astype(BF)

    return call(
        kernel,
        "ring_add",
        limit=8,
        flops=4 * rows * columns,
        moved=12 * rows * columns,
        grid=(2,),
        in_specs=[
            SMEM_SPEC,
            pl.BlockSpec((rows, columns), lambda j: (first + j, 0)),
            pl.BlockSpec((rows, columns), (lambda j: (0, 0)) if single else (lambda j: (j, 0))),
        ],
        out_specs=pl.BlockSpec((rows, columns), lambda j: (j, 0)),
        out_shape=shaped((2 * rows, columns)),
    )(core, own, moving)


def blank(shape):
    def kernel(out_ref):
        pass

    return call(
        kernel,
        "blank",
        limit=1,
        out_specs=pl.BlockSpec(memory_space=pl.ANY),
        out_shape=shaped(shape),
    )()


class Plan:
    def __init__(self, boundary):
        self.micro = boundary.shape[1]
        self.tok_rows = boundary.shape[3]
        self.n_ctx = lax.axis_size("ctx")
        self.nw = lax.axis_size("wshard")
        self.g = self.n_ctx // (self.micro * self.nw)
        self.r = self.tok_rows // (self.g * self.nw)
        self.i = lax.axis_index("ctx")
        self.w = lax.axis_index("wshard")
        self.rows = self.n_ctx * self.r
        self.members = self.g * self.nw
        count = self.n_ctx
        chips = [2 * p if p < count // 2 else 2 * (count - 1 - p) + 1 for p in range(count)]
        self.half = count // 2
        self.way = 1 - 2 * self.w
        self.ring_pairs = []
        for p in range(count):
            self.ring_pairs.append((chips[p] * 2, chips[(p + 1) % count] * 2))
            self.ring_pairs.append((chips[p] * 2 + 1, chips[(p - 1) % count] * 2 + 1))
        place = jnp.where(self.i % 2 == 0, self.i // 2, count - 1 - self.i // 2)

        def chip(at):
            at = at % count
            return jnp.where(at < count // 2, 2 * at, 2 * (count - 1 - at) + 1)

        self.behind = [chip(place - self.way * k) for k in range(self.half + 1)]
        self.ahead = [chip(place + self.way * k) for k in range(self.half + 1)]
        self.wrows = D // (self.n_ctx * self.nw)
        near = range(self.half - 1, 0, -1)
        theirs = [2 * self.ahead[self.half] + 1 - self.w]
        mine = [2 * self.ahead[self.half] + self.w]
        for k in near:
            theirs += [2 * self.behind[k], 2 * self.behind[k] + 1]
            mine += [2 * self.ahead[k], 2 * self.ahead[k] + 1]
        mine += [2 * self.i, 2 * self.i + 1]
        self.theirs = jnp.stack(theirs).astype(jnp.int32)
        self.mine = jnp.stack(mine).astype(jnp.int32)
        self.core = self.w[None].astype(jnp.int32)

    def swap(self, array):
        return lax.ppermute(array, "wshard", [(0, 1), (1, 0)])

    def step(self, array):
        return lax.ppermute(array, BOTH, self.ring_pairs)

    def in_order(self, own, other):
        first = self.w == 0
        return jnp.concatenate(
            [jnp.where(first, own, other), jnp.where(first, other, own)], axis=0
        )

    def across(self, local):
        parts = local.reshape(self.micro, self.g, self.nw, self.r, D)
        parts = lax.all_to_all(parts.transpose(2, 0, 1, 3, 4), "wshard", 0, 0, tiled=True)
        return parts.transpose(1, 0, 2, 3, 4).reshape(self.n_ctx, self.r, D)

    def along(self, parts):
        return lax.all_to_all(parts, "ctx", 0, 0, tiled=True).reshape(self.rows, D)

    def back_along(self, rows):
        return lax.all_to_all(rows.reshape(self.n_ctx, self.r, D), "ctx", 0, 0, tiled=True)

    def back_across(self, parts):
        parts = parts.reshape(self.micro, self.nw, self.g, self.r, D).transpose(1, 0, 2, 3, 4)
        parts = lax.all_to_all(parts, "wshard", 0, 0, tiled=True)
        return parts.transpose(1, 2, 0, 3, 4).reshape(self.micro, self.tok_rows, D)

    def total(self, value):
        by = 1
        while by < self.n_ctx * self.nw:
            pairs = [(n, n ^ by) for n in range(self.n_ctx * self.nw)]
            value = value + lax.ppermute(value, BOTH, pairs)
            by *= 2
        return value

    def rotation(self, by):
        pairs = []
        for flat in range(self.n_ctx * self.nw):
            group, place = divmod(flat, self.members)
            pairs.append((flat, group * self.members + (place + by) % self.members))
        return pairs

    def gather_rows(self, rows):
        return [rows] + [
            lax.ppermute(rows, BOTH, self.rotation(by)) for by in range(1, self.members)
        ]

    def scatter_rows(self, terms):
        return [terms[0]] + [
            lax.ppermute(terms[by], BOTH, self.rotation(-by)) for by in range(1, self.members)
        ]


class Gather:
    def __init__(self, plan, shard, *deps):
        self.plan = plan
        self.rows = shard.shape[0]
        self.whole = blank((plan.n_ctx, plan.nw * self.rows, shard.shape[1]))
        self.current = plan.in_order(shard, plan.swap(shard))
        self.start = self.current
        self.put(self.current, plan.i)
        self.k = 0

    def put(self, block, chip):
        self.whole = lax.dynamic_update_index_in_dim(self.whole, block, chip, 0)

    def advance(self, *deps, late=()):
        plan = self.plan
        self.k += 1
        current = after(self.current, *deps) if deps else self.current
        if self.k < plan.half:
            current = plan.step(current)
            if late:
                current = after(current, *late)
            self.put(current, plan.behind[self.k])
            self.put(plan.swap(current), plan.ahead[self.k])
        else:
            part = lax.dynamic_slice_in_dim(current, plan.w * self.rows, self.rows, 0)
            current = plan.step(part)
            if late:
                current = after(current, *late)
            self.put(plan.in_order(current, plan.swap(current)), plan.behind[plan.half])
        self.current = current
        return current

    def result(self):
        return self.whole.reshape(D, self.whole.shape[2])


class Reduce:
    def __init__(self, plan, clock):
        self.plan, self.clock = plan, clock
        self.pairs, self.others = [], []
        self.k = plan.half

    def theirs(self, *pairs):
        plan = self.plan
        lefts, rights = pairs[0]
        tied = [([self.clock.tie(lefts[0])] + list(lefts[1:]), rights)] + list(pairs[1:])
        (term,) = weight_rows(plan.theirs, plan.wrows, tied)
        self.others.append(plan.swap(self.clock.mark(term)))
        self.pairs += list(pairs)

    def mine(self):
        plan = self.plan
        lefts, rights = self.pairs[0]
        tied = [([self.clock.tie(lefts[0])] + list(lefts[1:]), rights)] + self.pairs[1:]
        term, self.own = weight_rows(plan.mine, plan.wrows, tied, self.others)
        self.moving = plan.step(self.clock.mark(term))
        self.k -= 1

    def advance(self):
        plan = self.plan
        moving = self.clock.tie(self.moving)
        term = ring_add(plan.core, self.own, moving, 2 * (plan.half - 1 - self.k))
        self.moving = plan.step(self.clock.mark(term))
        self.k -= 1

    def result(self):
        plan = self.plan
        rows = plan.wrows
        final = self.moving.astype(F32) + self.own[-2 * rows :].astype(F32)
        keep = lax.dynamic_slice_in_dim(final, plan.w * rows, rows, 0)
        give = lax.dynamic_slice_in_dim(final, (1 - plan.w) * rows, rows, 0)
        return keep + plan.swap(give.astype(BF)).astype(F32)


class Clock:
    def __init__(self):
        self.last = None

    def tie(self, value):
        return value if self.last is None else after(value, self.last)

    def mark(self, value):
        self.last = value
        return value


def interleave(keys, values):
    lead = keys.shape[0]
    both = jnp.stack([keys.reshape(lead, PAIRS, LANES), values.reshape(lead, PAIRS, LANES)], axis=2)
    return both.reshape(lead, 2 * D)


def apart(both):
    lead = both.shape[0]
    both = both.reshape(lead, PAIRS, 2, LANES)
    return both[:, :, 0].reshape(lead, D), both[:, :, 1].reshape(lead, D)


def body(
    boundary, segment_ids, qkv_weight, attn_out_weight, ffn_in_weight, ffn_out_weight, norm_gains
):
    section = lax.axis_index("section")
    sections = lax.axis_size("section")
    plan = Plan(boundary)
    rows = plan.rows

    pad = FFP - FF
    wide_shard = jnp.concatenate(
        [
            interleave(qkv_weight[0][:, D : 2 * D], qkv_weight[0][:, 2 * D :]),
            qkv_weight[0][:, :D],
            attn_out_weight[0],
            jnp.pad(norm_gains[0].T, ((0, 0), (0, LANES - 2))),
        ],
        axis=1,
    )
    in_shard = jnp.pad(ffn_in_weight[0][:, :FF], ((0, 0), (0, pad)))
    gate_shard = jnp.pad(ffn_in_weight[0][:, FF:], ((0, 0), (0, pad)))
    back_shard = jnp.pad(ffn_out_weight[0].T, ((0, 0), (0, pad)))
    get_wide = Gather(plan, wide_shard)
    get_in = Gather(plan, in_shard)
    parts = plan.across(after(boundary[0, :, 0], get_wide.start, get_in.start))
    got = [get.advance() for get in (get_wide, get_in)]
    get_gate = Gather(plan, after(gate_shard, *got))
    get_back = Gather(plan, after(back_shard, *got))
    own = plan.along(after(parts, *got))
    got = [get.advance() for get in (get_wide, get_in)]
    ids = after(segment_ids[:, 0], *got)
    for n in range(plan.half - 2):
        got = get_wide.advance(), get_in.advance(*([own] if n == plan.half - 3 else []))
        if n == 0:
            got_first = got
    got_gate, got_back = get_gate.advance(got[1]), get_back.advance(got[0])

    ids = plan.in_order(ids[None], plan.swap(ids[None])).transpose(1, 0, 2)
    ids = jnp.repeat(ids.reshape(plan.micro * plan.nw, plan.tok_rows), plan.g, axis=0)
    line = after(lax.all_to_all(ids, "ctx", 0, 0, tiled=True).reshape(-1), *got_first)
    grid = line.reshape(plan.n_ctx, plan.members, plan.r)
    place = (plan.i % plan.g) * plan.nw + plan.w
    seg_pieces = [
        lax.dynamic_index_in_dim(grid, (place - by) % plan.members, 1, keepdims=False).reshape(rows)
        for by in range(plan.members)
    ]
    segq = seg_pieces[0]
    segk = jnp.concatenate(seg_pieces)
    token = (
        lax.broadcasted_iota(jnp.int32, (plan.n_ctx, plan.r), 0) * plan.tok_rows
        + place * plan.r
        + lax.broadcasted_iota(jnp.int32, (plan.n_ctx, plan.r), 1)
    ).reshape(rows)
    first = jnp.sum((line[None, :] < segq[:, None]).astype(jnp.int32), axis=1)
    position = (token - first).astype(F32)
    exponent = jnp.arange(HEAD_DIM // 2, dtype=F32) * (-2.0 / HEAD_DIM)
    angles = position[:, None] * (ROPE_BASE**exponent)[None, :]
    cosine, sine = jnp.cos(angles), jnp.sin(angles)
    cos_rows = jnp.concatenate([cosine] * 4, axis=1)
    sin_rows = jnp.concatenate([-sine, sine] * 2, axis=1)
    qmarks, kmarks = query_marks(segq), key_marks(segk)

    w_kv = w_mix = get_wide.result()
    w_in = get_in.result()
    gains = gains_of(w_mix)

    def first_half(x):
        a, kv = keys_values(x, gains, w_kv, cos_rows, sin_rows)
        kv_list = plan.gather_rows(kv)
        return a, kv_list, queries_of(a, w_mix, cos_rows, sin_rows)

    _, kv_list, q = first_half(after(own, got_gate))
    got_gate = get_gate.advance()
    o, _ = attend(after(q, got_back, got_gate), kv_list, qmarks, kmarks, 0, PAIRS)
    got = get_back.advance(late=(o,)), get_gate.advance(late=(o,))
    h, b = project(own, [after(o, *got)], gains, w_mix)
    for one in (get_gate, get_back):
        while one.k < plan.half:
            one.advance()
    w_gate, w_back = get_gate.result(), get_back.result()
    (z,) = ffn_in(b, w_in, w_gate, False)
    first_out = ffn_out(h, z, w_back)

    def forward(x):
        a, kv_list, q = first_half(x)
        o, lse = attend(q, kv_list, qmarks, kmarks, 0, PAIRS)
        h, b = project(x, [o], gains, w_mix)
        z, act, slope = ffn_in(b, w_in, w_gate, True)
        return ffn_out(h, z, w_back), (x, a, q, kv_list, o, lse, h, b, z, act, slope)

    def backward(stash, grad):
        x, a, q, kv_list, o, lse, h, b, z, act, slope = stash
        da, dg = ffn_back(grad, act, slope, w_back)
        dh, dh_low, _ = hidden_back(grad, da, dg, h, gains, w_in, w_gate)
        dq, terms = attend_back(
            q, kv_list, dh_low, o, lse, qmarks, kmarks, w_mix, cos_rows, sin_rows, 0
        )
        dkv = keys_back(plan.scatter_rows(terms), cos_rows, sin_rows)
        return input_back(x, dh, [dq], [dkv], gains, w_kv, w_mix)[0]

    def last_backward(stash, grad, choose):
        x, a, q, kv_list, o, lse, h, b, z, act, slope = stash
        clock = Clock()
        back, grow, out, mixed = (Reduce(plan, clock) for _ in range(4))
        da, dg = ffn_back(clock.tie(grad), act, slope, w_back)
        clock.mark(da)
        grow.theirs(([b], [da, dg]))
        back.theirs(([grad], [z]))
        grow.mine()
        back.mine()
        dh, dh_low, gain_second = hidden_back(clock.tie(grad), da, dg, h, gains, w_in, w_gate)
        clock.mark(dh)
        grow.advance()
        back.advance()
        out.theirs(([o], [dh_low]))
        parts = []
        count = PAIRS // 4
        for n in range(4):
            cut = slice(n * count * LANES, (n + 1) * count * LANES)
            dq, terms = attend_back(
                clock.tie(q),
                kv_list,
                dh_low,
                o[:, cut],
                lse[n * count : (n + 1) * count],
                qmarks,
                kmarks,
                w_mix,
                cos_rows,
                sin_rows,
                n * count,
            )
            clock.mark(dq)
            parts.append((dq, plan.scatter_rows(terms)))
            if n == 0:
                out.mine()
            elif n == 1:
                for one in (grow, back, out):
                    one.advance()
        dkv_list = [keys_back(terms, cos_rows, sin_rows) for _, terms in parts]
        dq_list = [dq for dq, _ in parts]
        mixed.theirs(([a], dkv_list + dq_list))
        for one in (grow, back, out):
            one.advance()
        dx, gain_first = input_back(clock.tie(x), dh, dq_list, dkv_list, gains, w_kv, w_mix)
        clock.mark(dx)
        mixed.mine()
        mixed.moving = after(mixed.moving, grow.moving, back.moving)
        mixed.advance()
        sent = plan.back_along(after(choose(dx), clock.last))
        gain = jnp.concatenate([gain_first, gain_second], axis=0)
        gain = plan.total(after(gain, clock.last))
        for one in (grow, back, out):
            while one.k:
                one.advance()
        while mixed.k:
            if mixed.k == 1:
                mixed.moving = after(mixed.moving, sent)
            mixed.advance()
        start = (plan.i * plan.nw + plan.w) * plan.wrows
        gain = lax.dynamic_slice_in_dim(gain, start, plan.wrows, 1)
        return sent, [back.result(), grow.result(), out.result(), mixed.result(), gain]

    def handed(array, by):
        pairs = [(s, s + by) for s in range(sections) if 0 <= s + by < sections]
        return lax.ppermute(array, "section", pairs)

    x_in = jnp.where(section == 0, own, handed(first_out, 1))
    out, stash = forward(x_in)
    first_dx = backward(stash, own)
    grad_in = jnp.where(section == sections - 1, own, after(handed(first_dx, -1), out))
    sent, (g_back, g_grow, g_attn, g_mix, g_gain) = last_backward(
        stash, grad_in, lambda dx: jnp.where(section == 0, dx, out)
    )
    boundary_local = plan.back_across(sent)
    g_key, g_value = apart(g_mix[:, : 2 * D])
    return (
        boundary_local[None, :, None],
        jnp.concatenate([g_mix[:, 2 * D :], g_key, g_value], axis=1)[None],
        g_attn[None],
        jnp.concatenate([g_grow[:, :FF], g_grow[:, FFP : FFP + FF]], axis=1)[None],
        g_back[:, :FF].T[None],
        g_gain[None],
    )


def solution(mesh):
    placed = (
        P("section", None, "wshard", "ctx", None),
        P(None, "wshard", "ctx"),
        P("section", ("ctx", "wshard"), None),
        P("section", ("ctx", "wshard"), None),
        P("section", ("ctx", "wshard"), None),
        P("section", None, ("ctx", "wshard")),
        P("section", None, ("ctx", "wshard")),
    )
    return jax.shard_map(
        body,
        mesh=mesh,
        in_specs=placed,
        out_specs=(placed[0],) + placed[2:],
        check_vma=False,
    )
```
